32 devices in a mesh: fsdp: 8 (over y, x, core), sp: 4 (over z).
Axes of the slice: x: 2, y: 2, z: 4, core: 2. Of those that a mesh axis runs over, the one named last changes fastest.
Arguments:
- residual_in: float32 [8, 2, 1024, 1152], P('fsdp', None, 'sp'), may hold values from -6 to 6
- condition: float32 [8, 2, 1152], P('fsdp'), may hold values from -6 to 6
- text_states: bfloat16 [8, 2, 120, 4096], P('fsdp', None, 'sp'), may hold values from -6 to 6
- slot_item: int32 [8, 2], P('fsdp'), may hold values from 0 to 1, as said below
- cotangent: bfloat16 [8, 2, 1024, 1152], P('fsdp', None, 'sp'), may hold values from -6 to 6
- w_ada: float32 [1152, 6912], P(('fsdp', 'sp')), may hold values from -0.1875 to 0.1875
- w_qkv: float32 [1152, 3456], P(('fsdp', 'sp')), may hold values from -0.1875 to 0.1875
- w_out: float32 [1152, 1152], P(('fsdp', 'sp')), may hold values from -0.75 to 0.75
- w_cross_q: float32 [1152, 1152], P(('fsdp', 'sp')), may hold values from -0.1875 to 0.1875
- w_cross_kv: float32 [4096, 2304], P(('fsdp', 'sp')), may hold values from -0.09375 to 0.09375
- w_cross_out: float32 [1152, 1152], P(('fsdp', 'sp')), may hold values from -0.5 to 0.5
- w_up: float32 [1152, 4608], P(('fsdp', 'sp')), may hold values from -0.1875 to 0.1875
- w_down: float32 [4608, 1152], P(('fsdp', 'sp')), may hold values from -0.09375 to 0.09375
- w_temp_qkv: float32 [1152, 3456], P(('fsdp', 'sp')), may hold values from -0.1875 to 0.1875
- w_temp_out: float32 [1152, 1152], P(('fsdp', 'sp')), may hold values from -0.25 to 0.25
- g_cross: float32 [1152], P(('fsdp', 'sp')), may hold values from 0.5 to 1.5
- g_temp: float32 [1152], P(('fsdp', 'sp')), may hold values from 0.5 to 1.5
- t_gate: float32 [1152], P(('fsdp', 'sp')), may hold values from 0.5 to 1.5
Outputs:
- output: float32 [8, 2, 1024, 1152], P('fsdp', None, 'sp')
- input_grad: float32 [8, 2, 1024, 1152], P('fsdp', None, 'sp')
- grad_w_ada: float32 [1152, 6912], P(('fsdp', 'sp'))
- grad_w_qkv: float32 [1152, 3456], P(('fsdp', 'sp'))
- grad_w_out: float32 [1152, 1152], P(('fsdp', 'sp'))
- grad_w_cross_q: float32 [1152, 1152], P(('fsdp', 'sp'))
- grad_w_cross_kv: float32 [4096, 2304], P(('fsdp', 'sp'))
- grad_w_cross_out: float32 [1152, 1152], P(('fsdp', 'sp'))
- grad_w_up: float32 [1152, 4608], P(('fsdp', 'sp'))
- grad_w_down: float32 [4608, 1152], P(('fsdp', 'sp'))
- grad_w_temp_qkv: float32 [1152, 3456], P(('fsdp', 'sp'))
- grad_w_temp_out: float32 [1152, 1152], P(('fsdp', 'sp'))
- grad_g_cross: float32 [1152], P(('fsdp', 'sp'))
- grad_g_temp: float32 [1152], P(('fsdp', 'sp'))
- grad_t_gate: float32 [1152], P(('fsdp', 'sp'))
The draws below stay inside these ranges and needn't reach their ends.
Inputs may be any that keep to these rules, and one draw needn't show every extreme that they name: `slot_item`: each group holds either one video whose 2 frames use slot 0's condition and text (all entries 0) or 2 images (entries 0, 1, ...); group 0 holds a video and group 1 images.
All inputs are finite; a program needn't handle non-finite values.
Results may differ from the reference program's by a relative error of at most 0.022.
Values may be sent and summed in bfloat16 or wider, within the bound.
A program may use at most 512 MiB of HBM per device.

```python
import jax
import jax.numpy as jnp
from jax import lax

D = 1152
HEADS = 16
HEAD_DIM = 72
FF = 4608
TEXT_D = 4096
TEXT = 120
PATCH = 1024
SLOTS = 2
GROUPS = 8


def draw_slot_item(key, part):
    flags = jax.random.randint(key, (GROUPS,), 0, 2)
    flags = flags.at[0].set(1).at[1].set(0)
    order = jnp.arange(SLOTS, dtype=jnp.int32)
    return jnp.where(flags[:, None] == 1, jnp.zeros_like(order)[None, :], order[None, :]).astype(jnp.int32)


def level_of(key, extent, shards, low, top_value):
    def one(position, parts):
        steps = jax.random.uniform(jax.random.fold_in(jax.random.fold_in(key, 6), position), (parts,), jnp.float32, low / len(shards), top_value / len(shards))
        return jnp.repeat(jnp.exp(steps), extent[position] // parts).reshape((-1,) + (1,) * (len(extent) - position - 1))

    factor_of = one(*shards[0])
    for cut in shards[1:]:
        factor_of = factor_of * one(*cut)
    return factor_of


def scatter_about(stream_key, dims, spread, bound, cuts=(), held_as=jnp.bfloat16):
    factor_of = level_of(stream_key, dims, cuts, -0.22, 0.18) if cuts else 1.0
    drawn = jax.random.normal(stream_key, dims, jnp.float32) * spread * factor_of
    return jnp.minimum(jnp.maximum(drawn, -bound), bound).astype(held_as)


def setup_inputs(seed: int = 0) -> dict:
    key_list = jax.random.split(jax.random.key(seed), 19)
    return {
        "residual_in": scatter_about(key_list[0], (GROUPS, SLOTS, PATCH, D), 1.0, 6.0, ((0, 8), (2, 4)), jnp.float32),
        "condition": scatter_about(key_list[1], (GROUPS, SLOTS, D), 1.0, 6.0, ((0, 8),), jnp.float32),
        "text_states": scatter_about(key_list[2], (GROUPS, SLOTS, TEXT, TEXT_D), 1.0, 6.0, ((0, 8), (2, 4))),
        "slot_item": draw_slot_item(jax.random.fold_in(key_list[18], 71), 0),
        "cotangent": scatter_about(key_list[4], (GROUPS, SLOTS, PATCH, D), 1.0, 6.0, ((0, 8), (2, 4))),
        "w_ada": scatter_about(key_list[5], (D, 6 * D), D ** -0.5, 0.1875, ((0, 32),), jnp.float32),
        "w_qkv": scatter_about(key_list[6], (D, 3 * D), D ** -0.5, 0.1875, ((0, 32),), jnp.float32),
        "w_out": scatter_about(key_list[7], (D, D), (D // 16) ** -0.5, 0.75, ((0, 32),), jnp.float32),
        "w_cross_q": scatter_about(key_list[8], (D, D), D ** -0.5, 0.1875, ((0, 32),), jnp.float32),
        "w_cross_kv": scatter_about(key_list[9], (TEXT_D, 2 * D), TEXT_D ** -0.5, 0.09375, ((0, 32),), jnp.float32),
        "w_cross_out": scatter_about(key_list[10], (D, D), (D // 8) ** -0.5, 0.5, ((0, 32),), jnp.float32),
        "w_up": scatter_about(key_list[11], (D, FF), D ** -0.5, 0.1875, ((0, 32),), jnp.float32),
        "w_down": scatter_about(key_list[12], (FF, D), FF ** -0.5, 0.09375, ((0, 32),), jnp.float32),
        "w_temp_qkv": scatter_about(key_list[13], (D, 3 * D), D ** -0.5, 0.1875, ((0, 32),), jnp.float32),
        "w_temp_out": scatter_about(key_list[14], (D, D), (D // 2) ** -0.5, 0.25, ((0, 32),), jnp.float32),
        "g_cross": jnp.clip(1.0 + 0.1 * jax.random.normal(key_list[15], (D,), jnp.float32), 0.5, 1.5),
        "g_temp": jnp.clip(1.0 + 0.1 * jax.random.normal(key_list[16], (D,), jnp.float32), 0.5, 1.5),
        "t_gate": jnp.clip(0.5 + 1.0 * jax.random.uniform(key_list[17], (D,), jnp.float32) ** level_of(key_list[17], (D,), ((0, 32),), -0.2, 0.2), 0.5, 1.5),
    }


@jax.custom_vjp
def low(v):
    return lax.optimization_barrier(v.astype(jnp.bfloat16)).astype(jnp.float32)

@jax.custom_vjp
def low_back(v):
    return v

def low_keep(v):
    return (low(v), None)

def low_pass(kept, grad):
    return (grad,)

def back_keep(v):
    return (v, None)

def back_low(kept, grad):
    return (low(grad),)
low.defvjp(low_keep, low_pass)
low_back.defvjp(back_keep, back_low)
highest = lax.Precision.HIGHEST
epsilon = 1e-06

def matmul(left, right):
    return jnp.dot(left, right, precision=highest, preferred_element_type=jnp.float32)

def normalize(values):
    centred = values - lax.optimization_barrier(jnp.mean(values, axis=-1, keepdims=True))
    return centred * lax.rsqrt(lax.optimization_barrier(jnp.mean(centred * centred, axis=-1, keepdims=True)) + epsilon)

def spatial_item(triple):
    query, key_rows, value_rows = triple
    scores = low_back(jnp.dot(query, key_rows.T, precision=highest, preferred_element_type=jnp.float32) * HEAD_DIM ** (-0.5))
    probs = jax.nn.softmax(scores, axis=-1)
    return matmul(low(probs), value_rows)

def group_forward(resid, cond_used, text_used, video, weights):
    w_ada, w_qkv, w_out, w_cross_q, w_cross_kv, w_cross_out, w_up, w_down, w_temp_qkv, w_temp_out, g_cross, g_temp, t_gate = weights
    score_scale = HEAD_DIM ** (-0.5)
    modulation = matmul(low(jax.nn.silu(cond_used)), w_ada).reshape(SLOTS, 6, 1, D)
    shift_one = modulation[:, 0]
    scale_one = modulation[:, 1]
    gate_one = modulation[:, 2]
    shift_two = modulation[:, 3]
    scale_two = modulation[:, 4]
    gate_two = modulation[:, 5]
    h_one = low(normalize(resid) * (1.0 + scale_one) + shift_one)
    qkv_rows = low_back(low(matmul(h_one.reshape(SLOTS * PATCH, D), w_qkv)))
    items = qkv_rows.reshape(SLOTS, PATCH, 3, HEADS, HEAD_DIM).transpose(2, 0, 3, 1, 4).reshape(3, SLOTS * HEADS, PATCH, HEAD_DIM)
    attended = lax.map(jax.checkpoint(spatial_item), (items[0], items[1], items[2]))
    attended = attended.reshape(SLOTS, HEADS, PATCH, HEAD_DIM).transpose(0, 2, 1, 3).reshape(SLOTS * PATCH, D)
    attended = low_back(low(attended))
    branch_one = low_back(matmul(attended, w_out)).reshape(SLOTS, PATCH, D)
    x_one = resid + gate_one * branch_one
    cross_in = low(normalize(x_one) * g_cross)
    query_c = low_back(low(matmul(cross_in.reshape(SLOTS * PATCH, D), w_cross_q))).reshape(SLOTS, PATCH, HEADS, HEAD_DIM)
    text_kv = low_back(low(matmul(text_used.reshape(SLOTS * TEXT, TEXT_D), w_cross_kv))).reshape(SLOTS, TEXT, 2, HEADS, HEAD_DIM)
    scores_c = low_back(jnp.einsum('sqhd,skhd->shqk', query_c, text_kv[:, :, 0], precision=highest) * score_scale)
    probs_c = jax.nn.softmax(scores_c, axis=-1)
    cross_out = jnp.einsum('shqk,skhd->sqhd', low(probs_c), text_kv[:, :, 1], precision=highest)
    cross_out = low_back(low(cross_out.reshape(SLOTS * PATCH, D)))
    branch_two = low_back(matmul(cross_out, w_cross_out)).reshape(SLOTS, PATCH, D)
    x_two = x_one + branch_two
    h_three = low(normalize(x_two) * (1.0 + scale_two) + shift_two)
    up_proj = low_back(matmul(h_three.reshape(SLOTS * PATCH, D), w_up))
    activated = low(jax.nn.gelu(up_proj, approximate=True))
    branch_three = low_back(matmul(activated, w_down)).reshape(SLOTS, PATCH, D)
    x_three = x_two + gate_two * branch_three
    temp_in = low(normalize(x_three) * g_temp)
    temp_qkv = low_back(low(matmul(temp_in.reshape(SLOTS * PATCH, D), w_temp_qkv))).reshape(SLOTS, PATCH, 3, HEADS, HEAD_DIM)
    scores_t = low_back(jnp.einsum('aphd,bphd->phab', temp_qkv[:, :, 0], temp_qkv[:, :, 1], precision=highest) * score_scale)
    probs_t = jax.nn.softmax(scores_t, axis=-1)
    temp_out = jnp.einsum('phab,bphd->aphd', low(probs_t), temp_qkv[:, :, 2], precision=highest)
    temp_out = low_back(low(temp_out.reshape(SLOTS * PATCH, D)))
    branch_four = low_back(matmul(temp_out, w_temp_out)).reshape(SLOTS, PATCH, D)
    return x_three + video * t_gate * branch_four

def reference(residual_in, condition, text_states, slot_item, cotangent, w_ada, w_qkv, w_out, w_cross_q, w_cross_kv, w_cross_out, w_up, w_down, w_temp_qkv, w_temp_out, g_cross, g_temp, t_gate):
    cond_used = jnp.take_along_axis(condition, slot_item[:, :, None].astype(jnp.int32), axis=1)
    text_used = jnp.take_along_axis(text_states.astype(jnp.float32), slot_item[:, :, None, None].astype(jnp.int32), axis=1)
    video = (slot_item[:, -1] == 0).astype(jnp.float32)
    params = (w_ada, w_qkv, w_out, w_cross_q, w_cross_kv, w_cross_out, w_up, w_down, w_temp_qkv, w_temp_out, g_cross, g_temp, t_gate)

    def forward(resid_all, param_set):
        weights = tuple((low(weight_one) for weight_one in param_set))

        def one_group(pack):
            return group_forward(pack[0], pack[1], pack[2], pack[3], weights)
        return lax.map(one_group, (resid_all, cond_used, text_used, video))
    output, pull = jax.vjp(forward, residual_in, params)
    input_grad, grads = pull(cotangent.astype(jnp.float32))
    return (output, input_grad, grads[0], grads[1], grads[2], grads[3], grads[4], grads[5], grads[6], grads[7], grads[8], grads[9], grads[10], grads[11], grads[12])
```

```python
import functools
import jax, jax.numpy as jnp
from jax import lax
from jax.experimental import pallas as pl
from jax.experimental.pallas import tpu as pltpu
HD=72
F32=jnp.float32; BF=jnp.bfloat16
def nt(a,b): return lax.dot_general(a,b,(((1,),(1,)),((),())),preferred_element_type=F32)
def tn(a,b): return lax.dot_general(a,b,(((0,),(0,)),((),())),preferred_element_type=F32)
def nn(a,b): return jnp.dot(a,b,preferred_element_type=F32)

def spatial_fwd_kernel(heads, scale, qkv, o, st, os):
    T = qkv.shape[0]
    W = heads*HD
    for i in range(3*heads):
        st[i] = jnp.zeros(st.shape[1:], BF)
        st[i, :, :HD] = qkv[:, i*HD:(i+1)*HD]
    tile = 256
    def head(h, _):
        k = st[heads+h]; v = st[2*heads+h]
        def rows(i, _):
            q = st[h, pl.ds(pl.multiple_of(i*tile,tile), tile), :]
            s = nt(q,k)
            m = jnp.max(s,axis=-1,keepdims=True)
            e = jnp.exp((s-m)*scale)
            l = jnp.sum(e,axis=-1,keepdims=True)
            r = nn(e.astype(BF), v)
            os[h, pl.ds(pl.multiple_of(i*tile,tile), tile), :] = (r/l).astype(BF)
            return 0
        lax.fori_loop(0, T//tile, rows, 0)
        return 0
    lax.fori_loop(0, heads, head, 0)
    for h in range(heads):
        o[:, h*HD:(h+1)*HD] = os[h, :, :HD]

def spatial_fwd(qkv, heads, scale):
    T=qkv.shape[0]
    return pl.pallas_call(functools.partial(spatial_fwd_kernel,heads,scale),
        out_shape=jax.ShapeDtypeStruct((T,heads*HD),BF),
        in_specs=[pl.BlockSpec(memory_space=pltpu.VMEM)],
        out_specs=pl.BlockSpec(memory_space=pltpu.VMEM),
        scratch_shapes=[pltpu.VMEM((3*heads,T,128),BF),pltpu.VMEM((heads,T,128),BF)],
        compiler_params=pltpu.CompilerParams(vmem_limit_bytes=48*2**20),
        cost_estimate=pl.CostEstimate(flops=4*heads*T*T*128,bytes_accessed=T*heads*HD*8,transcendentals=heads*T*T),
        name="spatial_fwd")(qkv)

def spatial_bwd_kernel(heads, scale, qkv, go, g, st, gs, acc):
    T = qkv.shape[0]
    for i in range(3*heads):
        st[i] = jnp.zeros(st.shape[1:], BF)
        st[i, :, :HD] = qkv[:, i*HD:(i+1)*HD]
    for h in range(heads):
        gs[h] = jnp.zeros(gs.shape[1:], BF)
        gs[h, :, :HD] = go[:, h*HD:(h+1)*HD]
    tile = 256
    def head(h, _):
        k = st[heads+h]; v = st[2*heads+h]
        acc[...] = jnp.zeros(acc.shape, F32)
        def cols(i, _):
            sl = pl.ds(pl.multiple_of(i*tile,tile), tile)
            q = st[h, sl, :]; gq_in = gs[h, sl, :]
            s = nt(k,q)
            m = jnp.max(s,axis=0,keepdims=True)
            e = jnp.exp((s-m)*scale)
            p = e * (1.0/jnp.sum(e,axis=0,keepdims=True))
            dp = nt(v,gq_in)
            t = dp*p
            d = jnp.sum(t,axis=0,keepdims=True)
            ds = (t-p*d).astype(BF)
            acc[0] += nn(ds,q)
            acc[1] += nn(p.astype(BF),gq_in)
            st[h, sl, :] = (tn(ds,k)*scale).astype(BF)
            return 0
        lax.fori_loop(0, T//tile, cols, 0)
        st[heads+h] = (acc[0]*scale).astype(BF)
        st[2*heads+h] = acc[1].astype(BF)
        return 0
    lax.fori_loop(0, heads, head, 0)
    for i in range(3*heads):
        g[:, i*HD:(i+1)*HD] = st[i, :, :HD]

def spatial_bwd(qkv, go, heads, scale):
    T=qkv.shape[0]
    return pl.pallas_call(functools.partial(spatial_bwd_kernel,heads,scale),
        out_shape=jax.ShapeDtypeStruct((T,3*heads*HD),BF),
        in_specs=[pl.BlockSpec(memory_space=pltpu.VMEM)]*2,
        out_specs=pl.BlockSpec(memory_space=pltpu.VMEM),
        scratch_shapes=[pltpu.VMEM((3*heads,T,128),BF),pltpu.VMEM((heads,T,128),BF),pltpu.VMEM((2,T,128),F32)],
        compiler_params=pltpu.CompilerParams(vmem_limit_bytes=56*2**20),
        cost_estimate=pl.CostEstimate(flops=10*heads*T*T*128,bytes_accessed=T*heads*HD*16,transcendentals=heads*T*T),
        name="spatial_bwd")(qkv, go)

def cross_fwd_kernel(heads, scale, q, kv, o):
    S,T,W = q.shape
    for h in range(heads):
        c = slice(h*HD,(h+1)*HD); cv = slice(W+h*HD, W+(h+1)*HD)
        s = nt(q[0,:,c], kv[0,:,c])
        m = jnp.max(s,axis=-1,keepdims=True)
        e = jnp.exp((s-m)*scale)
        l = jnp.sum(e,axis=-1,keepdims=True)
        o[0,:,c] = (nn(e.astype(BF), kv[0,:,cv])/l).astype(BF)

def cross_fwd(q, kv, heads, scale):
    S,T,W = q.shape; K=kv.shape[1]
    return pl.pallas_call(functools.partial(cross_fwd_kernel,heads,scale),
        grid=(S,),
        out_shape=jax.ShapeDtypeStruct((S,T,W),BF),
        in_specs=[pl.BlockSpec((1,T,W),lambda s:(s,0,0)),pl.BlockSpec((1,K,2*W),lambda s:(s,0,0))],
        out_specs=pl.BlockSpec((1,T,W),lambda s:(s,0,0)),
        compiler_params=pltpu.CompilerParams(vmem_limit_bytes=32*2**20),
        cost_estimate=pl.CostEstimate(flops=4*S*heads*T*K*128,bytes_accessed=S*T*W*4,transcendentals=S*heads*T*K),
        name="cross_fwd")(q,kv)

def cross_bwd_kernel(heads, scale, q, kv, go, gq, gkv):
    S,T,W = q.shape
    for h in range(heads):
        c = slice(h*HD,(h+1)*HD); cv = slice(W+h*HD, W+(h+1)*HD)
        qh=q[0,:,c]; kh=kv[0,:,c]; vh=kv[0,:,cv]; gh=go[0,:,c]
        s = nt(kh,qh)
        m = jnp.max(s,axis=0,keepdims=True)
        e = jnp.exp((s-m)*scale)
        p = e*(1.0/jnp.sum(e,axis=0,keepdims=True))
        dp = nt(vh,gh)
        t = dp*p
        ds = (t-p*jnp.sum(t,axis=0,keepdims=True)).astype(BF)
        gq[0,:,c] = (tn(ds,kh)*scale).astype(BF)
        gkv[0,:,c] = nn(ds,qh)*scale
        gkv[0,:,cv] = nn(p.astype(BF),gh)

def cross_bwd(q, kv, go, heads, scale):
    S,T,W = q.shape; K=kv.shape[1]
    return pl.pallas_call(functools.partial(cross_bwd_kernel,heads,scale),
        grid=(S,),
        out_shape=(jax.ShapeDtypeStruct((S,T,W),BF),jax.ShapeDtypeStruct((S,K,2*W),F32)),
        in_specs=[pl.BlockSpec((1,T,W),lambda s:(s,0,0)),pl.BlockSpec((1,K,2*W),lambda s:(s,0,0)),pl.BlockSpec((1,T,W),lambda s:(s,0,0))],
        out_specs=(pl.BlockSpec((1,T,W),lambda s:(s,0,0)),pl.BlockSpec((1,K,2*W),lambda s:(s,0,0))),
        compiler_params=pltpu.CompilerParams(vmem_limit_bytes=32*2**20),
        cost_estimate=pl.CostEstimate(flops=10*S*heads*T*K*128,bytes_accessed=S*T*W*8,transcendentals=S*heads*T*K),
        name="cross_bwd")(q,kv,go)


HEADS = 16
EPS = 1e-06
HIGHEST = lax.Precision.HIGHEST
BOTH = ("fsdp", "sp")


def normalize(values):
    centred = values - jnp.mean(values, axis=-1, keepdims=True)
    return centred * lax.rsqrt(jnp.mean(centred * centred, axis=-1, keepdims=True) + EPS)


def normalize_back(values, grad_out):
    return jax.vjp(normalize, values)[1](grad_out)[0]


def gelu_tanh(values):
    return jax.nn.gelu(values, approximate=True)


def scatter(grad):
    part = lax.psum_scatter(grad.astype(BF), "fsdp", scatter_dimension=0, tiled=True)
    return lax.psum_scatter(part, "sp", scatter_dimension=0, tiled=True).astype(F32)


class Moves:
    def __init__(self, fsdp, sp, slots):
        self.fsdp, self.sp, self.slots = fsdp, sp, slots
        self.core = lax.axis_index("fsdp") % 2
        self.z = lax.axis_index("sp")
        self.rounds = []
        for r in range(sp):
            pairs = []
            for f in range(fsdp):
                for z in range(sp):
                    t = (z - r) % sp
                    pairs.append((f * sp + z, (f - f % 2 + t % 2) * sp + slots * (f % 2) + t // 2))
            self.rounds.append(pairs)
        self.swap = [(f, f ^ 1) for f in range(fsdp)]

    def out(self, tokens):
        rows = tokens.shape[0] // self.sp
        blocks = tokens.reshape(self.sp, rows, tokens.shape[1])
        got = []
        for r, pairs in enumerate(self.rounds):
            t = (self.z - r) % self.sp
            block = lax.dynamic_index_in_dim(blocks, t, 0, keepdims=False)
            got.append(lax.ppermute(block, BOTH, pairs))
        return jnp.concatenate(got, axis=0)

    def home(self, tokens):
        rows = tokens.shape[0] // self.sp
        out = jnp.zeros((self.sp, rows, tokens.shape[1]), tokens.dtype)
        for r, pairs in enumerate(self.rounds):
            back = lax.ppermute(tokens[r * rows : (r + 1) * rows], BOTH, [(b, a) for a, b in pairs])
            t = (self.z - r) % self.sp
            out = lax.dynamic_update_index_in_dim(out, back, t, 0)
        return out.reshape(tokens.shape)

    def exchange(self, array):
        return lax.ppermute(array, "fsdp", self.swap)


def local(
    residual_in,
    condition,
    text_states,
    slot_item,
    cotangent,
    w_ada,
    w_qkv,
    w_out,
    w_cross_q,
    w_cross_kv,
    w_cross_out,
    w_up,
    w_down,
    w_temp_qkv,
    w_temp_out,
    g_cross,
    g_temp,
    t_gate,
):
    slots, patches, width = residual_in.shape[1:]
    text_local, text_width = text_states.shape[2:]
    sp = lax.axis_size("sp")
    fsdp = lax.axis_size("fsdp")
    f_index, z_index = lax.axis_index("fsdp"), lax.axis_index("sp")
    rows = w_qkv.shape[0]
    tok = slots * patches
    scale = HD ** (-0.5)
    moves = Moves(fsdp, sp, slots)
    core = f_index % 2

    def gather(shard):
        return lax.all_gather(shard.astype(BF), BOTH, axis=0, tiled=True)

    chosen = slot_item[0]
    video = (chosen[-1] == 0).astype(F32)

    cond = condition[0]
    cond_used = jnp.where((chosen == 0)[:, None], cond[0][None], cond[1][None])
    silu_low = jax.nn.silu(cond_used).astype(BF)
    silu_all = lax.all_gather(silu_low, "fsdp", axis=0, tiled=True)
    silu_rows = lax.dynamic_slice_in_dim(silu_all, (f_index * sp + z_index) * rows, rows, 1)
    mod_part = nn(silu_rows, w_ada.astype(BF))
    modulation = lax.psum(
        lax.psum_scatter(mod_part, "fsdp", scatter_dimension=0, tiled=True), "sp"
    ).reshape(slots, 6, 1, width)
    shift_one, scale_one, gate_one, shift_two, scale_two, gate_two = (modulation[:, i] for i in range(6))

    heads_half = HEADS // 2
    half = heads_half * HD
    qkv_full = gather(w_qkv)
    qkv_half = lax.dynamic_index_in_dim(
        qkv_full.reshape(width, 3, 2, half), core, 2, keepdims=False
    ).reshape(width, 3 * half)
    vectors = lax.all_gather(jnp.stack([g_cross, g_temp, t_gate]).astype(BF), BOTH, axis=1, tiled=True).astype(F32)
    gain_cross, gain_temp, temp_gate = vectors[0], vectors[1], vectors[2]
    out_full = gather(w_out)
    cross_q_full = gather(w_cross_q)
    cross_out_full = gather(w_cross_out)
    up_full = gather(w_up)
    down_full = gather(w_down)
    temp_qkv_full = gather(w_temp_qkv)
    temp_out_full = gather(w_temp_out)

    kv_rows = w_cross_kv.shape[0]
    kv_weight = lax.all_gather(w_cross_kv.astype(BF), "fsdp", axis=0, tiled=True)
    text = text_states[0]
    text_used = jnp.where((chosen == 0)[:, None, None], text[0][None], text[1][None])
    text_cut = text_used.reshape(slots * text_local, fsdp, sp, kv_rows)
    text_mine = lax.all_to_all(text_cut, "sp", split_axis=2, concat_axis=0, tiled=True)
    text_mine = text_mine.reshape(sp * slots * text_local, fsdp * kv_rows)
    kv_part = lax.psum_scatter(nn(text_mine, kv_weight), "sp", scatter_dimension=0, tiled=True).astype(BF)
    kv_all = (
        lax.all_gather(kv_part.reshape(1, slots, text_local, 2 * width), "sp", axis=0, tiled=True)
        .transpose(1, 0, 2, 3)
        .reshape(slots, sp * text_local, 2 * width)
    )

    resid = residual_in[0]
    normed_one = normalize(resid)
    h_one = (normed_one * (1.0 + scale_one) + shift_one).astype(BF).reshape(tok, width)
    h_mine = moves.out(h_one)
    h_slot = jnp.concatenate([h_mine, moves.exchange(h_mine)], axis=0)
    qkv = nn(h_slot, qkv_half).astype(BF)
    o_slot = spatial_fwd(qkv, heads_half, scale)
    o_mine = o_slot[:tok]
    o_other = moves.exchange(o_slot[tok:])
    o_full = jnp.where(
        core == 0,
        jnp.concatenate([o_mine, o_other], axis=1),
        jnp.concatenate([o_other, o_mine], axis=1),
    )
    attn_tok = moves.home(o_full)
    branch_one = nn(attn_tok, out_full).reshape(slots, patches, width)
    x_one = resid + gate_one * branch_one

    normed_two = normalize(x_one)
    cross_in = (normed_two * gain_cross).astype(BF).reshape(tok, width)
    query_c = nn(cross_in, cross_q_full).astype(BF).reshape(slots, patches, width)
    cross_out = cross_fwd(query_c, kv_all, HEADS, scale).reshape(tok, width)
    branch_two = nn(cross_out, cross_out_full).reshape(slots, patches, width)
    x_two = x_one + branch_two

    normed_three = normalize(x_two)
    h_three = (normed_three * (1.0 + scale_two) + shift_two).astype(BF).reshape(tok, width)
    up_proj = nn(h_three, up_full)
    activated = gelu_tanh(up_proj).astype(BF)
    branch_three = nn(activated, down_full).reshape(slots, patches, width)
    x_three = x_two + gate_two * branch_three

    normed_four = normalize(x_three)
    temp_in = (normed_four * gain_temp).astype(BF).reshape(tok, width)
    trip = nn(temp_in, temp_qkv_full).astype(BF).reshape(slots, patches, 3, width)
    tq = [trip[a, :, 0].astype(F32) for a in range(slots)]
    tk = [trip[a, :, 1].astype(F32) for a in range(slots)]
    tv = [trip[a, :, 2].astype(F32) for a in range(slots)]
    member = (jnp.arange(width)[:, None] // HD == jnp.arange(HEADS)[None, :]).astype(F32)
    member_low = member.T.astype(BF)

    def per_head(lefts, rights):
        products = jnp.stack([a * b for a in lefts for b in rights])
        return jnp.dot(
            products.reshape(-1, width), member, precision=HIGHEST, preferred_element_type=F32
        ).reshape(slots, slots, patches, HEADS)

    def spread(values):
        return nn(values.astype(BF).reshape(-1, HEADS), member_low).reshape(slots, slots, patches, width)

    probs_t = jax.nn.softmax(per_head(tq, tk) * scale, axis=1)
    probs_wide = spread(probs_t)
    temp_out = jnp.stack(
        [sum(probs_wide[a, b] * tv[b] for b in range(slots)) for a in range(slots)]
    ).astype(BF).reshape(tok, width)
    branch_four = nn(temp_out, temp_out_full).reshape(slots, patches, width)
    output = x_three + (video * temp_gate) * branch_four

    grad_out = cotangent[0].astype(F32)
    grad_tgate = video * jnp.sum(grad_out * branch_four, axis=(0, 1))
    grad_b4 = (grad_out * (video * temp_gate)).astype(BF).reshape(tok, width)
    grad_wto = tn(temp_out, grad_b4)
    grad_to = nt(grad_b4, temp_out_full).astype(BF).astype(F32).reshape(slots, patches, width)
    grad_to = [grad_to[a] for a in range(slots)]
    dp_t = per_head(grad_to, tv)
    ds_t = probs_t * (dp_t - jnp.sum(dp_t * probs_t, axis=1, keepdims=True))
    ds_wide = spread(ds_t)
    pairs = range(slots)
    grad_trip = jnp.stack(
        [
            jnp.stack([scale * sum(ds_wide[a, b] * tk[b] for b in pairs) for a in pairs]),
            jnp.stack([scale * sum(ds_wide[a, b] * tq[a] for a in pairs) for b in pairs]),
            jnp.stack([sum(probs_wide[a, b] * grad_to[a] for a in pairs) for b in pairs]),
        ],
        axis=2,
    ).astype(BF).reshape(tok, 3 * width)
    grad_wtq = tn(temp_in, grad_trip)
    grad_temp_in = nt(grad_trip, temp_qkv_full).reshape(slots, patches, width)
    grad_gtemp = jnp.sum(grad_temp_in * normed_four, axis=(0, 1))
    grad_three = grad_out + normalize_back(x_three, grad_temp_in * gain_temp)

    grad_gate_two = jnp.sum(grad_three * branch_three, axis=1)
    grad_b3 = (grad_three * gate_two).astype(BF).reshape(tok, width)
    grad_wdown = tn(activated, grad_b3)
    grad_act = nt(grad_b3, down_full)
    grad_up = jax.vjp(gelu_tanh, up_proj)[1](grad_act)[0].astype(BF)
    grad_wup = tn(h_three, grad_up)
    grad_h_three = nt(grad_up, up_full).reshape(slots, patches, width)
    grad_shift_two = jnp.sum(grad_h_three, axis=1)
    grad_scale_two = jnp.sum(grad_h_three * normed_three, axis=1)
    grad_two = grad_three + normalize_back(x_two, grad_h_three * (1.0 + scale_two))

    grad_b2 = grad_two.astype(BF).reshape(tok, width)
    grad_wco = tn(cross_out, grad_b2)
    grad_co = nt(grad_b2, cross_out_full).astype(BF).reshape(slots, patches, width)
    grad_qc, grad_kv = cross_bwd(query_c, kv_all, grad_co, HEADS, scale)
    grad_qc = grad_qc.reshape(tok, width)
    grad_kv = (
        grad_kv.reshape(slots, sp, text_local, 2 * width)
        .transpose(1, 0, 2, 3)
        .reshape(sp * slots * text_local, 2 * width)
        .astype(BF)
    )
    grad_kv = lax.all_gather(
        lax.psum_scatter(grad_kv, "sp", scatter_dimension=0, tiled=True), "sp", axis=0, tiled=True
    )
    grad_wckv = tn(text_mine, grad_kv)
    grad_wcq = tn(cross_in, grad_qc)
    grad_cross_in = nt(grad_qc, cross_q_full).reshape(slots, patches, width)
    grad_gcross = jnp.sum(grad_cross_in * normed_two, axis=(0, 1))
    grad_one = grad_two + normalize_back(x_one, grad_cross_in * gain_cross)

    grad_gate_one = jnp.sum(grad_one * branch_one, axis=1)
    grad_b1 = (grad_one * gate_one).astype(BF).reshape(tok, width)
    grad_wout = tn(attn_tok, grad_b1)
    grad_attn = nt(grad_b1, out_full).astype(BF)
    go_mine = moves.out(grad_attn)
    low_half, high_half = go_mine[:, :half], go_mine[:, half:]
    go_other = moves.exchange(jnp.where(core == 0, high_half, low_half))
    go_slot = jnp.concatenate([jnp.where(core == 0, low_half, high_half), go_other], axis=0)
    grad_qkv = spatial_bwd(qkv, go_slot, heads_half, scale)
    grad_wqkv_half = tn(h_slot, grad_qkv).astype(BF)
    gh_slot = nt(grad_qkv, qkv_half)
    gh_mine = (gh_slot[:tok] + moves.exchange(gh_slot[tok:])).astype(BF)
    grad_h_one = moves.home(gh_mine).astype(F32).reshape(slots, patches, width)
    grad_shift_one = jnp.sum(grad_h_one, axis=1)
    grad_scale_one = jnp.sum(grad_h_one * normed_one, axis=1)
    input_grad = grad_one + normalize_back(resid, grad_h_one * (1.0 + scale_one))

    wide = grad_wqkv_half.reshape(width, 3, 1, half)
    zeros = jnp.zeros_like(wide)
    grad_wqkv = jnp.where(
        core == 0, jnp.concatenate([wide, zeros], axis=2), jnp.concatenate([zeros, wide], axis=2)
    ).reshape(width, 3 * width)

    small = jnp.concatenate(
        [
            jnp.stack(
                [
                    grad_shift_one,
                    grad_scale_one,
                    grad_gate_one,
                    grad_shift_two,
                    grad_scale_two,
                    grad_gate_two,
                ],
                axis=1,
            ).reshape(slots * 6, width),
            jnp.stack([grad_gcross, grad_gtemp, grad_tgate]),
        ],
        axis=0,
    )
    small_all = lax.all_gather(small, BOTH, axis=0).reshape(fsdp, sp, slots * 6 + 3, width)
    small_sp = jnp.sum(small_all, axis=1)
    grad_mod = small_sp[:, : slots * 6].reshape(fsdp * slots, 6 * width)
    grad_wada = jnp.dot(silu_rows.astype(F32).T, grad_mod, precision=HIGHEST, preferred_element_type=F32)
    grad_vec = lax.dynamic_slice_in_dim(
        jnp.sum(small_sp[:, slots * 6 :], axis=0), (f_index * sp + z_index) * rows, rows, 1
    )
    grad_wckv = lax.psum_scatter(grad_wckv.astype(BF), "fsdp", scatter_dimension=0, tiled=True).astype(F32)
    return (
        output[None],
        input_grad[None],
        grad_wada,
        scatter(grad_wqkv),
        scatter(grad_wout),
        scatter(grad_wcq),
        grad_wckv,
        scatter(grad_wco),
        scatter(grad_wup),
        scatter(grad_wdown),
        scatter(grad_wtq),
        scatter(grad_wto),
        grad_vec[0],
        grad_vec[1],
        grad_vec[2],
    )


def solution(mesh):
    P = jax.sharding.PartitionSpec
    tokens = P("fsdp", None, "sp", None)
    weight = P(BOTH, None)
    vector = P(BOTH)
    return jax.shard_map(
        local,
        mesh=mesh,
        in_specs=(tokens, P("fsdp", None, None), tokens, P("fsdp", None), tokens)
        + (weight,) * 10
        + (vector,) * 3,
        out_specs=(tokens, tokens) + (weight,) * 10 + (vector,) * 3,
        check_vma=False,
    )
```

```python
import functools
from types import SimpleNamespace
import jax, jax.numpy as jnp
from jax import lax
from jax.experimental import pallas as pl
from jax.experimental.pallas import tpu as pltpu
HD=72
F32=jnp.float32; BF=jnp.bfloat16
def nt(a,b): return lax.dot_general(a,b,(((1,),(1,)),((),())),preferred_element_type=F32)
def tn(a,b): return lax.dot_general(a,b,(((0,),(0,)),((),())),preferred_element_type=F32)
def nn(a,b): return jnp.dot(a,b,preferred_element_type=F32)

def spatial_fwd_kernel(heads, scale, qkv, o, st, os):
    T = qkv.shape[0]
    W = heads*HD
    for i in range(3*heads):
        st[i] = jnp.zeros(st.shape[1:], BF)
        st[i, :, :HD] = qkv[:, i*HD:(i+1)*HD]
    tile = 256
    def head(h, _):
        k = st[heads+h]; v = st[2*heads+h]
        def rows(i, _):
            q = st[h, pl.ds(pl.multiple_of(i*tile,tile), tile), :]
            s = nt(q,k)
            m = jnp.max(s,axis=-1,keepdims=True)
            e = jnp.exp((s-m)*scale)
            l = jnp.sum(e,axis=-1,keepdims=True)
            r = nn(e.astype(BF), v)
            os[h, pl.ds(pl.multiple_of(i*tile,tile), tile), :] = (r/l).astype(BF)
            return 0
        lax.fori_loop(0, T//tile, rows, 0)
        return 0
    lax.fori_loop(0, heads, head, 0)
    for h in range(heads):
        o[:, h*HD:(h+1)*HD] = os[h, :, :HD]

def spatial_fwd(qkv, heads, scale):
    T=qkv.shape[0]
    return pl.pallas_call(functools.partial(spatial_fwd_kernel,heads,scale),
        out_shape=jax.ShapeDtypeStruct((T,heads*HD),BF),
        in_specs=[pl.BlockSpec(memory_space=pltpu.VMEM)],
        out_specs=pl.BlockSpec(memory_space=pltpu.VMEM),
        scratch_shapes=[pltpu.VMEM((3*heads,T,128),BF),pltpu.VMEM((heads,T,128),BF)],
        compiler_params=pltpu.CompilerParams(vmem_limit_bytes=48*2**20),
        cost_estimate=pl.CostEstimate(flops=4*heads*T*T*128,bytes_accessed=T*heads*HD*8,transcendentals=heads*T*T),
        name="spatial_fwd")(qkv)

def spatial_bwd_kernel(heads, scale, qkv, go, g, st, gs, acc):
    T = qkv.shape[0]
    for i in range(3*heads):
        st[i] = jnp.zeros(st.shape[1:], BF)
        st[i, :, :HD] = qkv[:, i*HD:(i+1)*HD]
    for h in range(heads):
        gs[h] = jnp.zeros(gs.shape[1:], BF)
        gs[h, :, :HD] = go[:, h*HD:(h+1)*HD]
    tile = 256
    def head(h, _):
        k = st[heads+h]; v = st[2*heads+h]
        acc[...] = jnp.zeros(acc.shape, F32)
        def cols(i, _):
            sl = pl.ds(pl.multiple_of(i*tile,tile), tile)
            q = st[h, sl, :]; gq_in = gs[h, sl, :]
            s = nt(k,q)
            m = jnp.max(s,axis=0,keepdims=True)
            e = jnp.exp((s-m)*scale)
            p = e * (1.0/jnp.sum(e,axis=0,keepdims=True))
            dp = nt(v,gq_in)
            t = dp*p
            d = jnp.sum(t,axis=0,keepdims=True)
            ds = (t-p*d).astype(BF)
            acc[0] += nn(ds,q)
            acc[1] += nn(p.astype(BF),gq_in)
            st[h, sl, :] = (tn(ds,k)*scale).astype(BF)
            return 0
        lax.fori_loop(0, T//tile, cols, 0)
        st[heads+h] = (acc[0]*scale).astype(BF)
        st[2*heads+h] = acc[1].astype(BF)
        return 0
    lax.fori_loop(0, heads, head, 0)
    for i in range(3*heads):
        g[:, i*HD:(i+1)*HD] = st[i, :, :HD]

def spatial_bwd(qkv, go, heads, scale):
    T=qkv.shape[0]
    return pl.pallas_call(functools.partial(spatial_bwd_kernel,heads,scale),
        out_shape=jax.ShapeDtypeStruct((T,3*heads*HD),BF),
        in_specs=[pl.BlockSpec(memory_space=pltpu.VMEM)]*2,
        out_specs=pl.BlockSpec(memory_space=pltpu.VMEM),
        scratch_shapes=[pltpu.VMEM((3*heads,T,128),BF),pltpu.VMEM((heads,T,128),BF),pltpu.VMEM((2,T,128),F32)],
        compiler_params=pltpu.CompilerParams(vmem_limit_bytes=56*2**20),
        cost_estimate=pl.CostEstimate(flops=10*heads*T*T*128,bytes_accessed=T*heads*HD*16,transcendentals=heads*T*T),
        name="spatial_bwd")(qkv, go)

def cross_fwd_kernel(heads, scale, q, kv, o):
    S,T,W = q.shape
    for h in range(heads):
        c = slice(h*HD,(h+1)*HD); cv = slice(W+h*HD, W+(h+1)*HD)
        s = nt(q[0,:,c], kv[0,:,c])
        m = jnp.max(s,axis=-1,keepdims=True)
        e = jnp.exp((s-m)*scale)
        l = jnp.sum(e,axis=-1,keepdims=True)
        o[0,:,c] = (nn(e.astype(BF), kv[0,:,cv])/l).astype(BF)

def cross_fwd(q, kv, heads, scale):
    S,T,W = q.shape; K=kv.shape[1]
    return pl.pallas_call(functools.partial(cross_fwd_kernel,heads,scale),
        grid=(S,),
        out_shape=jax.ShapeDtypeStruct((S,T,W),BF),
        in_specs=[pl.BlockSpec((1,T,W),lambda s:(s,0,0)),pl.BlockSpec((1,K,2*W),lambda s:(s,0,0))],
        out_specs=pl.BlockSpec((1,T,W),lambda s:(s,0,0)),
        compiler_params=pltpu.CompilerParams(vmem_limit_bytes=32*2**20),
        cost_estimate=pl.CostEstimate(flops=4*S*heads*T*K*128,bytes_accessed=S*T*W*4,transcendentals=S*heads*T*K),
        name="cross_fwd")(q,kv)

def cross_bwd_kernel(heads, scale, q, kv, go, gq, gkv):
    S,T,W = q.shape
    for h in range(heads):
        c = slice(h*HD,(h+1)*HD); cv = slice(W+h*HD, W+(h+1)*HD)
        qh=q[0,:,c]; kh=kv[0,:,c]; vh=kv[0,:,cv]; gh=go[0,:,c]
        s = nt(kh,qh)
        m = jnp.max(s,axis=0,keepdims=True)
        e = jnp.exp((s-m)*scale)
        p = e*(1.0/jnp.sum(e,axis=0,keepdims=True))
        dp = nt(vh,gh)
        t = dp*p
        ds = (t-p*jnp.sum(t,axis=0,keepdims=True)).astype(BF)
        gq[0,:,c] = (tn(ds,kh)*scale).astype(BF)
        gkv[0,:,c] = nn(ds,qh)*scale
        gkv[0,:,cv] = nn(p.astype(BF),gh)

def cross_bwd(q, kv, go, heads, scale):
    S,T,W = q.shape; K=kv.shape[1]
    return pl.pallas_call(functools.partial(cross_bwd_kernel,heads,scale),
        grid=(S,),
        out_shape=(jax.ShapeDtypeStruct((S,T,W),BF),jax.ShapeDtypeStruct((S,K,2*W),F32)),
        in_specs=[pl.BlockSpec((1,T,W),lambda s:(s,0,0)),pl.BlockSpec((1,K,2*W),lambda s:(s,0,0)),pl.BlockSpec((1,T,W),lambda s:(s,0,0))],
        out_specs=(pl.BlockSpec((1,T,W),lambda s:(s,0,0)),pl.BlockSpec((1,K,2*W),lambda s:(s,0,0))),
        compiler_params=pltpu.CompilerParams(vmem_limit_bytes=32*2**20),
        cost_estimate=pl.CostEstimate(flops=10*S*heads*T*K*128,bytes_accessed=S*T*W*8,transcendentals=S*heads*T*K),
        name="cross_bwd")(q,kv,go)


MESH = pl.DeviceIdType.MESH
BLOCK = 144
PIECE = 36
WIDE = 1152


class Place:
    def __init__(self, sp):
        self.sp = sp
        self.f = lax.axis_index("fsdp")
        self.z = lax.axis_index("sp")
        self.core = self.f % 2
        self.x = (self.f // 2) % 2
        self.y = self.f // 4
        self.q = self.f // 2

    def flip(self, bit):
        step = {"core": 1, "x": 2, "y": 4}[bit]
        here = {"core": self.core, "x": self.x, "y": self.y}[bit]
        return (self.f + step * (1 - 2 * here), self.z)

    def along(self, r):
        return (self.f, (self.z + r) % self.sp)

    def peers(self):
        return [self.flip(b) for b in ("core", "x", "y")] + [self.along(r) for r in range(1, self.sp)]


def greet(place):
    barrier = pltpu.get_barrier_semaphore()
    peers = place.peers()
    for peer in peers:
        pl.semaphore_signal(barrier, inc=1, device_id=peer, device_id_type=MESH)
    pl.semaphore_wait(barrier, len(peers))


def remote(src, dst, send, recv, device):
    return pltpu.make_async_remote_copy(
        src_ref=src, dst_ref=dst, send_sem=send, recv_sem=recv, device_id=device, device_id_type=MESH
    )


class Gather:
    def __init__(self, place, chunks, send, recv):
        self.place, self.chunks, self.send, self.recv = place, chunks, send, recv

    def region(self, i, f):
        array, row, rows, columns, _ = self.chunks[i]
        return array.at[pl.ds(pl.multiple_of(row(f), 16), rows), columns]

    def copy(self, i, event, f, bit):
        src = self.region(i, f)
        return remote(src, src, self.send.at[i, event], self.recv.at[i, event], self.place.flip(bit))

    def bits(self, i):
        return ("x", "y") if self.chunks[i][4] == 0 else ("y", "x")

    def copies(self, i):
        p = self.place
        first, second = self.bits(i)
        f = p.f
        f_first = p.flip(first)[0]
        f_second = p.flip(second)[0]
        f_diagonal = f_first + f_second - f
        return [
            self.copy(i, 0, f, first),
            self.copy(i, 1, f, second),
            self.copy(i, 2, f_first, second),
            self.copy(i, 3, f, "core"),
            self.copy(i, 4, f_first, "core"),
            self.copy(i, 5, f_second, "core"),
            self.copy(i, 6, f_diagonal, "core"),
        ]

    def begin(self, i):
        c = self.copies(i)
        for e in (0, 1, 3):
            c[e].start()

    def middle(self, i):
        c = self.copies(i)
        c[0].wait_recv()
        c[2].start()
        c[4].start()

    def late(self, i):
        c = self.copies(i)
        c[1].wait_recv()
        c[5].start()
        c[2].wait_recv()
        c[6].start()

    def finish(self, i):
        c = self.copies(i)
        for e in (3, 4, 5, 6):
            c[e].wait_recv()
        for one in c:
            one.wait_send()


def gather_kernel(plan, sp, shards, down_shard, text_shard, *rest):
    n_out = len({o for o, _ in plan})
    outs = rest[:n_out]
    down, text = rest[n_out], rest[n_out + 1]
    landed, block, send, recv, zsend, zrecv, dsend, drecv, local_sem = rest[n_out + 2 :]
    p = Place(sp)
    greet(p)
    n = len(plan)
    ahead = 3

    def launch(i):
        if i < n:
            for r in range(1, sp):
                remote(
                    shards.at[i], landed.at[i, p.z], zsend.at[i, r - 1], zrecv.at[i, r - 1], p.along(r)
                ).start()
            landed[i, p.z] = shards[i]
        elif i == n:
            for r in range(1, sp):
                remote(down_shard, down_own, dsend.at[r - 1], drecv.at[p.z], p.along(r)).start()

    rows = down_shard.shape[0]
    down_own = down.at[pl.ds(pl.multiple_of(p.f * (sp * rows) + p.z * rows, 16), rows), :]
    for i in range(ahead):
        launch(i)
    pltpu.make_async_copy(down_shard, down_own, drecv.at[p.z]).start()
    trows = text_shard.shape[0]
    text_own = text.at[pl.ds(pl.multiple_of(p.f * trows, 16), trows), :]
    text_copy = pltpu.make_async_copy(text_shard, text_own, local_sem.at[2])
    text_copy.start()

    chunks = [
        (outs[o], lambda f: f * BLOCK, BLOCK, pl.ds(c, WIDE), k % 2) for k, (o, c) in enumerate(plan)
    ]
    chunks += [
        (down, lambda f, j=j: f * (sp * rows) + j * rows, rows, pl.ds(0, WIDE), (n + j) % 2) for j in range(sp)
    ]
    chunks += [(text, lambda f: f * trows, trows, pl.ds(k * WIDE, WIDE), (n + k) % 2) for k in range(2)]
    g = Gather(p, chunks, send, recv)

    def ready(i):
        if i < n:
            for r in range(1, sp):
                remote(
                    shards.at[i], landed.at[i, p.z], zsend.at[i, r - 1], zrecv.at[i, r - 1], p.along(r)
                ).wait_recv()
            slot = i % 2
            for zz in range(sp):
                block[slot, PIECE * zz : PIECE * (zz + 1), :] = landed[i, zz]
            copy = pltpu.make_async_copy(block.at[slot], g.region(i, p.f), local_sem.at[slot])
            copy.start()
            copy.wait()
        elif i < n + sp:
            remote(down_shard, down_own, dsend.at[0], drecv.at[i - n], p.along(1)).wait_recv()
        elif i == n + sp:
            text_copy.wait()

    total = len(chunks)
    for t in range(total + 2):
        if t < total:
            launch(t + ahead)
            ready(t)
            g.begin(t)
        if 0 <= t - 1 < total:
            g.middle(t - 1)
        if 0 <= t - 2 < total:
            g.late(t - 2)
    for i in range(total):
        g.finish(i)
    for i in range(n):
        for r in range(1, sp):
            remote(
                shards.at[i], landed.at[i, p.z], zsend.at[i, r - 1], zrecv.at[i, r - 1], p.along(r)
            ).wait_send()
    for r in range(1, sp):
        remote(down_shard, down_own, dsend.at[r - 1], drecv.at[p.z], p.along(r)).wait_send()


def gather_all(plan, widths, sp, shards, down_shard, text_shard):
    n = len(plan)
    total = n + sp + 2
    any_space = pl.BlockSpec(memory_space=pl.ANY)
    vmem = pl.BlockSpec(memory_space=pltpu.VMEM)
    dma = pltpu.SemaphoreType.DMA
    return pl.pallas_call(
        functools.partial(gather_kernel, plan, sp),
        out_shape=[jax.ShapeDtypeStruct((8 * BLOCK, w), BF) for w in widths]
        + [
            jax.ShapeDtypeStruct((8 * sp * down_shard.shape[0], WIDE), BF),
            jax.ShapeDtypeStruct((8 * text_shard.shape[0], 2 * WIDE), BF),
        ],
        in_specs=[vmem, any_space, any_space],
        out_specs=[any_space] * (len(widths) + 2),
        scratch_shapes=[
            pltpu.VMEM((n, sp, PIECE, WIDE), BF),
            pltpu.VMEM((2, BLOCK, WIDE), BF),
            dma((total, 7)),
            dma((total, 7)),
            dma((n, sp - 1)),
            dma((n, sp - 1)),
            dma((sp - 1,)),
            dma((sp,)),
            dma((3,)),
        ],
        compiler_params=pltpu.CompilerParams(
            collective_id=1, has_side_effects=True, vmem_limit_bytes=48 * 2**20
        ),
        name="gather_all",
    )(shards, down_shard, text_shard)


RING = 6
PIECES, DOWN, TEXT_ROWS, HALVES = range(4)
DELAY = 2


class Reduce:
    def __init__(self, place, chunks, sems):
        self.p, self.chunks = place, chunks
        self.core_send, self.core_recv, self.two_send = sems.core_send, sems.core_recv, sems.two_send
        self.two_recv, self.one_send, self.one_recv, self.load = sems.two_recv, sems.one_send, sems.one_recv, sems.load

    def slot(self, i):
        return self.chunks[i].slot

    def before(self, i):
        same = [k for k in range(i) if self.chunks[k].sums is self.chunks[i].sums and self.slot(k) == self.slot(i)]
        return same[-1] if same else None

    def after(self, i):
        return [k for k in range(i + 1, len(self.chunks)) if self.before(k) == i]

    def cross(self, i):
        c = self.chunks[i]
        return remote(
            c.sent(1 - self.p.core), c.arrived, self.core_send.at[i], self.core_recv.at[i], self.p.flip("core")
        )

    def start(self, i):
        if self.chunks[i].sent is not None:
            self.cross(i).start()

    def loads(self, i):
        c = self.chunks[i]
        sums = c.sums.at[self.slot(i)]
        out = []
        if c.kept is not None:
            out.append(pltpu.make_async_copy(c.kept(self.p.core), sums, self.load.at[i % 3, 0]))
            if c.sent is not None:
                out.append(pltpu.make_async_copy(c.arrived, c.other.at[i % 2], self.load.at[i % 3, 1]))
        else:
            out.append(pltpu.make_async_copy(c.arrived, sums, self.load.at[i % 3, 0]))
        return out

    def prefetch(self, i):
        k = self.before(i)
        if k is not None:
            self.two(k).wait_send()
            self.one(k).wait_send()
        if self.chunks[i].sent is not None:
            self.cross(i).wait_recv()
        for copy in self.loads(i):
            copy.start()

    def views(self, i):
        c, p = self.chunks[i], self.p
        sums = c.sums
        s = self.slot(i)
        if c.order == 0:
            return ("y", "x", sums.at[s, 1 - p.y], lambda k: (s, p.y, k), 1 - p.x, p.x)
        return ("x", "y", sums.at[s, :, 1 - p.x], lambda k: (s, k, p.x), 1 - p.y, p.y)

    def two(self, i):
        first, _, leaving, _, _, _ = self.views(i)
        return remote(leaving, self.chunks[i].two, self.two_send.at[i], self.two_recv.at[i], self.p.flip(first))

    def one(self, i):
        _, second, _, at, away, _ = self.views(i)
        return remote(
            self.chunks[i].sums.at[at(away)],
            self.chunks[i].one,
            self.one_send.at[i],
            self.one_recv.at[i],
            self.p.flip(second),
        )

    def add(self, i):
        c = self.chunks[i]
        for copy in self.loads(i):
            copy.wait()
        s = self.slot(i)
        if c.kept is not None and c.sent is not None:
            rows = c.sums.shape[-2]
            sums, other = c.sums, c.other

            def tile(t, _):
                r = pl.ds(pl.multiple_of(t * 16, 16), 16)
                for a in range(2):
                    for b in range(2):
                        sums[s, a, b, r, :] = (
                            sums[s, a, b, r, :].astype(F32) + other[i % 2, a, b, r, :].astype(F32)
                        ).astype(BF)
                return 0

            lax.fori_loop(0, rows // 16, tile, 0)
        self.two(i).start()

    def second(self, i):
        c = self.chunks[i]
        _, _, _, at, away, stay = self.views(i)
        self.two(i).wait_recv()
        sums, two = c.sums, c.two
        rows = sums.shape[-2]

        def fold(k):
            def tile(t, _):
                r = pl.ds(pl.multiple_of(t * 16, 16), 16)
                here = at(k) + (r, slice(None))
                sums[here] = (sums[here].astype(F32) + two[k, r, :].astype(F32)).astype(BF)
                return 0

            lax.fori_loop(0, rows // 16, tile, 0)

        fold(away)
        self.one(i).start()
        fold(stay)

    def third(self, i, store):
        c = self.chunks[i]
        _, _, _, at, _, stay = self.views(i)
        self.one(i).wait_recv()
        store(lambda r: c.sums[at(stay) + (r, slice(None))].astype(F32) + c.one[r, :].astype(F32))

    def drain(self, i, total):
        if self.chunks[i].sent is not None:
            self.cross(i).wait_send()
        if not self.after(i):
            self.two(i).wait_send()
            self.one(i).wait_send()


def along_z(p, sp, source, landing, send, recv):
    return [
        remote(source((p.z + r) % sp), landing(r - 1), send(r - 1), recv(r - 1), p.along(r)) for r in range(1, sp)
    ]


class Sums:
    def __init__(self, sp, plan, down, text, half):
        self.sp, self.plan, self.down, self.text, self.half = sp, plan, down, text, half
        self.blocks = len(plan) + (sp if down else 0)
        self.total = self.blocks + (2 if text else 0) + (2 if half else 0)
        shape = jax.ShapeDtypeStruct
        self.results, self.landings, self.scratch = {}, {}, {}
        block = (BLOCK, WIDE)
        if self.blocks:
            self.landings.update(arrived=shape((self.blocks, 2, 2) + block, BF))
            self.scratch.update(sums=pltpu.VMEM((RING, 2, 2) + block, BF))
            self.scratch.update(other=pltpu.VMEM((2, 2, 2) + block, BF))
            self.scratch.update(two=pltpu.VMEM((self.blocks, 2) + block, BF))
            self.scratch.update(one=pltpu.VMEM((self.blocks,) + block, BF))
        if plan:
            n = len(plan)
            self.results.update(piece=shape((n, PIECE, WIDE), F32))
            self.scratch.update(pieces=pltpu.VMEM((n, sp, PIECE, WIDE), BF))
            self.scratch.update(pieces_in=pltpu.VMEM((n, sp - 1, PIECE, WIDE), BF))
        if down:
            self.results.update(down=shape(block, F32))
            self.scratch.update(blocks_d=pltpu.VMEM((sp,) + block, BF))
            self.scratch.update(blocks_d_in=pltpu.VMEM((sp - 1,) + block, BF))
        if text:
            self.results.update(text=shape((2, text, WIDE), F32))
            self.landings.update(arrived_text=shape((2, 2, 2, text, WIDE), BF))
            self.scratch.update(sums_t=pltpu.VMEM((2, 2, 2, text, WIDE), BF))
            self.scratch.update(other_t=pltpu.VMEM((2, 2, 2, text, WIDE), BF))
            self.scratch.update(two_t=pltpu.VMEM((2, 2, text, WIDE), BF))
            self.scratch.update(one_t=pltpu.VMEM((2, text, WIDE), BF))
        if half:
            self.results.update(half=shape((2, PIECE, half), F32))
            self.landings.update(arrived_half=shape((2, 2, BLOCK, half), BF))
            self.scratch.update(sums_h=pltpu.VMEM((2, 2, 2, BLOCK, half), BF))
            self.scratch.update(two_h=pltpu.VMEM((2, 2, BLOCK, half), BF))
            self.scratch.update(one_h=pltpu.VMEM((2, BLOCK, half), BF))
            self.scratch.update(pieces_h=pltpu.VMEM((2, sp, PIECE, half), BF))
            self.scratch.update(pieces_h_in=pltpu.VMEM((2, sp - 1, PIECE, half), BF))
        dma = pltpu.SemaphoreType.DMA
        each = dma((self.total,))
        self.scratch.update(
            core_send=each, core_recv=each, two_send=each, two_recv=each, one_send=each, one_recv=each
        )
        self.scratch.update(load=dma((3, 2)))
        self.scratch.update(zsend=dma((self.total, sp - 1)))
        self.scratch.update(zrecv=dma((self.total, sp - 1)))

    def arrays(self, grads, down=None, text=None, halves=None):
        out = [g.reshape(2, 2, 2, BLOCK, g.shape[1]) for g in grads]
        if self.down:
            out.append(down.reshape(2, 2, 2, self.sp, BLOCK, WIDE))
        if self.text:
            out.append(text.reshape(2, 2, 2, self.text, 2 * WIDE))
        if self.half:
            out.append(halves.reshape(2, 2, 2, BLOCK, self.half))
        return out

    def bind(self, place, arrays, refs):
        arrays = list(arrays)
        self.p, self.refs = place, refs
        halves = arrays.pop() if self.half else None
        text = arrays.pop() if self.text else None
        down = arrays.pop() if self.down else None
        chunks = []
        if self.text:
            for k in range(2):
                view = lambda core, k=k: text.at[:, :, core, :, pl.ds(k * WIDE, WIDE)]
                chunks.append(SimpleNamespace(kept=view, sent=view, kind=TEXT_ROWS, index=k, slot=k))
                chunks[-1].__dict__.update(sums=refs.sums_t, other=refs.other_t, arrived=refs.arrived_text.at[k])
                chunks[-1].__dict__.update(two=refs.two_t.at[k], one=refs.one_t.at[k])
        blocks = []
        if self.down:
            for j in range(self.sp):
                view = lambda core, j=j: down.at[:, :, core, j]
                blocks.append(SimpleNamespace(kept=view, sent=view, kind=DOWN, index=j))
        for k, (o, c) in enumerate(self.plan):
            view = lambda core, o=o, c=c: arrays[o].at[:, :, core, :, pl.ds(c, WIDE)]
            blocks.append(SimpleNamespace(kept=view, sent=view, kind=PIECES, index=k))
        for k, c in enumerate(blocks):
            c.__dict__.update(sums=refs.sums, other=refs.other, arrived=refs.arrived.at[k], slot=k % RING)
            c.__dict__.update(two=refs.two.at[k], one=refs.one.at[k])
        chunks, plain = blocks, chunks
        if self.half:
            view = lambda core: halves.at[:, :, core]
            for k in range(2):
                chunks.append(SimpleNamespace(kept=None if k else view, sent=view if k else None, kind=HALVES, index=k, slot=k))
                chunks[-1].__dict__.update(sums=refs.sums_h, arrived=refs.arrived_half)
                chunks[-1].__dict__.update(two=refs.two_h.at[k], one=refs.one_h.at[k])
        chunks = chunks + plain
        for k, c in enumerate(chunks):
            c.order = k % 2
        self.chunks = chunks
        self.red = Reduce(place, chunks, refs)

    def sends(self, i):
        c, refs, p, sp = self.chunks[i], self.refs, self.p, self.sp
        k = c.index
        sems = (lambda r: refs.zsend.at[i, r], lambda r: refs.zrecv.at[i, r])
        if c.kind == PIECES:
            return along_z(p, sp, lambda z: refs.pieces.at[k, z], lambda r: refs.pieces_in.at[k, r], *sems)
        if c.kind == HALVES:
            return along_z(p, sp, lambda z: refs.pieces_h.at[k, z], lambda r: refs.pieces_h_in.at[k, r], *sems)
        if c.kind == DOWN and k == sp - 1:
            return along_z(p, sp, lambda z: refs.blocks_d.at[z], lambda r: refs.blocks_d_in.at[r], *sems)
        return []

    def store(self, i):
        c, sp = self.chunks[i], self.sp
        k = c.index

        def cut(target):
            def inner(value):
                for z in range(sp):
                    low = PIECE * z - PIECE * z % 16
                    high = PIECE * (z + 1)
                    high += -high % 16
                    rows = value(pl.ds(low, high - low))
                    target[k, z] = rows[PIECE * z - low : PIECE * z - low + PIECE].astype(BF)

            return inner

        def tiles(target, rows, kind):
            def inner(value):
                def tile(t, _):
                    r = pl.ds(pl.multiple_of(t * 16, 16), 16)
                    target[k, r, :] = value(r).astype(kind)
                    return 0

                lax.fori_loop(0, rows // 16, tile, 0)

            return inner

        if c.kind == PIECES:
            return cut(self.refs.pieces)
        if c.kind == HALVES:
            return cut(self.refs.pieces_h)
        if c.kind == DOWN:
            return tiles(self.refs.blocks_d, BLOCK, BF)
        return tiles(self.refs.text, self.text, F32)

    def last(self, i):
        c, refs, p, sp = self.chunks[i], self.refs, self.p, self.sp
        k = c.index
        for copy in self.sends(i):
            copy.wait_recv()
        if c.kind in (PIECES, HALVES):
            result, mine, others_in = (
                (refs.piece, refs.pieces, refs.pieces_in)
                if c.kind == PIECES
                else (refs.half, refs.pieces_h, refs.pieces_h_in)
            )
            result[k] = mine[k, p.z].astype(F32) + sum(others_in[k, r].astype(F32) for r in range(sp - 1))
        elif c.kind == DOWN and k == sp - 1:

            def tile(t, _):
                r = pl.ds(pl.multiple_of(t * 16, 16), 16)
                refs.down[r, :] = refs.blocks_d[p.z, r, :].astype(F32) + sum(
                    refs.blocks_d_in[a, r, :].astype(F32) for a in range(sp - 1)
                )
                return 0

            lax.fori_loop(0, BLOCK // 16, tile, 0)

    ahead = 4

    def begin(self):
        for i in range(min(self.ahead, self.total)):
            self.red.start(i)
        self.red.prefetch(0)

    def step(self, t):
        red, total = self.red, self.total
        if t + self.ahead < total:
            red.start(t + self.ahead)
        if t + 1 < total:
            red.prefetch(t + 1)
        if t < total:
            red.add(t)
        if 0 <= t - DELAY < total:
            red.second(t - DELAY)
        i = t - 2 * DELAY
        if 0 <= i < total:
            red.third(i, self.store(i))
            for copy in self.sends(i):
                copy.start()
        if 0 <= i - 2 < total:
            self.last(i - 2)

    def steps(self):
        return [functools.partial(self.step, t) for t in range(self.total + 2 * DELAY + 2)]

    def end(self):
        for i in range(self.total):
            self.red.drain(i, self.total)
            for copy in self.sends(i):
                copy.wait_send()


MOD_ROWS = 16
START, WAIT_RECV, WAIT_SEND = range(3)
TILE = 8


class Pairs:
    def __init__(self, p):
        self.p = p

    def owner(self, t):
        p = self.p
        return (p.f - p.core + t % 2, 2 * p.core + t // 2)

    def is_owner(self, t):
        p = self.p
        return jnp.logical_and(p.core == t % 2, p.z == 2 * p.core + t // 2)

    def source(self, z):
        p = self.p
        return (p.f - p.core + p.z // 2, z)

    def is_source(self, z):
        p = self.p
        return jnp.logical_and(p.core == p.z // 2, p.z == z)

    def mine(self):
        return 2 * (self.p.z % 2) + self.p.core


def to_owners(p, blocks, landing, send, recv, do):
    pairs = Pairs(p)
    for i in range(4):
        if do == WAIT_RECV:
            remote(blocks.at[0], landing.at[i], send.at[0], recv.at[i], pairs.owner(0)).wait_recv()
            continue
        far = remote(blocks.at[i], landing.at[p.z], send.at[i], recv.at[p.z], pairs.owner(i))
        near = pltpu.make_async_copy(blocks.at[i], landing.at[p.z], recv.at[p.z])

        @pl.when(jnp.logical_not(pairs.is_owner(i)))
        def _():
            far.start() if do == START else far.wait_send()

        if do == START:

            @pl.when(pairs.is_owner(i))
            def _():
                near.start()


def to_homes(p, blocks, landing, send, recv, do):
    pairs = Pairs(p)
    mine = pairs.mine()
    for i in range(4):
        if do == WAIT_RECV:
            remote(blocks.at[0], landing.at[i], send.at[0], recv.at[i], pairs.source(0)).wait_recv()
            continue
        far = remote(blocks.at[i], landing.at[mine], send.at[i], recv.at[mine], pairs.source(i))
        near = pltpu.make_async_copy(blocks.at[i], landing.at[mine], recv.at[mine])

        @pl.when(jnp.logical_not(pairs.is_source(i)))
        def _():
            far.start() if do == START else far.wait_send()

        if do == START:

            @pl.when(pairs.is_source(i))
            def _():
                near.start()


def others(p):
    out = []
    for m in range(1, 8):
        f = p.f
        for bit, step, here in ((1, 1, p.core), (2, 2, p.x), (4, 4, p.y)):
            if m & bit:
                f = f + step * (1 - 2 * here)
        out.append((f, p.z))
    return out


def group(p):
    sib = p.flip("core")[0]
    return [p.along(r) for r in range(1, p.sp)] + [(sib, (p.z + r) % p.sp) for r in range(1, p.sp)]


def greet_list(peers):
    barrier = pltpu.get_barrier_semaphore()
    for peer in peers:
        pl.semaphore_signal(barrier, inc=1, device_id=peer, device_id_type=MESH)
    pl.semaphore_wait(barrier, len(peers))


def front_kernel(
    sp,
    shards,
    ada,
    silu,
    vectors,
    text,
    resid,
    full,
    h_slot,
    modulation,
    vectors_all,
    text_mine,
    silu_in,
    landed,
    block,
    parts,
    parts_in,
    sums_in,
    vec_own,
    vec_in,
    text_in,
    h_blocks,
    send,
    recv,
    zsend,
    zrecv,
    csend,
    crecv,
    local_sem,
    s1,
    r1,
    s2,
    r2,
    s3,
    r3,
    sv1,
    rv1,
    sv2,
    rv2,
    st,
    rt,
    sh,
    rh,
    sx,
    rx,
):
    p = Place(sp)
    near = others(p)
    greet_list(near + group(p))
    here = lambda f: full.at[pl.ds(pl.multiple_of(f * BLOCK, 16), BLOCK), :]
    orders = [1 - p.core, p.core]

    def cond(m):
        f = near[m][0]
        return remote(silu.at[f * sp + p.z], silu_in.at[p.f], s1.at[m], r1.at[m], near[m])

    for m in range(7):
        cond(m).start()
    silu_in[p.f] = silu[p.f * sp + p.z]

    vec_own[...] = vectors[:TILE, :].astype(F32)
    vec_in[p.z] = vec_own[...]

    def vec_z(r):
        return remote(vec_own, vec_in.at[p.z], sv1.at[r - 1], rv1.at[r - 1], p.along(r))

    for r in range(1, sp):
        vec_z(r).start()

    def spread(k, r):
        return remote(
            shards.at[orders[k]], landed.at[orders[k], p.z], zsend.at[k, r - 1], zrecv.at[k, r - 1], p.along(r)
        )

    for k in range(2):
        for r in range(1, sp):
            spread(k, r).start()
        landed[orders[k], p.z] = shards[orders[k]]

    def text_z(r):
        z = (p.z + r) % sp
        return remote(text.at[z], text_in.at[p.z], st.at[r - 1], rt.at[r - 1], p.along(r))

    for r in range(1, sp):
        text_z(r).start()
    text_in[p.z] = text[p.z]

    for m in range(7):
        cond(m).wait_recv()
    rows = jnp.concatenate([silu_in[f][:2] for f in range(8)], axis=0).astype(BF)
    slots = 2
    for j in range(6):
        res = nn(rows, ada[:, j * WIDE : (j + 1) * WIDE])
        for f in range(8):
            parts[f, slots * j : slots * (j + 1), :] = res[slots * f : slots * (f + 1)]
    for f in range(8):
        parts[f, 6 * slots :, :] = jnp.zeros((MOD_ROWS - 6 * slots, WIDE), F32)

    def part(m):
        return remote(parts.at[near[m][0]], parts_in.at[m], s2.at[m], r2.at[m], near[m])

    for m in range(7):
        part(m).start()

    sibling = p.flip("core")[0]

    def cross():
        return remote(block.at[0], here(p.f), csend.at[0], crecv.at[0], p.flip("core"))

    def copies(k):
        f = sibling if k == 0 else p.f
        first, second = ("x", "y") if k == 0 else ("y", "x")
        step = p.flip(first)[0] - p.f
        return [
            remote(here(g), here(g), send.at[k, e], recv.at[k, e], p.flip(bit))
            for e, g, bit in ((0, f, first), (1, f, second), (2, f + step, second))
        ]

    for k in range(2):
        for r in range(1, sp):
            spread(k, r).wait_recv()
        for zz in range(sp):
            block[k, PIECE * zz : PIECE * (zz + 1), :] = landed[orders[k], zz]
        if k == 0:
            cross().start()
    own = pltpu.make_async_copy(block.at[1], here(p.f), local_sem.at[0])
    own.start()

    for m in range(7):
        part(m).wait_recv()
    parts[p.f] = parts[p.f] + sum(parts_in[m] for m in range(7))

    def total(r):
        return remote(parts.at[p.f], sums_in.at[r - 1], s3.at[r - 1], r3.at[r - 1], p.along(r))

    for r in range(1, sp):
        total(r).start()
    own.wait()
    for e in (0, 1):
        copies(1)[e].start()
    cross().wait_recv()
    for e in (0, 1):
        copies(0)[e].start()
    for r in range(1, sp):
        vec_z(r).wait_recv()

    def vec_f(m):
        return remote(vec_in, vectors_all.at[p.f], sv2.at[m], rv2.at[m], near[m])

    for m in range(7):
        vec_f(m).start()
    vectors_all[p.f] = vec_in[...]
    for r in range(1, sp):
        total(r).wait_recv()
    modulation[...] = parts[p.f] + sum(sums_in[r] for r in range(sp - 1))

    patches = resid.shape[1]
    step = 32
    for s in range(slots):
        for k in range(2):

            def tile(i, _):
                r = pl.multiple_of(i * step, step)
                v = resid[s, pl.ds(k * (patches // 2) + r, step), :]
                c = v - jnp.mean(v, axis=-1, keepdims=True)
                n = c * lax.rsqrt(jnp.mean(c * c, axis=-1, keepdims=True) + 1e-06)
                h = n * (1.0 + modulation[slots + s : slots + s + 1, :]) + modulation[s : s + 1, :]
                h_blocks[2 * s + k, pl.ds(r, step), :] = h.astype(BF)
                return 0

            lax.fori_loop(0, patches // 2 // step, tile, 0)
    to_owners(p, h_blocks, h_slot.at[0], sh, rh, START)
    for k in (1, 0):
        copies(k)[0].wait_recv()
        copies(k)[2].start()
    for r in range(1, sp):
        text_z(r).wait_recv()
    text_rows = text_in.shape[1]
    for zz in range(sp):
        text_mine[text_rows * zz : text_rows * (zz + 1), :] = text_in[zz]
    to_owners(p, h_blocks, h_slot.at[0], sh, rh, WAIT_RECV)
    swap = remote(h_slot.at[0], h_slot.at[1], sx.at[0], rx.at[0], p.flip("core"))
    swap.start()
    for k in range(2):
        copies(k)[1].wait_recv()
        copies(k)[2].wait_recv()
        for e in range(3):
            copies(k)[e].wait_send()
        for r in range(1, sp):
            spread(k, r).wait_send()
    cross().wait_send()
    for m in range(7):
        vec_f(m).wait_recv()
        vec_f(m).wait_send()
        part(m).wait_send()
        cond(m).wait_send()
    for r in range(1, sp):
        vec_z(r).wait_send()
        total(r).wait_send()
        text_z(r).wait_send()
    to_owners(p, h_blocks, h_slot.at[0], sh, rh, WAIT_SEND)
    swap.wait()


def front(sp, shards, ada, silu, vectors, text, resid):
    half = shards.shape[2]
    patches = resid.shape[1]
    text_rows, depth = text.shape[1:]
    dma = pltpu.SemaphoreType.DMA
    vmem = pl.BlockSpec(memory_space=pltpu.VMEM)
    any_space = pl.BlockSpec(memory_space=pl.ANY)
    shape = jax.ShapeDtypeStruct
    lanes = silu.shape[2]
    return pl.pallas_call(
        functools.partial(front_kernel, sp),
        out_shape=[
            shape((8 * BLOCK, half), BF),
            shape((2, 4, patches // 2, WIDE), BF),
            shape((MOD_ROWS, WIDE), F32),
            shape((8, sp, TILE, lanes), F32),
            shape((sp * text_rows, depth), BF),
            shape((8, TILE, lanes), F32),
        ],
        in_specs=[vmem] * 6,
        out_specs=[any_space] + [vmem] * 5,
        scratch_shapes=[
            pltpu.VMEM((2, sp, PIECE, half), BF),
            pltpu.VMEM((2, BLOCK, half), BF),
            pltpu.VMEM((8, MOD_ROWS, WIDE), F32),
            pltpu.VMEM((7, MOD_ROWS, WIDE), F32),
            pltpu.VMEM((sp - 1, MOD_ROWS, WIDE), F32),
            pltpu.VMEM((TILE, lanes), F32),
            pltpu.VMEM((sp, TILE, lanes), F32),
            pltpu.VMEM((sp, text_rows, depth), BF),
            pltpu.VMEM((4, patches // 2, WIDE), BF),
            dma((2, 3)),
            dma((2, 3)),
            dma((2, sp - 1)),
            dma((2, sp - 1)),
            dma((1,)),
            dma((1,)),
            dma((1,)),
        ]
        + [dma((7,))] * 4
        + [dma((sp - 1,))] * 4
        + [dma((7,))] * 2
        + [dma((sp - 1,))] * 2
        + [dma((4,))] * 2
        + [dma((1,))] * 2,
        compiler_params=pltpu.CompilerParams(
            collective_id=4, has_side_effects=True, vmem_limit_bytes=48 * 2**20
        ),
        name="front",
    )(shards, ada, silu, vectors, text, resid)


LAG = 2
FIRST = 5
PER = 2


def interleave(first, per, work, steps):
    steps = list(steps)
    for _ in range(first):
        steps.pop(0)()
    for k, piece in enumerate(work):
        piece()
        if steps and k % per == per - 1:
            steps.pop(0)()
    for step in steps:
        step()


class SumAlong:
    def __init__(self, p, part, landing, out, send, recv, send_again, recv_again):
        self.p, self.part, self.landing, self.out = p, part, landing, out
        self.sems = (send, recv, send_again, recv_again)

    def parts(self):
        send, recv = self.sems[:2]
        return along_z(
            self.p,
            self.p.sp,
            lambda z: self.part.at[z],
            lambda r: self.landing.at[r],
            lambda r: send.at[r],
            lambda r: recv.at[r],
        )

    def shares(self):
        own = self.out.at[self.p.z]
        send, recv = self.sems[2:]
        return [
            remote(own, own, send.at[r - 1], recv.at[r - 1], self.p.along(r)) for r in range(1, self.p.sp)
        ]

    def start(self):
        for copy in self.parts():
            copy.start()

    def sum(self):
        for copy in self.parts():
            copy.wait_recv()
        z = self.p.z
        for c in range(self.out.shape[2] // WIDE):
            cols = slice(c * WIDE, (c + 1) * WIDE)
            self.out[z, :, cols] = (
                self.part[z, :, cols].astype(F32)
                + sum(self.landing[r, :, cols].astype(F32) for r in range(self.p.sp - 1))
            ).astype(BF)
        for copy in self.shares():
            copy.start()

    def end(self):
        for copy in self.parts():
            copy.wait_send()
        for copy in self.shares():
            copy.wait()


def attend_kernel(plan, sp, heads, scale, n_out, *refs):
    shards, down_shard, text_shard, h_slot, qkv_w, text_mine = refs[:6]
    refs = refs[6:]
    outs = refs[:n_out]
    down, text, qkv, attn, kv = refs[n_out : n_out + 5]
    refs = refs[n_out + 5 :]
    landed, block, stack, heads_out, o_send, o_recv, o_full, text_w, kv_part, kv_in = refs[:10]
    send, recv, zsend, zrecv, dsend, drecv, local_sem, osem, hsend, hrecv = refs[10:20]
    p = Place(sp)
    along = SumAlong(p, kv_part, kv_in, kv, *refs[20:])
    greet_list([p.flip(b) for b in ("core", "x", "y")] + group(p))
    n = len(plan)
    rows = down_shard.shape[0]
    trows = text_shard.shape[0]
    down_own = down.at[pl.ds(pl.multiple_of(p.f * (sp * rows) + p.z * rows, 16), rows), :]
    text_own = text.at[pl.ds(pl.multiple_of(p.f * trows, 16), trows), :]
    text_copy = pltpu.make_async_copy(text_shard, text_own, local_sem.at[2])
    text_copy.start()

    chunks = [(text, lambda f: f * trows, trows, pl.ds(k * WIDE, WIDE), k % 2) for k in range(2)]
    chunks += [(outs[o], lambda f: f * BLOCK, BLOCK, pl.ds(c, WIDE), k % 2) for k, (o, c) in enumerate(plan)]
    chunks += [
        (down, lambda f, j=j: f * (sp * rows) + j * rows, rows, pl.ds(0, WIDE), (n + j) % 2) for j in range(sp)
    ]
    total = len(chunks)
    g = Gather(p, chunks, send, recv)

    def pieces(i):
        return [
            remote(shards.at[i], landed.at[i, p.z], zsend.at[i, r - 1], zrecv.at[i, r - 1], p.along(r))
            for r in range(1, sp)
        ]

    def down_z(r):
        return remote(down_shard, down_own, dsend.at[r - 1], drecv.at[p.z], p.along(r))

    def launch(i):
        if i < n:
            for copy in pieces(i):
                copy.start()
            landed[i, p.z] = shards[i]
        elif i == n:
            for r in range(1, sp):
                down_z(r).start()

    def ready(t):
        if t == 0:
            text_copy.wait()
        i = t - 2
        if 0 <= i < n:
            for copy in pieces(i):
                copy.wait_recv()
            slot = i % 2
            for zz in range(sp):
                block[slot, PIECE * zz : PIECE * (zz + 1), :] = landed[i, zz]
            copy = pltpu.make_async_copy(block.at[slot], g.region(t, p.f), local_sem.at[slot])
            copy.start()
            copy.wait()
        elif i >= n:
            remote(down_shard, down_own, dsend.at[0], drecv.at[i - n], p.along(1)).wait_recv()

    ahead = 3
    pltpu.make_async_copy(down_shard, down_own, drecv.at[p.z]).start()
    for i in range(ahead):
        launch(i)

    def step(t):
        if t < total:
            if t >= 2:
                launch(t - 2 + ahead)
            ready(t)
            g.begin(t)
        if 0 <= t - LAG < total:
            g.middle(t - LAG)
        if 0 <= t - 2 * LAG < total:
            g.late(t - 2 * LAG)

    T = qkv.shape[0]
    half = heads * HD
    tile = 256

    def project(i):
        hb = h_slot.shape[2]
        for b in range(tile // hb):
            k = i * (tile // hb) + b
            qkv[hb * k : hb * (k + 1), :] = nn(h_slot[k // 4, k % 4], qkv_w[...]).astype(BF)

    def stage():
        for i in range(3 * heads):
            stack[i] = jnp.zeros(stack.shape[1:], BF)
            stack[i, :, :HD] = qkv[:, i * HD : (i + 1) * HD]

    def head(h):
        def tile_of(i, _):
            q = stack[h, pl.ds(pl.multiple_of(i * tile, tile), tile), :]
            s = nt(q, stack[heads + h])
            m = jnp.max(s, axis=-1, keepdims=True)
            e = jnp.exp((s - m) * scale)
            l = jnp.sum(e, axis=-1, keepdims=True)
            r = nn(e.astype(BF), stack[2 * heads + h])
            heads_out[h, pl.ds(pl.multiple_of(i * tile, tile), tile), :] = (r / l).astype(BF)
            return 0

        lax.fori_loop(0, T // tile, tile_of, 0)

    def o_cross():
        return remote(o_send, o_recv, osem.at[0], osem.at[1], p.flip("core"))

    def o_out():
        for h in range(heads):
            o_send[:, h * HD : (h + 1) * HD] = heads_out[h, T // 2 :, :HD]
        o_cross().start()

    def o_home():
        o_cross().wait_recv()
        hb = T // 8
        low = p.core == 0
        for b in range(4):
            r = slice(hb * b, hb * (b + 1))
            mine = jnp.concatenate([heads_out[h, r, :HD] for h in range(heads)], axis=1)
            other = o_recv[r, :]
            o_full[b, :, :half] = jnp.where(low, mine, other)
            o_full[b, :, half:] = jnp.where(low, other, mine)
        to_homes(p, o_full, attn, hsend, hrecv, START)

    text_load = pltpu.make_async_copy(text, text_w, local_sem.at[3])

    def text_start():
        g.finish(0)
        g.finish(1)
        text_load.start()

    krows = kv.shape[1]

    def kv_product():
        text_load.wait()
        for c in range(2):
            cols = slice(c * WIDE, (c + 1) * WIDE)
            res = nn(text_mine[...], text_w[:, cols])
            for z in range(sp):
                kv_part[z, :, cols] = res[krows * z : krows * (z + 1)].astype(BF)
        along.start()

    work = [functools.partial(project, i) for i in range(T // tile)]
    work += [text_start, stage]
    work += [functools.partial(head, h) for h in range(heads)]
    work.insert(-5, kv_product)
    work.insert(-2, along.sum)
    work += [o_out, o_home]
    interleave(FIRST, PER, work, [functools.partial(step, t) for t in range(total + 2 * LAG)])
    for i in range(2, total):
        g.finish(i)
    for i in range(n):
        for copy in pieces(i):
            copy.wait_send()
    for r in range(1, sp):
        down_z(r).wait_send()
    to_homes(p, o_full, attn, hsend, hrecv, WAIT_RECV)
    to_homes(p, o_full, attn, hsend, hrecv, WAIT_SEND)
    o_cross().wait_send()
    along.end()


def attend(plan, widths, sp, heads, scale, shards, down_shard, text_shard, h_slot, qkv_w, text_mine):
    n = len(plan)
    total = n + sp + 2
    T = 8 * h_slot.shape[2]
    half = heads * HD
    trows = text_shard.shape[0]
    krows = text_mine.shape[0] // sp
    any_space = pl.BlockSpec(memory_space=pl.ANY)
    vmem = pl.BlockSpec(memory_space=pltpu.VMEM)
    dma = pltpu.SemaphoreType.DMA
    shape = jax.ShapeDtypeStruct
    return pl.pallas_call(
        functools.partial(attend_kernel, plan, sp, heads, scale, len(widths)),
        out_shape=[shape((8 * BLOCK, w), BF) for w in widths]
        + [
            shape((8 * sp * down_shard.shape[0], WIDE), BF),
            shape((8 * trows, 2 * WIDE), BF),
            shape((T, 3 * half), BF),
            shape((4, T // 8, WIDE), BF),
            shape((sp, krows, 2 * WIDE), BF),
        ],
        in_specs=[vmem, any_space, any_space, vmem, vmem, vmem],
        out_specs=[any_space] * (len(widths) + 2) + [vmem] * 3,
        scratch_shapes=[
            pltpu.VMEM((n, sp, PIECE, WIDE), BF),
            pltpu.VMEM((2, BLOCK, WIDE), BF),
            pltpu.VMEM((3 * heads, T, 128), BF),
            pltpu.VMEM((heads, T, 128), BF),
            pltpu.VMEM((T // 2, half), BF),
            pltpu.VMEM((T // 2, half), BF),
            pltpu.VMEM((4, T // 8, WIDE), BF),
            pltpu.VMEM((8 * trows, 2 * WIDE), BF),
            pltpu.VMEM((sp, krows, 2 * WIDE), BF),
            pltpu.VMEM((sp - 1, krows, 2 * WIDE), BF),
            dma((total, 7)),
            dma((total, 7)),
            dma((n, sp - 1)),
            dma((n, sp - 1)),
            dma((sp - 1,)),
            dma((sp,)),
            dma((4,)),
            dma((2,)),
            dma((4,)),
            dma((4,)),
            dma((sp - 1,)),
            dma((sp - 1,)),
            dma((sp - 1,)),
            dma((sp - 1,)),
        ],
        compiler_params=pltpu.CompilerParams(
            collective_id=5, has_side_effects=True, vmem_limit_bytes=56 * 2**20
        ),
        cost_estimate=pl.CostEstimate(flops=2**34, bytes_accessed=2**28, transcendentals=2**23),
        name="attend",
    )(shards, down_shard, text_shard, h_slot, qkv_w, text_mine)


def split(refs, *counts):
    out = []
    for c in counts:
        out.append(refs[:c])
        refs = refs[c:]
    return out + [refs]


def attend_back_kernel(make, sp, heads, scale, *refs):
    sums = make()
    n_in = sums.n_in
    arrays, (go_blocks, qkv, kv_part), results, (g, kv), landings, scratch, rest = split(
        refs, n_in, 3, len(sums.results), 2, len(sums.landings), len(sums.scratch)
    )
    names = SimpleNamespace()
    for group_names, group_refs in ((sums.results, results), (sums.landings, landings), (sums.scratch, scratch)):
        names.__dict__.update(zip(group_names, group_refs))
    go_in, go_away, go_half, part, acc, gsend, grecv, esem, ksend, krecv = rest
    p = Place(sp)
    greet_list([p.flip(b) for b in ("core", "x", "y")] + group(p))
    sums.bind(p, arrays, names)
    to_owners(p, go_blocks, go_in, gsend, grecv, START)
    sums.begin()
    kv[p.z] = kv_part[...]

    def shares():
        own = kv.at[p.z]
        return [remote(own, own, ksend.at[r - 1], krecv.at[r - 1], p.along(r)) for r in range(1, sp)]

    T = qkv.shape[0]
    half = heads * HD
    rows = T // 8

    def cross():
        return remote(go_away, go_half.at[1], esem.at[0], esem.at[1], p.flip("core"))

    def cut():
        to_owners(p, go_blocks, go_in, gsend, grecv, WAIT_RECV)
        low = p.core == 0
        for b in range(4):
            first, other = go_in[b, :, :half], go_in[b, :, half:]
            go_half[0, b] = jnp.where(low, first, other)
            go_away[b] = jnp.where(low, other, first)
        cross().start()

    tile = 256

    def head(h):
        if h == 0:
            cross().wait_recv()
        for k in range(3):
            c = (k * heads + h) * HD
            part[k, :, :HD] = qkv[:, c : c + HD]
        for b in range(8):
            part[3, rows * b : rows * (b + 1), :HD] = go_half[b // 4, b % 4, :, h * HD : (h + 1) * HD]
        acc[...] = jnp.zeros(acc.shape, F32)

        def cols(i, _):
            sl = pl.ds(pl.multiple_of(i * tile, tile), tile)
            q, go = part[0, sl, :], part[3, sl, :]
            k, v = part[1], part[2]
            s = nt(k, q)
            m = jnp.max(s, axis=0, keepdims=True)
            e = jnp.exp((s - m) * scale)
            pr = e * (1.0 / jnp.sum(e, axis=0, keepdims=True))
            t = nt(v, go) * pr
            ds = (t - pr * jnp.sum(t, axis=0, keepdims=True)).astype(BF)
            acc[0] += nn(ds, q)
            acc[1] += nn(pr.astype(BF), go)
            part[0, sl, :] = (tn(ds, k) * scale).astype(BF)
            return 0

        lax.fori_loop(0, T // tile, cols, 0)
        c = h * HD
        g[:, c : c + HD] = part[0, :, :HD]
        c += half
        g[:, c : c + HD] = (acc[0, :, :HD] * scale).astype(BF)
        c += half
        g[:, c : c + HD] = acc[1, :, :HD].astype(BF)

    part[...] = jnp.zeros(part.shape, BF)
    work = [cut] + [functools.partial(head, h) for h in range(heads)]
    work.insert(2, lambda: [copy.start() for copy in shares()])
    interleave(2, 1, work, sums.steps())
    sums.end()
    for copy in shares():
        copy.wait()
    to_owners(p, go_blocks, go_in, gsend, grecv, WAIT_SEND)
    cross().wait_send()


def attend_back(plan, sp, heads, scale, grads, go_blocks, qkv, kv_part):
    def make():
        sums = Sums(sp, plan, False, 0, 0)
        sums.n_in = len(grads)
        return sums

    sums = make()
    T = qkv.shape[0]
    half = heads * HD
    any_space = pl.BlockSpec(memory_space=pl.ANY)
    vmem = pl.BlockSpec(memory_space=pltpu.VMEM)
    dma = pltpu.SemaphoreType.DMA
    out = pl.pallas_call(
        functools.partial(attend_back_kernel, make, sp, heads, scale),
        out_shape=list(sums.results.values()) + [jax.ShapeDtypeStruct(a, BF) for a in (qkv.shape, (sp,) + kv_part.shape)] + list(sums.landings.values()),
        in_specs=[any_space] * len(grads) + [vmem] * 3,
        out_specs=[vmem] * (len(sums.results) + 2) + [any_space] * len(sums.landings),
        scratch_shapes=list(sums.scratch.values())
        + [
            pltpu.VMEM((4, T // 8, WIDE), BF),
            pltpu.VMEM((4, T // 8, half), BF),
            pltpu.VMEM((2, 4, T // 8, half), BF),
            pltpu.VMEM((4, T, 128), BF),
            pltpu.VMEM((2, T, 128), F32),
            dma((4,)),
            dma((4,)),
            dma((2,)),
            dma((sp - 1,)),
            dma((sp - 1,)),
        ],
        compiler_params=pltpu.CompilerParams(
            collective_id=6, has_side_effects=True, vmem_limit_bytes=60 * 2**20
        ),
        cost_estimate=pl.CostEstimate(flops=2**35, bytes_accessed=2**28, transcendentals=2**23),
        name="attend_back",
    )(*sums.arrays(grads), go_blocks, qkv, kv_part)
    return out[:3]


def finish_kernel(make, sp, *refs):
    sums = make()
    arrays, (gh, resid, grad_one, mod, small), results, (out, small_all), landings, scratch, rest = split(
        refs, sums.n_in, 5, len(sums.results), 2, len(sums.landings), len(sums.scratch)
    )
    names = SimpleNamespace()
    for group_names, group_refs in ((sums.results, results), (sums.landings, landings), (sums.scratch, scratch)):
        names.__dict__.update(zip(group_names, group_refs))
    home, gh_in, blocks, mine, mine_in, partial, hsend, hrecv, esem, s1, r1, s2, r2 = rest
    p = Place(sp)
    near = others(p)
    greet_list(near + group(p))
    sums.bind(p, arrays, names)

    def cross():
        return remote(gh.at[1], gh_in, esem.at[0], esem.at[1], p.flip("core"))

    cross().start()
    sums.begin()
    half_rows = gh.shape[2]
    slots = resid.shape[0]

    def add():
        cross().wait_recv()
        step = 16
        for b in range(4):

            def tile(i, _):
                r = pl.ds(pl.multiple_of(i * step, step), step)
                blocks[b, r, :] = (gh[0, b, r, :] + gh_in[b, r, :]).astype(BF)
                return 0

            lax.fori_loop(0, half_rows // step, tile, 0)
        to_homes(p, blocks, home, hsend, hrecv, START)

    def tail():
        to_homes(p, blocks, home, hsend, hrecv, WAIT_RECV)
        step = 32
        partial[...] = jnp.zeros(partial.shape, F32)
        for b in range(4):
            s, k = b // 2, b % 2

            def tile(i, _):
                start = pl.multiple_of(i * step, step)
                r = pl.ds(k * half_rows + start, step)
                v = resid[s, r, :]
                c = v - jnp.mean(v, axis=-1, keepdims=True)
                inv = lax.rsqrt(jnp.mean(c * c, axis=-1, keepdims=True) + 1e-06)
                n = c * inv
                g = home[b, pl.ds(start, step), :].astype(F32)
                gn = g * n
                partial[s, 0] += sum(g[8 * j : 8 * j + 8] for j in range(step // 8))
                partial[s, 1] += sum(gn[8 * j : 8 * j + 8] for j in range(step // 8))
                d = g * (1.0 + mod[slots + s : slots + s + 1, :])
                back = d - jnp.mean(d, axis=-1, keepdims=True) - n * jnp.mean(d * n, axis=-1, keepdims=True)
                out[s, r, :] = grad_one[s, r, :] + back * inv
                return 0

            lax.fori_loop(0, half_rows // step, tile, 0)
        mine[...] = small[...]
        for s in range(slots):
            for j in range(2):
                mine[slots * j + s : slots * j + s + 1, :] = jnp.sum(partial[s, j], axis=0, keepdims=True)
        for copy in along():
            copy.start()

    def along():
        return [remote(mine, mine_in.at[r - 1], s1.at[r - 1], r1.at[r - 1], p.along(r)) for r in range(1, sp)]

    def share(m):
        own = small_all.at[p.f]
        return remote(own, own, s2.at[m], r2.at[m], near[m])

    def total():
        for copy in along():
            copy.wait_recv()
        small_all[p.f] = mine[...] + sum(mine_in[r] for r in range(sp - 1))
        for m in range(7):
            share(m).start()

    idle = lambda: None
    interleave(1, 1, [add, idle, idle, idle, tail, idle, total], sums.steps())
    sums.end()
    for m in range(7):
        share(m).wait()
    for copy in along():
        copy.wait_send()
    to_homes(p, blocks, home, hsend, hrecv, WAIT_SEND)
    cross().wait_send()


def finish(sp, down, text, halves, gh, resid, grad_one, mod, small):
    half = halves.shape[1]

    def make():
        sums = Sums(sp, [], True, text.shape[0] // 8, half)
        sums.n_in = 3
        return sums

    sums = make()
    rows = gh.shape[2]
    any_space = pl.BlockSpec(memory_space=pl.ANY)
    vmem = pl.BlockSpec(memory_space=pltpu.VMEM)
    dma = pltpu.SemaphoreType.DMA
    shape = jax.ShapeDtypeStruct
    out = pl.pallas_call(
        functools.partial(finish_kernel, make, sp),
        out_shape=list(sums.results.values())
        + [shape(resid.shape, F32), shape((8,) + small.shape, F32)]
        + list(sums.landings.values()),
        in_specs=[any_space] * 3 + [vmem] * 5,
        out_specs=[vmem] * (len(sums.results) + 2) + [any_space] * len(sums.landings),
        scratch_shapes=list(sums.scratch.values())
        + [
            pltpu.VMEM((4, rows, WIDE), BF),
            pltpu.VMEM((4, rows, WIDE), F32),
            pltpu.VMEM((4, rows, WIDE), BF),
            pltpu.VMEM(small.shape, F32),
            pltpu.VMEM((sp - 1,) + small.shape, F32),
            pltpu.VMEM((2, 2, 8, WIDE), F32),
            dma((4,)),
            dma((4,)),
            dma((2,)),
            dma((sp - 1,)),
            dma((sp - 1,)),
            dma((7,)),
            dma((7,)),
        ],
        compiler_params=pltpu.CompilerParams(
            collective_id=7, has_side_effects=True, vmem_limit_bytes=60 * 2**20
        ),
        name="finish",
    )(*sums.arrays([], down, text, halves), gh, resid, grad_one, mod, small)
    return out[:5]


def temporal_kernel(heads, scale, trip, go, out, g):
    slots, rows, width = go.shape
    lanes = lax.broadcasted_iota(jnp.int32, (width, 128), 0) // HD
    member = (lanes == lax.broadcasted_iota(jnp.int32, (width, 128), 1)).astype(F32).astype(BF)
    across = lax.broadcasted_iota(jnp.int32, (128, width), 1) // HD
    member_t = (across == lax.broadcasted_iota(jnp.int32, (128, width), 0)).astype(F32).astype(BF)
    pairs = [(a, b) for a in range(slots) for b in range(slots)]

    def part(a, k):
        return trip[a, :, k * width : (k + 1) * width].astype(F32)

    def per_head(x):
        high = x.astype(BF)
        return nn(high, member) + nn((x - high.astype(F32)).astype(BF), member)

    def wide(x):
        return nn(x.astype(BF), member_t)

    s = {(a, b): per_head(part(a, 0) * part(b, 1)) * scale for a, b in pairs}
    p = {}
    for a in range(slots):
        m = functools.reduce(jnp.maximum, [s[a, b] for b in range(slots)])
        e = [jnp.exp(s[a, b] - m) for b in range(slots)]
        total = sum(e)
        for b in range(slots):
            p[a, b] = e[b] / total
    pw = {k: wide(v) for k, v in p.items()}
    d = [go[a].astype(F32) for a in range(slots)]
    for a in range(slots):
        out[a] = sum(pw[a, b] * part(b, 2) for b in range(slots)).astype(BF)
    for b in range(slots):
        g[b, :, 2 * width :] = sum(pw[a, b] * d[a] for a in range(slots)).astype(BF)
    dp = {(a, b): per_head(d[a] * part(b, 2)) for a, b in pairs}
    ds = {}
    for a in range(slots):
        mean = sum(dp[a, b] * p[a, b] for b in range(slots))
        for b in range(slots):
            ds[a, b] = wide(p[a, b] * (dp[a, b] - mean))
    for a in range(slots):
        g[a, :, :width] = (scale * sum(ds[a, b] * part(b, 1) for b in range(slots))).astype(BF)
        g[a, :, width : 2 * width] = (scale * sum(ds[b, a] * part(b, 0) for b in range(slots))).astype(BF)


def temporal(trip, go, heads, scale):
    slots, patches, width = go.shape
    rows = 64
    block = lambda w: pl.BlockSpec((slots, rows, w), lambda i: (0, i, 0))
    return pl.pallas_call(
        functools.partial(temporal_kernel, heads, scale),
        grid=(patches // rows,),
        out_shape=[jax.ShapeDtypeStruct((slots, patches, w), BF) for w in (width, 3 * width)],
        in_specs=[block(3 * width), block(width)],
        out_specs=[block(width), block(3 * width)],
        compiler_params=pltpu.CompilerParams(vmem_limit_bytes=48 * 2**20),
        cost_estimate=pl.CostEstimate(flops=2**32, bytes_accessed=2**24, transcendentals=2**16),
        name="temporal",
    )(trip, go)


HEADS = 16
EPS = 1e-06
HIGHEST = lax.Precision.HIGHEST
BOTH = ("fsdp", "sp")
PLAN = (
    [(0, 0), (1, 0), (2, 0)] + [(3, k * WIDE) for k in range(4)] + [(4, k * WIDE) for k in range(3)] + [(5, 0)]
)


def normalize(values):
    centred = values - jnp.mean(values, axis=-1, keepdims=True)
    return centred * lax.rsqrt(jnp.mean(centred * centred, axis=-1, keepdims=True) + EPS)


def normalize_back(values, grad_out):
    return jax.vjp(normalize, values)[1](grad_out)[0]


def gelu_tanh(values):
    return jax.nn.gelu(values, approximate=True)


def scatter(grad):
    part = lax.psum_scatter(grad.astype(BF), "fsdp", scatter_dimension=0, tiled=True)
    return lax.psum_scatter(part, "sp", scatter_dimension=0, tiled=True).astype(F32)


def sum_along(parts, sp):
    z = lax.axis_index("sp")
    total = lax.dynamic_index_in_dim(parts, z, 0, keepdims=False).astype(F32)
    for r in range(1, sp):
        part = lax.dynamic_index_in_dim(parts, (z + r) % sp, 0, keepdims=False)
        total += lax.ppermute(part, "sp", [(k, (k + r) % sp) for k in range(sp)]).astype(F32)
    return total.astype(BF)


class Moves:
    def __init__(self, fsdp, sp, slots):
        self.fsdp, self.sp, self.slots = fsdp, sp, slots
        self.core = lax.axis_index("fsdp") % 2
        self.z = lax.axis_index("sp")
        self.rounds = []
        for r in range(sp):
            pairs = []
            for f in range(fsdp):
                for z in range(sp):
                    t = (z - r) % sp
                    pairs.append((f * sp + z, (f - f % 2 + t % 2) * sp + slots * (f % 2) + t // 2))
            self.rounds.append(pairs)
        self.swap = [(f, f ^ 1) for f in range(fsdp)]

    def out(self, tokens):
        rows = tokens.shape[0] // self.sp
        blocks = tokens.reshape(self.sp, rows, tokens.shape[1])
        got = []
        for r, pairs in enumerate(self.rounds):
            t = (self.z - r) % self.sp
            block = lax.dynamic_index_in_dim(blocks, t, 0, keepdims=False)
            got.append(lax.ppermute(block, BOTH, pairs))
        return jnp.roll(jnp.stack(got), self.mine(), axis=0).reshape(tokens.shape)

    def home(self, tokens):
        rows = tokens.shape[0] // self.sp
        tokens = jnp.roll(tokens.reshape(self.sp, rows, -1), -self.mine(), axis=0).reshape(tokens.shape)
        out = jnp.zeros((self.sp, rows, tokens.shape[1]), tokens.dtype)
        for r, pairs in enumerate(self.rounds):
            back = lax.ppermute(tokens[r * rows : (r + 1) * rows], BOTH, [(b, a) for a, b in pairs])
            t = (self.z - r) % self.sp
            out = lax.dynamic_update_index_in_dim(out, back, t, 0)
        return out.reshape(tokens.shape)

    def mine(self):
        return 2 * (self.z % 2) + self.core

    def exchange(self, array):
        return lax.ppermute(array, "fsdp", self.swap)


def local(
    residual_in,
    condition,
    text_states,
    slot_item,
    cotangent,
    w_ada,
    w_qkv,
    w_out,
    w_cross_q,
    w_cross_kv,
    w_cross_out,
    w_up,
    w_down,
    w_temp_qkv,
    w_temp_out,
    g_cross,
    g_temp,
    t_gate,
):
    slots, patches, width = residual_in.shape[1:]
    text_local, text_width = text_states.shape[2:]
    sp = lax.axis_size("sp")
    fsdp = lax.axis_size("fsdp")
    f_index, z_index = lax.axis_index("fsdp"), lax.axis_index("sp")
    rows = w_qkv.shape[0]
    tok = slots * patches
    scale = HD ** (-0.5)
    moves = Moves(fsdp, sp, slots)
    core = f_index % 2

    def gather(shard):
        return lax.all_gather(shard.astype(BF), BOTH, axis=0, tiled=True)

    chosen = slot_item[0]
    video = (chosen[-1] == 0).astype(F32)

    cond = condition[0]
    cond_used = jnp.where((chosen == 0)[:, None], cond[0][None], cond[1][None])
    silu_low = jax.nn.silu(cond_used).astype(BF)
    text = text_states[0]
    text_used = jnp.where((chosen == 0)[:, None, None], text[0][None], text[1][None])
    kv_rows = w_cross_kv.shape[0]
    text_cut = text_used.reshape(slots * text_local, fsdp, sp, kv_rows)
    heads_half = HEADS // 2
    half = heads_half * HD
    resid = residual_in[0]
    normed_one = normalize(resid)
    small_slice = fsdp == 8 and sp == 4
    stacked_vectors = jnp.stack([g_cross, g_temp, t_gate]).astype(BF)
    if small_slice:
        qkv_shards = w_qkv.astype(BF).reshape(rows, 3, 2, half).transpose(2, 0, 1, 3).reshape(2, rows, 3 * half)
        silu_blocks = silu_low.astype(F32).reshape(slots, fsdp * sp, rows).transpose(1, 0, 2)
        qkv_half, h_slot, mod_rows, vectors, text_mine, silu_rows = front(
            sp,
            qkv_shards,
            w_ada.astype(BF),
            jnp.pad(silu_blocks, ((0, 0), (0, TILE - slots), (0, 0))),
            jnp.pad(stacked_vectors, ((0, 2 * TILE - 3), (0, 0))),
            text_cut.transpose(2, 0, 1, 3).reshape(sp, slots * text_local, fsdp * kv_rows),
            resid,
        )
        silu_rows = silu_rows[:, :slots].reshape(fsdp * slots, rows).astype(BF)
        modulation = mod_rows[: 6 * slots].reshape(6, slots, 1, width)
        vectors = vectors[:, :, :3].transpose(2, 0, 1, 3).reshape(3, width)
        low = [w.astype(BF) for w in (w_out, w_cross_q, w_cross_out, w_up, w_temp_qkv, w_temp_out)]
        shards = jnp.stack([low[o][:, c : c + width] for o, c in PLAN])
        (
            out_full,
            cross_q_full,
            cross_out_full,
            up_full,
            temp_qkv_full,
            temp_out_full,
            down_full,
            _,
            qkv,
            attn_tok,
            kv_all,
        ) = attend(
            PLAN,
            [w.shape[1] for w in low],
            sp,
            heads_half,
            scale,
            shards,
            w_down.astype(BF),
            w_cross_kv.astype(BF),
            h_slot,
            qkv_half,
            text_mine,
        )
        h_slot = h_slot.reshape(2 * tok, width)
        attn_tok = attn_tok.reshape(tok, width)
        kv_all = (
            kv_all.reshape(sp, slots, text_local, 2 * width)
            .transpose(1, 0, 2, 3)
            .reshape(slots, sp * text_local, 2 * width)
        )
        shift_one, scale_one, gate_one, shift_two, scale_two, gate_two = (modulation[i] for i in range(6))
    else:
        silu_all = lax.all_gather(silu_low, "fsdp", axis=0, tiled=True)
        silu_rows = lax.dynamic_slice_in_dim(silu_all, (f_index * sp + z_index) * rows, rows, 1)
        modulation = lax.psum(
            lax.psum_scatter(nn(silu_rows, w_ada.astype(BF)), "fsdp", scatter_dimension=0, tiled=True), "sp"
        ).reshape(slots, 6, 1, width)
        shift_one, scale_one, gate_one, shift_two, scale_two, gate_two = (modulation[:, i] for i in range(6))
        vectors = lax.all_gather(stacked_vectors, BOTH, axis=1, tiled=True).astype(F32)
        qkv_half = lax.dynamic_index_in_dim(
            gather(w_qkv).reshape(width, 3, 2, half), core, 2, keepdims=False
        ).reshape(width, 3 * half)
        out_full = gather(w_out)
        cross_q_full = gather(w_cross_q)
        cross_out_full = gather(w_cross_out)
        up_full = gather(w_up)
        down_full = gather(w_down)
        temp_qkv_full = gather(w_temp_qkv)
        temp_out_full = gather(w_temp_out)
        kv_weight = lax.all_gather(w_cross_kv.astype(BF), "fsdp", axis=0, tiled=True)
        text_mine = lax.all_to_all(text_cut, "sp", split_axis=2, concat_axis=0, tiled=True)
        text_mine = text_mine.reshape(sp * slots * text_local, fsdp * kv_rows)
        kv_part = lax.psum_scatter(nn(text_mine, kv_weight), "sp", scatter_dimension=0, tiled=True).astype(BF)
        kv_all = (
            lax.all_gather(kv_part.reshape(1, slots, text_local, 2 * width), "sp", axis=0, tiled=True)
            .transpose(1, 0, 2, 3)
            .reshape(slots, sp * text_local, 2 * width)
        )
        h_one = (normed_one * (1.0 + scale_one) + shift_one).astype(BF).reshape(tok, width)
        h_mine = moves.out(h_one)
        h_slot = jnp.concatenate([h_mine, moves.exchange(h_mine)], axis=0)
        qkv = nn(h_slot, qkv_half).astype(BF)
        o_slot = spatial_fwd(qkv, heads_half, scale)
        o_mine = o_slot[:tok]
        o_other = moves.exchange(o_slot[tok:])
        o_full = jnp.where(
            core == 0,
            jnp.concatenate([o_mine, o_other], axis=1),
            jnp.concatenate([o_other, o_mine], axis=1),
        )
        attn_tok = moves.home(o_full)
    gain_cross, gain_temp, temp_gate = vectors[0], vectors[1], vectors[2]
    branch_one = nn(attn_tok, out_full).reshape(slots, patches, width)
    x_one = resid + gate_one * branch_one

    normed_two = normalize(x_one)
    cross_in = (normed_two * gain_cross).astype(BF).reshape(tok, width)
    query_c = nn(cross_in, cross_q_full).astype(BF).reshape(slots, patches, width)
    cross_out = cross_fwd(query_c, kv_all, HEADS, scale).reshape(tok, width)
    branch_two = nn(cross_out, cross_out_full).reshape(slots, patches, width)
    x_two = x_one + branch_two

    normed_three = normalize(x_two)
    h_three = (normed_three * (1.0 + scale_two) + shift_two).astype(BF).reshape(tok, width)
    up_proj = nn(h_three, up_full)
    activated = gelu_tanh(up_proj).astype(BF)
    branch_three = nn(activated, down_full).reshape(slots, patches, width)
    x_three = x_two + gate_two * branch_three

    normed_four = normalize(x_three)
    temp_in = (normed_four * gain_temp).astype(BF).reshape(tok, width)
    trip = nn(temp_in, temp_qkv_full).astype(BF).reshape(slots, patches, 3 * width)
    grad_out = cotangent[0].astype(F32)
    grad_b4 = (grad_out * (video * temp_gate)).astype(BF).reshape(tok, width)
    grad_to = nt(grad_b4, temp_out_full).astype(BF).reshape(slots, patches, width)
    temp_out, grad_trip = temporal(trip, grad_to, HEADS, scale)
    temp_out = temp_out.reshape(tok, width)
    grad_trip = grad_trip.reshape(tok, 3 * width)
    branch_four = nn(temp_out, temp_out_full).reshape(slots, patches, width)
    output = x_three + (video * temp_gate) * branch_four

    grad_tgate = video * jnp.sum(grad_out * branch_four, axis=(0, 1))
    grad_wto = tn(temp_out, grad_b4)
    grad_wtq = tn(temp_in, grad_trip)
    grad_temp_in = nt(grad_trip, temp_qkv_full).reshape(slots, patches, width)
    grad_gtemp = jnp.sum(grad_temp_in * normed_four, axis=(0, 1))
    grad_three = grad_out + normalize_back(x_three, grad_temp_in * gain_temp)

    grad_gate_two = jnp.sum(grad_three * branch_three, axis=1)
    grad_b3 = (grad_three * gate_two).astype(BF).reshape(tok, width)
    grad_wdown = tn(activated, grad_b3)
    grad_act = nt(grad_b3, down_full)
    grad_up = jax.vjp(gelu_tanh, up_proj)[1](grad_act)[0].astype(BF)
    grad_wup = tn(h_three, grad_up)
    grad_h_three = nt(grad_up, up_full).reshape(slots, patches, width)
    grad_shift_two = jnp.sum(grad_h_three, axis=1)
    grad_scale_two = jnp.sum(grad_h_three * normed_three, axis=1)
    grad_two = grad_three + normalize_back(x_two, grad_h_three * (1.0 + scale_two))

    grad_b2 = grad_two.astype(BF).reshape(tok, width)
    grad_wco = tn(cross_out, grad_b2)
    grad_co = nt(grad_b2, cross_out_full).astype(BF).reshape(slots, patches, width)
    grad_qc, grad_kv = cross_bwd(query_c, kv_all, grad_co, HEADS, scale)
    grad_qc = grad_qc.reshape(tok, width)
    grad_kv = (
        grad_kv.reshape(slots, sp, text_local, 2 * width)
        .transpose(1, 0, 2, 3)
        .reshape(sp * slots * text_local, 2 * width)
        .astype(BF)
    )
    grad_wcq = tn(cross_in, grad_qc)
    grad_cross_in = nt(grad_qc, cross_q_full).reshape(slots, patches, width)
    grad_gcross = jnp.sum(grad_cross_in * normed_two, axis=(0, 1))
    grad_one = grad_two + normalize_back(x_one, grad_cross_in * gain_cross)

    grad_gate_one = jnp.sum(grad_one * branch_one, axis=1)
    grad_b1 = (grad_one * gate_one).astype(BF).reshape(tok, width)
    grad_wout = tn(attn_tok, grad_b1)
    grad_attn = nt(grad_b1, out_full).astype(BF)
    if small_slice:
        late = [g.astype(BF) for g in (grad_wout, grad_wcq, grad_wco, grad_wup, grad_wtq, grad_wto)]
        pieces, grad_qkv, grad_kv = attend_back(
            PLAN,
            sp,
            heads_half,
            scale,
            late,
            grad_attn.reshape(sp, tok // sp, width),
            qkv,
            sum_along(grad_kv.reshape(sp, slots * text_local, 2 * width), sp),
        )
        grad_kv = grad_kv.reshape(sp * slots * text_local, 2 * width)
        own = [jnp.concatenate([pieces[k] for k, (o, _) in enumerate(PLAN) if o == i], axis=1) for i in range(len(late))]
        own_out, own_cq, own_co, own_up, own_tq, own_to = own
    else:
        go_mine = moves.out(grad_attn)
        low_half, high_half = go_mine[:, :half], go_mine[:, half:]
        go_other = moves.exchange(jnp.where(core == 0, high_half, low_half))
        go_slot = jnp.concatenate([jnp.where(core == 0, low_half, high_half), go_other], axis=0)
        grad_qkv = spatial_bwd(qkv, go_slot, heads_half, scale)
        grad_kv = lax.all_gather(
            lax.psum_scatter(grad_kv, "sp", scatter_dimension=0, tiled=True), "sp", axis=0, tiled=True
        )
    grad_wqkv_half = tn(h_slot, grad_qkv).astype(BF)
    grad_wckv = tn(text_mine, grad_kv)
    gh_slot = nt(grad_qkv, qkv_half)
    known = [grad_gate_one, grad_shift_two, grad_scale_two, grad_gate_two]
    known_vectors = [grad_gcross, grad_gtemp, grad_tgate]
    if small_slice:
        zero = jnp.zeros((slots, width), F32)
        own_down, own_text, own_half, input_grad, small_sp = finish(
            sp,
            grad_wdown.astype(BF),
            grad_wckv.astype(BF),
            grad_wqkv_half,
            gh_slot.reshape(2, sp, tok // sp, width),
            resid,
            grad_one,
            mod_rows,
            jnp.concatenate([zero, zero] + known + [jnp.stack(known_vectors + [zero[0]])], axis=0),
        )
        own_text = own_text.transpose(1, 0, 2).reshape(kv_rows, 2 * width)
        own_half = jnp.where(core == 0, own_half, own_half[::-1])
        own_qkv = own_half.reshape(2, rows, 3, half).transpose(1, 2, 0, 3).reshape(rows, 3 * width)
    else:
        grad_h_one = moves.home((gh_slot[:tok] + moves.exchange(gh_slot[tok:])).astype(BF))
        grad_h_one = grad_h_one.astype(F32).reshape(slots, patches, width)
        input_grad = grad_one + normalize_back(resid, grad_h_one * (1.0 + scale_one))
        new = [jnp.sum(grad_h_one, axis=1), jnp.sum(grad_h_one * normed_one, axis=1)]
        small = jnp.concatenate(new + known + [jnp.stack(known_vectors)], axis=0)
        small_sp = jnp.sum(
            lax.all_gather(small, BOTH, axis=0).reshape(fsdp, sp, slots * 6 + 3, width), axis=1
        )
    grad_mod = small_sp[:, : slots * 6].reshape(fsdp, 6, slots, width).transpose(0, 2, 1, 3)
    grad_mod = grad_mod.reshape(fsdp * slots, 6 * width)
    grad_wada = jnp.dot(silu_rows.astype(F32).T, grad_mod, precision=HIGHEST, preferred_element_type=F32)
    grad_vec = lax.dynamic_slice_in_dim(
        jnp.sum(small_sp[:, slots * 6 : slots * 6 + 3], axis=0), (f_index * sp + z_index) * rows, rows, 1
    )
    if not small_slice:
        wide = grad_wqkv_half.reshape(width, 3, 1, half)
        zeros = jnp.zeros_like(wide)
        grad_wqkv = jnp.where(
            core == 0, jnp.concatenate([wide, zeros], axis=2), jnp.concatenate([zeros, wide], axis=2)
        ).reshape(width, 3 * width)
        own_qkv, own_out, own_cq, own_co = scatter(grad_wqkv), scatter(grad_wout), scatter(grad_wcq), scatter(grad_wco)
        own_up, own_down, own_tq, own_to = scatter(grad_wup), scatter(grad_wdown), scatter(grad_wtq), scatter(grad_wto)
        own_text = lax.psum_scatter(grad_wckv.astype(BF), "fsdp", scatter_dimension=0, tiled=True).astype(F32)
    return (
        output[None],
        input_grad[None],
        grad_wada,
        own_qkv,
        own_out,
        own_cq,
        own_text,
        own_co,
        own_up,
        own_down,
        own_tq,
        own_to,
        grad_vec[0],
        grad_vec[1],
        grad_vec[2],
    )


def solution(mesh):
    P = jax.sharding.PartitionSpec
    tokens = P("fsdp", None, "sp", None)
    weight = P(BOTH, None)
    vector = P(BOTH)
    return jax.shard_map(
        local,
        mesh=mesh,
        in_specs=(tokens, P("fsdp", None, None), tokens, P("fsdp", None), tokens)
        + (weight,) * 10
        + (vector,) * 3,
        out_specs=(tokens, tokens) + (weight,) * 10 + (vector,) * 3,
        check_vma=False,
    )
```

```python
import functools
from types import SimpleNamespace
import jax, jax.numpy as jnp
from jax import lax
from jax.experimental import pallas as pl
from jax.experimental.pallas import tpu as pltpu
HD=72
F32=jnp.float32; BF=jnp.bfloat16
def nt(a,b): return lax.dot_general(a,b,(((1,),(1,)),((),())),preferred_element_type=F32)
def tn(a,b): return lax.dot_general(a,b,(((0,),(0,)),((),())),preferred_element_type=F32)
def nn(a,b): return jnp.dot(a,b,preferred_element_type=F32)

def spatial_fwd_kernel(heads, scale, qkv, o, st, os):
    T = qkv.shape[0]
    W = heads*HD
    for i in range(3*heads):
        st[i] = jnp.zeros(st.shape[1:], BF)
        st[i, :, :HD] = qkv[:, i*HD:(i+1)*HD]
    tile = 256
    def head(h, _):
        k = st[heads+h]; v = st[2*heads+h]
        def rows(i, _):
            q = st[h, pl.ds(pl.multiple_of(i*tile,tile), tile), :]
            s = nt(q,k)
            m = jnp.max(s,axis=-1,keepdims=True)
            e = jnp.exp((s-m)*scale)
            l = jnp.sum(e,axis=-1,keepdims=True)
            r = nn(e.astype(BF), v)
            os[h, pl.ds(pl.multiple_of(i*tile,tile), tile), :] = (r/l).astype(BF)
            return 0
        lax.fori_loop(0, T//tile, rows, 0)
        return 0
    lax.fori_loop(0, heads, head, 0)
    for h in range(heads):
        o[:, h*HD:(h+1)*HD] = os[h, :, :HD]

def spatial_fwd(qkv, heads, scale):
    T=qkv.shape[0]
    return pl.pallas_call(functools.partial(spatial_fwd_kernel,heads,scale),
        out_shape=jax.ShapeDtypeStruct((T,heads*HD),BF),
        in_specs=[pl.BlockSpec(memory_space=pltpu.VMEM)],
        out_specs=pl.BlockSpec(memory_space=pltpu.VMEM),
        scratch_shapes=[pltpu.VMEM((3*heads,T,128),BF),pltpu.VMEM((heads,T,128),BF)],
        compiler_params=pltpu.CompilerParams(vmem_limit_bytes=48*2**20),
        cost_estimate=pl.CostEstimate(flops=4*heads*T*T*128,bytes_accessed=T*heads*HD*8,transcendentals=heads*T*T),
        name="spatial_fwd")(qkv)

def spatial_bwd_kernel(heads, scale, qkv, go, g, st, gs, acc):
    T = qkv.shape[0]
    for i in range(3*heads):
        st[i] = jnp.zeros(st.shape[1:], BF)
        st[i, :, :HD] = qkv[:, i*HD:(i+1)*HD]
    for h in range(heads):
        gs[h] = jnp.zeros(gs.shape[1:], BF)
        gs[h, :, :HD] = go[:, h*HD:(h+1)*HD]
    tile = 256
    def head(h, _):
        k = st[heads+h]; v = st[2*heads+h]
        acc[...] = jnp.zeros(acc.shape, F32)
        def cols(i, _):
            sl = pl.ds(pl.multiple_of(i*tile,tile), tile)
            q = st[h, sl, :]; gq_in = gs[h, sl, :]
            s = nt(k,q)
            m = jnp.max(s,axis=0,keepdims=True)
            e = jnp.exp((s-m)*scale)
            p = e * (1.0/jnp.sum(e,axis=0,keepdims=True))
            dp = nt(v,gq_in)
            t = dp*p
            d = jnp.sum(t,axis=0,keepdims=True)
            ds = (t-p*d).astype(BF)
            acc[0] += nn(ds,q)
            acc[1] += nn(p.astype(BF),gq_in)
            st[h, sl, :] = (tn(ds,k)*scale).astype(BF)
            return 0
        lax.fori_loop(0, T//tile, cols, 0)
        st[heads+h] = (acc[0]*scale).astype(BF)
        st[2*heads+h] = acc[1].astype(BF)
        return 0
    lax.fori_loop(0, heads, head, 0)
    for i in range(3*heads):
        g[:, i*HD:(i+1)*HD] = st[i, :, :HD]

def spatial_bwd(qkv, go, heads, scale):
    T=qkv.shape[0]
    return pl.pallas_call(functools.partial(spatial_bwd_kernel,heads,scale),
        out_shape=jax.ShapeDtypeStruct((T,3*heads*HD),BF),
        in_specs=[pl.BlockSpec(memory_space=pltpu.VMEM)]*2,
        out_specs=pl.BlockSpec(memory_space=pltpu.VMEM),
        scratch_shapes=[pltpu.VMEM((3*heads,T,128),BF),pltpu.VMEM((heads,T,128),BF),pltpu.VMEM((2,T,128),F32)],
        compiler_params=pltpu.CompilerParams(vmem_limit_bytes=56*2**20),
        cost_estimate=pl.CostEstimate(flops=10*heads*T*T*128,bytes_accessed=T*heads*HD*16,transcendentals=heads*T*T),
        name="spatial_bwd")(qkv, go)

def cross_fwd_kernel(heads, scale, q, kv, o):
    S,T,W = q.shape
    for h in range(heads):
        c = slice(h*HD,(h+1)*HD); cv = slice(W+h*HD, W+(h+1)*HD)
        s = nt(q[0,:,c], kv[0,:,c])
        m = jnp.max(s,axis=-1,keepdims=True)
        e = jnp.exp((s-m)*scale)
        l = jnp.sum(e,axis=-1,keepdims=True)
        o[0,:,c] = (nn(e.astype(BF), kv[0,:,cv])/l).astype(BF)

def cross_fwd(q, kv, heads, scale):
    S,T,W = q.shape; K=kv.shape[1]
    return pl.pallas_call(functools.partial(cross_fwd_kernel,heads,scale),
        grid=(S,),
        out_shape=jax.ShapeDtypeStruct((S,T,W),BF),
        in_specs=[pl.BlockSpec((1,T,W),lambda s:(s,0,0)),pl.BlockSpec((1,K,2*W),lambda s:(s,0,0))],
        out_specs=pl.BlockSpec((1,T,W),lambda s:(s,0,0)),
        compiler_params=pltpu.CompilerParams(vmem_limit_bytes=32*2**20),
        cost_estimate=pl.CostEstimate(flops=4*S*heads*T*K*128,bytes_accessed=S*T*W*4,transcendentals=S*heads*T*K),
        name="cross_fwd")(q,kv)

def cross_bwd_kernel(heads, scale, q, kv, go, gq, gkv):
    S,T,W = q.shape
    for h in range(heads):
        c = slice(h*HD,(h+1)*HD); cv = slice(W+h*HD, W+(h+1)*HD)
        qh=q[0,:,c]; kh=kv[0,:,c]; vh=kv[0,:,cv]; gh=go[0,:,c]
        s = nt(kh,qh)
        m = jnp.max(s,axis=0,keepdims=True)
        e = jnp.exp((s-m)*scale)
        p = e*(1.0/jnp.sum(e,axis=0,keepdims=True))
        dp = nt(vh,gh)
        t = dp*p
        ds = (t-p*jnp.sum(t,axis=0,keepdims=True)).astype(BF)
        gq[0,:,c] = (tn(ds,kh)*scale).astype(BF)
        gkv[0,:,c] = nn(ds,qh)*scale
        gkv[0,:,cv] = nn(p.astype(BF),gh)

def cross_bwd(q, kv, go, heads, scale):
    S,T,W = q.shape; K=kv.shape[1]
    return pl.pallas_call(functools.partial(cross_bwd_kernel,heads,scale),
        grid=(S,),
        out_shape=(jax.ShapeDtypeStruct((S,T,W),BF),jax.ShapeDtypeStruct((S,K,2*W),F32)),
        in_specs=[pl.BlockSpec((1,T,W),lambda s:(s,0,0)),pl.BlockSpec((1,K,2*W),lambda s:(s,0,0)),pl.BlockSpec((1,T,W),lambda s:(s,0,0))],
        out_specs=(pl.BlockSpec((1,T,W),lambda s:(s,0,0)),pl.BlockSpec((1,K,2*W),lambda s:(s,0,0))),
        compiler_params=pltpu.CompilerParams(vmem_limit_bytes=32*2**20),
        cost_estimate=pl.CostEstimate(flops=10*S*heads*T*K*128,bytes_accessed=S*T*W*8,transcendentals=S*heads*T*K),
        name="cross_bwd")(q,kv,go)


MESH = pl.DeviceIdType.MESH
BLOCK = 144
PIECE = 36
WIDE = 1152


class Place:
    def __init__(self, sp):
        self.sp = sp
        self.f = lax.axis_index("fsdp")
        self.z = lax.axis_index("sp")
        self.core = self.f % 2
        self.x = (self.f // 2) % 2
        self.y = self.f // 4
        self.q = self.f // 2

    def flip(self, bit):
        step = {"core": 1, "x": 2, "y": 4}[bit]
        here = {"core": self.core, "x": self.x, "y": self.y}[bit]
        return (self.f + step * (1 - 2 * here), self.z)

    def along(self, r):
        return (self.f, (self.z + r) % self.sp)

    def peers(self):
        return [self.flip(b) for b in ("core", "x", "y")] + [self.along(r) for r in range(1, self.sp)]


def greet(place):
    barrier = pltpu.get_barrier_semaphore()
    peers = place.peers()
    for peer in peers:
        pl.semaphore_signal(barrier, inc=1, device_id=peer, device_id_type=MESH)
    pl.semaphore_wait(barrier, len(peers))


def remote(src, dst, send, recv, device):
    return pltpu.make_async_remote_copy(
        src_ref=src, dst_ref=dst, send_sem=send, recv_sem=recv, device_id=device, device_id_type=MESH
    )


class Gather:
    def __init__(self, place, chunks, send, recv):
        self.place, self.chunks, self.send, self.recv = place, chunks, send, recv

    def region(self, i, f):
        array, row, rows, columns, _ = self.chunks[i]
        return array.at[pl.ds(pl.multiple_of(row(f), 16), rows), columns]

    def copy(self, i, event, f, bit):
        src = self.region(i, f)
        return remote(src, src, self.send.at[i, event], self.recv.at[i, event], self.place.flip(bit))

    def bits(self, i):
        return ("x", "y") if self.chunks[i][4] == 0 else ("y", "x")

    def copies(self, i):
        p = self.place
        first, second = self.bits(i)
        f = p.f
        f_first = p.flip(first)[0]
        f_second = p.flip(second)[0]
        f_diagonal = f_first + f_second - f
        return [
            self.copy(i, 0, f, first),
            self.copy(i, 1, f, second),
            self.copy(i, 2, f_first, second),
            self.copy(i, 3, f, "core"),
            self.copy(i, 4, f_first, "core"),
            self.copy(i, 5, f_second, "core"),
            self.copy(i, 6, f_diagonal, "core"),
        ]

    def begin(self, i):
        c = self.copies(i)
        for e in (0, 1, 3):
            c[e].start()

    def middle(self, i):
        c = self.copies(i)
        c[0].wait_recv()
        c[2].start()
        c[4].start()

    def late(self, i):
        c = self.copies(i)
        c[1].wait_recv()
        c[5].start()
        c[2].wait_recv()
        c[6].start()

    def finish(self, i):
        c = self.copies(i)
        for e in (3, 4, 5, 6):
            c[e].wait_recv()
        for one in c:
            one.wait_send()


def gather_kernel(plan, sp, shards, down_shard, text_shard, *rest):
    n_out = len({o for o, _ in plan})
    outs = rest[:n_out]
    down, text = rest[n_out], rest[n_out + 1]
    landed, block, send, recv, zsend, zrecv, dsend, drecv, local_sem = rest[n_out + 2 :]
    p = Place(sp)
    greet(p)
    n = len(plan)
    ahead = 3

    def launch(i):
        if i < n:
            for r in range(1, sp):
                remote(
                    shards.at[i], landed.at[i, p.z], zsend.at[i, r - 1], zrecv.at[i, r - 1], p.along(r)
                ).start()
            landed[i, p.z] = shards[i]
        elif i == n:
            for r in range(1, sp):
                remote(down_shard, down_own, dsend.at[r - 1], drecv.at[p.z], p.along(r)).start()

    rows = down_shard.shape[0]
    down_own = down.at[pl.ds(pl.multiple_of(p.f * (sp * rows) + p.z * rows, 16), rows), :]
    for i in range(ahead):
        launch(i)
    pltpu.make_async_copy(down_shard, down_own, drecv.at[p.z]).start()
    trows = text_shard.shape[0]
    text_own = text.at[pl.ds(pl.multiple_of(p.f * trows, 16), trows), :]
    text_copy = pltpu.make_async_copy(text_shard, text_own, local_sem.at[2])
    text_copy.start()

    chunks = [
        (outs[o], lambda f: f * BLOCK, BLOCK, pl.ds(c, WIDE), k % 2) for k, (o, c) in enumerate(plan)
    ]
    chunks += [
        (down, lambda f, j=j: f * (sp * rows) + j * rows, rows, pl.ds(0, WIDE), (n + j) % 2) for j in range(sp)
    ]
    chunks += [(text, lambda f: f * trows, trows, pl.ds(k * WIDE, WIDE), (n + k) % 2) for k in range(2)]
    g = Gather(p, chunks, send, recv)

    def ready(i):
        if i < n:
            for r in range(1, sp):
                remote(
                    shards.at[i], landed.at[i, p.z], zsend.at[i, r - 1], zrecv.at[i, r - 1], p.along(r)
                ).wait_recv()
            slot = i % 2
            for zz in range(sp):
                block[slot, PIECE * zz : PIECE * (zz + 1), :] = landed[i, zz]
            copy = pltpu.make_async_copy(block.at[slot], g.region(i, p.f), local_sem.at[slot])
            copy.start()
            copy.wait()
        elif i < n + sp:
            remote(down_shard, down_own, dsend.at[0], drecv.at[i - n], p.along(1)).wait_recv()
        elif i == n + sp:
            text_copy.wait()

    total = len(chunks)
    for t in range(total + 2):
        if t < total:
            launch(t + ahead)
            ready(t)
            g.begin(t)
        if 0 <= t - 1 < total:
            g.middle(t - 1)
        if 0 <= t - 2 < total:
            g.late(t - 2)
    for i in range(total):
        g.finish(i)
    for i in range(n):
        for r in range(1, sp):
            remote(
                shards.at[i], landed.at[i, p.z], zsend.at[i, r - 1], zrecv.at[i, r - 1], p.along(r)
            ).wait_send()
    for r in range(1, sp):
        remote(down_shard, down_own, dsend.at[r - 1], drecv.at[p.z], p.along(r)).wait_send()


def gather_all(plan, widths, sp, shards, down_shard, text_shard):
    n = len(plan)
    total = n + sp + 2
    any_space = pl.BlockSpec(memory_space=pl.ANY)
    vmem = pl.BlockSpec(memory_space=pltpu.VMEM)
    dma = pltpu.SemaphoreType.DMA
    return pl.pallas_call(
        functools.partial(gather_kernel, plan, sp),
        out_shape=[jax.ShapeDtypeStruct((8 * BLOCK, w), BF) for w in widths]
        + [
            jax.ShapeDtypeStruct((8 * sp * down_shard.shape[0], WIDE), BF),
            jax.ShapeDtypeStruct((8 * text_shard.shape[0], 2 * WIDE), BF),
        ],
        in_specs=[vmem, any_space, any_space],
        out_specs=[any_space] * (len(widths) + 2),
        scratch_shapes=[
            pltpu.VMEM((n, sp, PIECE, WIDE), BF),
            pltpu.VMEM((2, BLOCK, WIDE), BF),
            dma((total, 7)),
            dma((total, 7)),
            dma((n, sp - 1)),
            dma((n, sp - 1)),
            dma((sp - 1,)),
            dma((sp,)),
            dma((3,)),
        ],
        compiler_params=pltpu.CompilerParams(
            collective_id=1, has_side_effects=True, vmem_limit_bytes=48 * 2**20
        ),
        name="gather_all",
    )(shards, down_shard, text_shard)


RING = 6
PIECES, DOWN, TEXT_ROWS, HALVES = range(4)
DELAY = 2


class Reduce:
    def __init__(self, place, chunks, sems):
        self.p, self.chunks = place, chunks
        self.core_send, self.core_recv, self.two_send = sems.core_send, sems.core_recv, sems.two_send
        self.two_recv, self.one_send, self.one_recv, self.load = sems.two_recv, sems.one_send, sems.one_recv, sems.load

    def slot(self, i):
        return self.chunks[i].slot

    def before(self, i):
        same = [k for k in range(i) if self.chunks[k].sums is self.chunks[i].sums and self.slot(k) == self.slot(i)]
        return same[-1] if same else None

    def after(self, i):
        return [k for k in range(i + 1, len(self.chunks)) if self.before(k) == i]

    def cross(self, i):
        c = self.chunks[i]
        return remote(
            c.sent(1 - self.p.core), c.arrived, self.core_send.at[i], self.core_recv.at[i], self.p.flip("core")
        )

    def start(self, i):
        if self.chunks[i].sent is not None:
            self.cross(i).start()

    def loads(self, i):
        c = self.chunks[i]
        sums = c.sums.at[self.slot(i)]
        out = []
        if c.kept is not None:
            out.append(pltpu.make_async_copy(c.kept(self.p.core), sums, self.load.at[i % 3, 0]))
            if c.sent is not None:
                out.append(pltpu.make_async_copy(c.arrived, c.other.at[i % 2], self.load.at[i % 3, 1]))
        else:
            out.append(pltpu.make_async_copy(c.arrived, sums, self.load.at[i % 3, 0]))
        return out

    def prefetch(self, i):
        k = self.before(i)
        if k is not None:
            self.two(k).wait_send()
            self.one(k).wait_send()
        if self.chunks[i].sent is not None:
            self.cross(i).wait_recv()
        for copy in self.loads(i):
            copy.start()

    def views(self, i):
        c, p = self.chunks[i], self.p
        sums = c.sums
        s = self.slot(i)
        if c.order == 0:
            return ("y", "x", sums.at[s, 1 - p.y], lambda k: (s, p.y, k), 1 - p.x, p.x)
        return ("x", "y", sums.at[s, :, 1 - p.x], lambda k: (s, k, p.x), 1 - p.y, p.y)

    def two(self, i):
        first, _, leaving, _, _, _ = self.views(i)
        return remote(leaving, self.chunks[i].two, self.two_send.at[i], self.two_recv.at[i], self.p.flip(first))

    def one(self, i):
        _, second, _, at, away, _ = self.views(i)
        return remote(
            self.chunks[i].sums.at[at(away)],
            self.chunks[i].one,
            self.one_send.at[i],
            self.one_recv.at[i],
            self.p.flip(second),
        )

    def add(self, i):
        c = self.chunks[i]
        for copy in self.loads(i):
            copy.wait()
        s = self.slot(i)
        if c.kept is not None and c.sent is not None:
            rows = c.sums.shape[-2]
            sums, other = c.sums, c.other

            def tile(t, _):
                r = pl.ds(pl.multiple_of(t * 16, 16), 16)
                for a in range(2):
                    for b in range(2):
                        sums[s, a, b, r, :] = (
                            sums[s, a, b, r, :].astype(F32) + other[i % 2, a, b, r, :].astype(F32)
                        ).astype(BF)
                return 0

            lax.fori_loop(0, rows // 16, tile, 0)
        self.two(i).start()

    def second(self, i):
        c = self.chunks[i]
        _, _, _, at, away, stay = self.views(i)
        self.two(i).wait_recv()
        sums, two = c.sums, c.two
        rows = sums.shape[-2]

        def fold(k):
            def tile(t, _):
                r = pl.ds(pl.multiple_of(t * 16, 16), 16)
                here = at(k) + (r, slice(None))
                sums[here] = (sums[here].astype(F32) + two[k, r, :].astype(F32)).astype(BF)
                return 0

            lax.fori_loop(0, rows // 16, tile, 0)

        fold(away)
        self.one(i).start()
        fold(stay)

    def third(self, i, store):
        c = self.chunks[i]
        _, _, _, at, _, stay = self.views(i)
        self.one(i).wait_recv()
        store(lambda r: c.sums[at(stay) + (r, slice(None))].astype(F32) + c.one[r, :].astype(F32))

    def drain(self, i, total):
        if self.chunks[i].sent is not None:
            self.cross(i).wait_send()
        if not self.after(i):
            self.two(i).wait_send()
            self.one(i).wait_send()


def along_z(p, sp, source, landing, send, recv):
    return [
        remote(source((p.z + r) % sp), landing(r - 1), send(r - 1), recv(r - 1), p.along(r)) for r in range(1, sp)
    ]


class Sums:
    def __init__(self, sp, plan, down, text, half):
        self.sp, self.plan, self.down, self.text, self.half = sp, plan, down, text, half
        self.blocks = len(plan) + (sp if down else 0)
        self.total = self.blocks + (2 if text else 0) + (2 if half else 0)
        shape = jax.ShapeDtypeStruct
        self.results, self.landings, self.scratch = {}, {}, {}
        block = (BLOCK, WIDE)
        if self.blocks:
            self.landings.update(arrived=shape((self.blocks, 2, 2) + block, BF))
            self.scratch.update(sums=pltpu.VMEM((min(RING, self.blocks), 2, 2) + block, BF))
            self.scratch.update(other=pltpu.VMEM((2, 2, 2) + block, BF))
            self.scratch.update(two=pltpu.VMEM((self.blocks, 2) + block, BF))
            self.scratch.update(one=pltpu.VMEM((self.blocks,) + block, BF))
        if plan:
            n = len(plan)
            self.results.update(piece=shape((n, PIECE, WIDE), F32))
            self.scratch.update(pieces=pltpu.VMEM((n, sp, PIECE, WIDE), BF))
            self.scratch.update(pieces_in=pltpu.VMEM((n, sp - 1, PIECE, WIDE), BF))
        if down:
            self.results.update(down=shape(block, F32))
            self.scratch.update(blocks_d=pltpu.VMEM((sp,) + block, BF))
            self.scratch.update(blocks_d_in=pltpu.VMEM((sp - 1,) + block, BF))
        if text:
            self.results.update(text=shape((2, text, WIDE), F32))
            self.landings.update(arrived_text=shape((2, 2, 2, text, WIDE), BF))
            self.scratch.update(sums_t=pltpu.VMEM((2, 2, 2, text, WIDE), BF))
            self.scratch.update(other_t=pltpu.VMEM((2, 2, 2, text, WIDE), BF))
            self.scratch.update(two_t=pltpu.VMEM((2, 2, text, WIDE), BF))
            self.scratch.update(one_t=pltpu.VMEM((2, text, WIDE), BF))
        if half:
            self.results.update(half=shape((2, PIECE, half), F32))
            self.landings.update(arrived_half=shape((2, 2, BLOCK, half), BF))
            self.scratch.update(sums_h=pltpu.VMEM((2, 2, 2, BLOCK, half), BF))
            self.scratch.update(two_h=pltpu.VMEM((2, 2, BLOCK, half), BF))
            self.scratch.update(one_h=pltpu.VMEM((2, BLOCK, half), BF))
            self.scratch.update(pieces_h=pltpu.VMEM((2, sp, PIECE, half), BF))
            self.scratch.update(pieces_h_in=pltpu.VMEM((2, sp - 1, PIECE, half), BF))
        dma = pltpu.SemaphoreType.DMA
        each = dma((self.total,))
        self.scratch.update(
            core_send=each, core_recv=each, two_send=each, two_recv=each, one_send=each, one_recv=each
        )
        self.scratch.update(load=dma((3, 2)))
        self.scratch.update(zsend=dma((self.total, sp - 1)))
        self.scratch.update(zrecv=dma((self.total, sp - 1)))

    def arrays(self, grads, down=None, text=None, halves=None):
        out = [g.reshape(2, 2, 2, BLOCK, g.shape[1]) for g in grads]
        if self.down:
            out.append(down.reshape(2, 2, 2, self.sp, BLOCK, WIDE))
        if self.text:
            out.append(text.reshape(2, 2, 2, self.text, 2 * WIDE))
        if self.half:
            out.append(halves.reshape(2, 2, 2, BLOCK, self.half))
        return out

    def bind(self, place, arrays, refs):
        arrays = list(arrays)
        self.p, self.refs = place, refs
        halves = arrays.pop() if self.half else None
        text = arrays.pop() if self.text else None
        down = arrays.pop() if self.down else None
        chunks = []
        if self.text:
            for k in range(2):
                view = lambda core, k=k: text.at[:, :, core, :, pl.ds(k * WIDE, WIDE)]
                chunks.append(SimpleNamespace(kept=view, sent=view, kind=TEXT_ROWS, index=k, slot=k))
                chunks[-1].__dict__.update(sums=refs.sums_t, other=refs.other_t, arrived=refs.arrived_text.at[k])
                chunks[-1].__dict__.update(two=refs.two_t.at[k], one=refs.one_t.at[k])
        blocks = []
        if self.down:
            for j in range(self.sp):
                view = lambda core, j=j: down.at[:, :, core, j]
                blocks.append(SimpleNamespace(kept=view, sent=view, kind=DOWN, index=j))
        for k, (o, c) in enumerate(self.plan):
            view = lambda core, o=o, c=c: arrays[o].at[:, :, core, :, pl.ds(c, WIDE)]
            blocks.append(SimpleNamespace(kept=view, sent=view, kind=PIECES, index=k))
        for k, c in enumerate(blocks):
            c.__dict__.update(sums=refs.sums, other=refs.other, arrived=refs.arrived.at[k], slot=k % min(RING, self.blocks))
            c.__dict__.update(two=refs.two.at[k], one=refs.one.at[k])
        chunks, plain = blocks, chunks
        if self.half:
            view = lambda core: halves.at[:, :, core]
            for k in range(2):
                chunks.append(SimpleNamespace(kept=None if k else view, sent=view if k else None, kind=HALVES, index=k, slot=k))
                chunks[-1].__dict__.update(sums=refs.sums_h, arrived=refs.arrived_half)
                chunks[-1].__dict__.update(two=refs.two_h.at[k], one=refs.one_h.at[k])
        chunks = chunks + plain
        for k, c in enumerate(chunks):
            c.order = k % 2
        self.chunks = chunks
        self.red = Reduce(place, chunks, refs)

    def sends(self, i):
        c, refs, p, sp = self.chunks[i], self.refs, self.p, self.sp
        k = c.index
        sems = (lambda r: refs.zsend.at[i, r], lambda r: refs.zrecv.at[i, r])
        if c.kind == PIECES:
            return along_z(p, sp, lambda z: refs.pieces.at[k, z], lambda r: refs.pieces_in.at[k, r], *sems)
        if c.kind == HALVES:
            return along_z(p, sp, lambda z: refs.pieces_h.at[k, z], lambda r: refs.pieces_h_in.at[k, r], *sems)
        if c.kind == DOWN and k == sp - 1:
            return along_z(p, sp, lambda z: refs.blocks_d.at[z], lambda r: refs.blocks_d_in.at[r], *sems)
        return []

    def store(self, i):
        c, sp = self.chunks[i], self.sp
        k = c.index

        def cut(target):
            def inner(value):
                for z in range(sp):
                    low = PIECE * z - PIECE * z % 16
                    high = PIECE * (z + 1)
                    high += -high % 16
                    rows = value(pl.ds(low, high - low))
                    target[k, z] = rows[PIECE * z - low : PIECE * z - low + PIECE].astype(BF)

            return inner

        def tiles(target, rows, kind):
            def inner(value):
                def tile(t, _):
                    r = pl.ds(pl.multiple_of(t * 16, 16), 16)
                    target[k, r, :] = value(r).astype(kind)
                    return 0

                lax.fori_loop(0, rows // 16, tile, 0)

            return inner

        if c.kind == PIECES:
            return cut(self.refs.pieces)
        if c.kind == HALVES:
            return cut(self.refs.pieces_h)
        if c.kind == DOWN:
            return tiles(self.refs.blocks_d, BLOCK, BF)
        return tiles(self.refs.text, self.text, F32)

    def last(self, i):
        c, refs, p, sp = self.chunks[i], self.refs, self.p, self.sp
        k = c.index
        for copy in self.sends(i):
            copy.wait_recv()
        if c.kind in (PIECES, HALVES):
            result, mine, others_in = (
                (refs.piece, refs.pieces, refs.pieces_in)
                if c.kind == PIECES
                else (refs.half, refs.pieces_h, refs.pieces_h_in)
            )
            result[k] = mine[k, p.z].astype(F32) + sum(others_in[k, r].astype(F32) for r in range(sp - 1))
        elif c.kind == DOWN and k == sp - 1:

            def tile(t, _):
                r = pl.ds(pl.multiple_of(t * 16, 16), 16)
                refs.down[r, :] = refs.blocks_d[p.z, r, :].astype(F32) + sum(
                    refs.blocks_d_in[a, r, :].astype(F32) for a in range(sp - 1)
                )
                return 0

            lax.fori_loop(0, BLOCK // 16, tile, 0)

    ahead = 4

    def begin(self):
        for i in range(min(self.ahead, self.total)):
            self.red.start(i)
        self.red.prefetch(0)

    def step(self, t):
        red, total = self.red, self.total
        if t + self.ahead < total:
            red.start(t + self.ahead)
        if t + 1 < total:
            red.prefetch(t + 1)
        if t < total:
            red.add(t)
        if 0 <= t - DELAY < total:
            red.second(t - DELAY)
        i = t - 2 * DELAY
        if 0 <= i < total:
            red.third(i, self.store(i))
            for copy in self.sends(i):
                copy.start()
        if 0 <= i - 2 < total:
            self.last(i - 2)

    def steps(self):
        return [functools.partial(self.step, t) for t in range(self.total + 2 * DELAY + 2)]

    def end(self):
        for i in range(self.total):
            self.red.drain(i, self.total)
            for copy in self.sends(i):
                copy.wait_send()


MOD_ROWS = 16
START, WAIT_RECV, WAIT_SEND = range(3)
TILE = 8


class Pairs:
    def __init__(self, p):
        self.p = p

    def owner(self, t):
        p = self.p
        return (p.f - p.core + t % 2, 2 * p.core + t // 2)

    def is_owner(self, t):
        p = self.p
        return jnp.logical_and(p.core == t % 2, p.z == 2 * p.core + t // 2)

    def source(self, z):
        p = self.p
        return (p.f - p.core + p.z // 2, z)

    def is_source(self, z):
        p = self.p
        return jnp.logical_and(p.core == p.z // 2, p.z == z)

    def mine(self):
        return 2 * (self.p.z % 2) + self.p.core


def to_owners(p, blocks, landing, send, recv, do, only=range(4)):
    pairs = Pairs(p)
    for i in only:
        if do == WAIT_RECV:
            remote(blocks.at[0], landing.at[i], send.at[0], recv.at[i], pairs.owner(0)).wait_recv()
            continue
        far = remote(blocks.at[i], landing.at[p.z], send.at[i], recv.at[p.z], pairs.owner(i))
        near = pltpu.make_async_copy(blocks.at[i], landing.at[p.z], recv.at[p.z])

        @pl.when(jnp.logical_not(pairs.is_owner(i)))
        def _():
            far.start() if do == START else far.wait_send()

        if do == START:

            @pl.when(pairs.is_owner(i))
            def _():
                near.start()


def to_homes(p, blocks, landing, send, recv, do):
    pairs = Pairs(p)
    mine = pairs.mine()
    for i in range(4):
        if do == WAIT_RECV:
            remote(blocks.at[0], landing.at[i], send.at[0], recv.at[i], pairs.source(0)).wait_recv()
            continue
        far = remote(blocks.at[i], landing.at[mine], send.at[i], recv.at[mine], pairs.source(i))
        near = pltpu.make_async_copy(blocks.at[i], landing.at[mine], recv.at[mine])

        @pl.when(jnp.logical_not(pairs.is_source(i)))
        def _():
            far.start() if do == START else far.wait_send()

        if do == START:

            @pl.when(pairs.is_source(i))
            def _():
                near.start()


def others(p):
    out = []
    for m in range(1, 8):
        f = p.f
        for bit, step, here in ((1, 1, p.core), (2, 2, p.x), (4, 4, p.y)):
            if m & bit:
                f = f + step * (1 - 2 * here)
        out.append((f, p.z))
    return out


def group(p):
    sib = p.flip("core")[0]
    return [p.along(r) for r in range(1, p.sp)] + [(sib, (p.z + r) % p.sp) for r in range(1, p.sp)]


def greet_list(peers):
    barrier = pltpu.get_barrier_semaphore()
    for peer in peers:
        pl.semaphore_signal(barrier, inc=1, device_id=peer, device_id_type=MESH)
    pl.semaphore_wait(barrier, len(peers))


def front_kernel(
    sp,
    shards,
    ada,
    silu,
    vectors,
    text,
    resid,
    full,
    h_slot,
    modulation,
    vectors_all,
    text_mine,
    silu_in,
    landed,
    block,
    parts,
    parts_in,
    sums_in,
    vec_own,
    vec_in,
    text_in,
    h_blocks,
    send,
    recv,
    zsend,
    zrecv,
    csend,
    crecv,
    local_sem,
    s1,
    r1,
    s2,
    r2,
    s3,
    r3,
    sv1,
    rv1,
    sv2,
    rv2,
    st,
    rt,
    sh,
    rh,
    sx,
    rx,
):
    p = Place(sp)
    near = others(p)
    greet_list(near + group(p))
    here = lambda f: full.at[pl.ds(pl.multiple_of(f * BLOCK, 16), BLOCK), :]
    orders = [1 - p.core, p.core]

    def cond(m):
        f = near[m][0]
        return remote(silu.at[f * sp + p.z], silu_in.at[p.f], s1.at[m], r1.at[m], near[m])

    for m in range(7):
        cond(m).start()
    silu_in[p.f] = silu[p.f * sp + p.z]

    vec_own[...] = vectors[:TILE, :].astype(F32)
    vec_in[p.z] = vec_own[...]

    def vec_z(r):
        return remote(vec_own, vec_in.at[p.z], sv1.at[r - 1], rv1.at[r - 1], p.along(r))

    for r in range(1, sp):
        vec_z(r).start()

    def spread(k, r):
        return remote(
            shards.at[orders[k]], landed.at[orders[k], p.z], zsend.at[k, r - 1], zrecv.at[k, r - 1], p.along(r)
        )

    for k in range(2):
        for r in range(1, sp):
            spread(k, r).start()
        landed[orders[k], p.z] = shards[orders[k]]

    def text_z(r):
        z = (p.z + r) % sp
        return remote(text.at[z], text_in.at[p.z], st.at[r - 1], rt.at[r - 1], p.along(r))

    for r in range(1, sp):
        text_z(r).start()
    text_in[p.z] = text[p.z]

    for m in range(7):
        cond(m).wait_recv()
    rows = jnp.concatenate([silu_in[f][:2] for f in range(8)], axis=0).astype(BF)
    slots = 2
    for j in range(6):
        res = nn(rows, ada[:, j * WIDE : (j + 1) * WIDE])
        for f in range(8):
            parts[f, slots * j : slots * (j + 1), :] = res[slots * f : slots * (f + 1)]
    for f in range(8):
        parts[f, 6 * slots :, :] = jnp.zeros((MOD_ROWS - 6 * slots, WIDE), F32)

    def part(m):
        return remote(parts.at[near[m][0]], parts_in.at[m], s2.at[m], r2.at[m], near[m])

    for m in range(7):
        part(m).start()

    sibling = p.flip("core")[0]

    def cross():
        return remote(block.at[0], here(p.f), csend.at[0], crecv.at[0], p.flip("core"))

    def copies(k):
        f = sibling if k == 0 else p.f
        first, second = ("x", "y") if k == 0 else ("y", "x")
        step = p.flip(first)[0] - p.f
        return [
            remote(here(g), here(g), send.at[k, e], recv.at[k, e], p.flip(bit))
            for e, g, bit in ((0, f, first), (1, f, second), (2, f + step, second))
        ]

    for k in range(2):
        for r in range(1, sp):
            spread(k, r).wait_recv()
        for zz in range(sp):
            block[k, PIECE * zz : PIECE * (zz + 1), :] = landed[orders[k], zz]
        if k == 0:
            cross().start()
    own = pltpu.make_async_copy(block.at[1], here(p.f), local_sem.at[0])
    own.start()

    for m in range(7):
        part(m).wait_recv()
    parts[p.f] = parts[p.f] + sum(parts_in[m] for m in range(7))

    def total(r):
        return remote(parts.at[p.f], sums_in.at[r - 1], s3.at[r - 1], r3.at[r - 1], p.along(r))

    for r in range(1, sp):
        total(r).start()
    own.wait()
    for e in (0, 1):
        copies(1)[e].start()
    cross().wait_recv()
    for e in (0, 1):
        copies(0)[e].start()
    for r in range(1, sp):
        vec_z(r).wait_recv()

    def vec_f(m):
        return remote(vec_in, vectors_all.at[p.f], sv2.at[m], rv2.at[m], near[m])

    for m in range(7):
        vec_f(m).start()
    vectors_all[p.f] = vec_in[...]
    for r in range(1, sp):
        total(r).wait_recv()
    modulation[...] = parts[p.f] + sum(sums_in[r] for r in range(sp - 1))

    patches = resid.shape[1]
    step = 32
    for s in range(slots):
        for k in range(2):

            def tile(i, _):
                r = pl.multiple_of(i * step, step)
                v = resid[s, pl.ds(k * (patches // 2) + r, step), :]
                c = v - jnp.mean(v, axis=-1, keepdims=True)
                n = c * lax.rsqrt(jnp.mean(c * c, axis=-1, keepdims=True) + 1e-06)
                h = n * (1.0 + modulation[slots + s : slots + s + 1, :]) + modulation[s : s + 1, :]
                h_blocks[2 * s + k, pl.ds(r, step), :] = h.astype(BF)
                return 0

            lax.fori_loop(0, patches // 2 // step, tile, 0)
            to_owners(p, h_blocks, h_slot.at[0], sh, rh, START, [2 * s + k])
    for k in (1, 0):
        copies(k)[0].wait_recv()
        copies(k)[2].start()
    for r in range(1, sp):
        text_z(r).wait_recv()
    text_rows = text_in.shape[1]
    for zz in range(sp):
        text_mine[text_rows * zz : text_rows * (zz + 1), :] = text_in[zz]

    def swap(z):
        return remote(h_slot.at[0, z], h_slot.at[1, z], sx.at[z], rx.at[z], p.flip("core"))

    for z in range(sp):
        to_owners(p, h_blocks, h_slot.at[0], sh, rh, WAIT_RECV, [z])
        swap(z).start()
    for k in range(2):
        copies(k)[1].wait_recv()
        copies(k)[2].wait_recv()
        for e in range(3):
            copies(k)[e].wait_send()
        for r in range(1, sp):
            spread(k, r).wait_send()
    cross().wait_send()
    for m in range(7):
        vec_f(m).wait_recv()
        vec_f(m).wait_send()
        part(m).wait_send()
        cond(m).wait_send()
    for r in range(1, sp):
        vec_z(r).wait_send()
        total(r).wait_send()
        text_z(r).wait_send()
    to_owners(p, h_blocks, h_slot.at[0], sh, rh, WAIT_SEND)
    for z in range(sp):
        swap(z).wait()


def front(sp, shards, ada, silu, vectors, text, resid):
    half = shards.shape[2]
    patches = resid.shape[1]
    text_rows, depth = text.shape[1:]
    dma = pltpu.SemaphoreType.DMA
    vmem = pl.BlockSpec(memory_space=pltpu.VMEM)
    any_space = pl.BlockSpec(memory_space=pl.ANY)
    shape = jax.ShapeDtypeStruct
    lanes = silu.shape[2]
    return pl.pallas_call(
        functools.partial(front_kernel, sp),
        out_shape=[
            shape((8 * BLOCK, half), BF),
            shape((2, 4, patches // 2, WIDE), BF),
            shape((MOD_ROWS, WIDE), F32),
            shape((8, sp, TILE, lanes), F32),
            shape((sp * text_rows, depth), BF),
            shape((8, TILE, lanes), F32),
        ],
        in_specs=[vmem] * 6,
        out_specs=[any_space] + [vmem] * 5,
        scratch_shapes=[
            pltpu.VMEM((2, sp, PIECE, half), BF),
            pltpu.VMEM((2, BLOCK, half), BF),
            pltpu.VMEM((8, MOD_ROWS, WIDE), F32),
            pltpu.VMEM((7, MOD_ROWS, WIDE), F32),
            pltpu.VMEM((sp - 1, MOD_ROWS, WIDE), F32),
            pltpu.VMEM((TILE, lanes), F32),
            pltpu.VMEM((sp, TILE, lanes), F32),
            pltpu.VMEM((sp, text_rows, depth), BF),
            pltpu.VMEM((4, patches // 2, WIDE), BF),
            dma((2, 3)),
            dma((2, 3)),
            dma((2, sp - 1)),
            dma((2, sp - 1)),
            dma((1,)),
            dma((1,)),
            dma((1,)),
        ]
        + [dma((7,))] * 4
        + [dma((sp - 1,))] * 4
        + [dma((7,))] * 2
        + [dma((sp - 1,))] * 2
        + [dma((4,))] * 4,
        compiler_params=pltpu.CompilerParams(
            collective_id=4, has_side_effects=True, vmem_limit_bytes=48 * 2**20
        ),
        name="front",
    )(shards, ada, silu, vectors, text, resid)


LAG = 3
FIRST = 8
PER = 2


def interleave(first, per, work, steps):
    steps = list(steps)
    for _ in range(first):
        steps.pop(0)()
    for k, piece in enumerate(work):
        piece()
        if steps and k % per == per - 1:
            steps.pop(0)()
    for step in steps:
        step()


class SumAlong:
    def __init__(self, p, part, landing, out, send, recv, send_again, recv_again):
        self.p, self.part, self.landing, self.out = p, part, landing, out
        self.sems = (send, recv, send_again, recv_again)

    def parts(self):
        send, recv = self.sems[:2]
        return along_z(
            self.p,
            self.p.sp,
            lambda z: self.part.at[z],
            lambda r: self.landing.at[r],
            lambda r: send.at[r],
            lambda r: recv.at[r],
        )

    def shares(self):
        own = self.out.at[self.p.z]
        send, recv = self.sems[2:]
        return [
            remote(own, own, send.at[r - 1], recv.at[r - 1], self.p.along(r)) for r in range(1, self.p.sp)
        ]

    def start(self):
        for copy in self.parts():
            copy.start()

    def sum(self):
        for copy in self.parts():
            copy.wait_recv()
        z = self.p.z
        for c in range(self.out.shape[2] // WIDE):
            cols = slice(c * WIDE, (c + 1) * WIDE)
            self.out[z, :, cols] = (
                self.part[z, :, cols].astype(F32)
                + sum(self.landing[r, :, cols].astype(F32) for r in range(self.p.sp - 1))
            ).astype(BF)
        for copy in self.shares():
            copy.start()

    def end(self):
        for copy in self.parts():
            copy.wait_send()
        for copy in self.shares():
            copy.wait()


def attend_kernel(plan, sp, heads, scale, n_out, *refs):
    shards, down_shard, text_shard, h_slot, qkv_w, text_mine, resid, mod, gain = refs[:9]
    refs = refs[9:]
    outs = refs[:n_out]
    down, text, qkv, attn, kv_all, branch, cross_in, query, cross, x_two = refs[n_out : n_out + 10]
    refs = refs[n_out + 10 :]
    landed, block, stack, heads_out, o_send, o_recv, o_full, text_w, kv_part, kv_in, kv, weights, x_one = refs[:13]
    send, recv, zsend, zrecv, dsend, drecv, local_sem, osem, hsend, hrecv, wsem = refs[13:24]
    p = Place(sp)
    along = SumAlong(p, kv_part, kv_in, kv, *refs[24:])
    greet_list([p.flip(b) for b in ("core", "x", "y")] + group(p))
    n = len(plan)
    rows = down_shard.shape[0]
    trows = text_shard.shape[0]
    down_own = down.at[pl.ds(pl.multiple_of(p.f * (sp * rows) + p.z * rows, 16), rows), :]
    text_own = text.at[pl.ds(pl.multiple_of(p.f * trows, 16), trows), :]
    text_copy = pltpu.make_async_copy(text_shard, text_own, local_sem.at[2])
    text_copy.start()

    chunks = [(text, lambda f: f * trows, trows, pl.ds(k * WIDE, WIDE), k % 2) for k in range(2)]
    chunks += [(outs[o], lambda f: f * BLOCK, BLOCK, pl.ds(c, WIDE), k % 2) for k, (o, c) in enumerate(plan)]
    chunks += [
        (down, lambda f, j=j: f * (sp * rows) + j * rows, rows, pl.ds(0, WIDE), (n + j) % 2) for j in range(sp)
    ]
    total = len(chunks)
    g = Gather(p, chunks, send, recv)

    def pieces(i):
        return [
            remote(shards.at[i], landed.at[i, p.z], zsend.at[i, r - 1], zrecv.at[i, r - 1], p.along(r))
            for r in range(1, sp)
        ]

    def down_z(r):
        return remote(down_shard, down_own, dsend.at[r - 1], drecv.at[p.z], p.along(r))

    def launch(i):
        if i < n:
            for copy in pieces(i):
                copy.start()
            landed[i, p.z] = shards[i]
        elif i == n:
            for r in range(1, sp):
                down_z(r).start()

    def ready(t):
        if t == 0:
            text_copy.wait()
        i = t - 2
        if 0 <= i < n:
            for copy in pieces(i):
                copy.wait_recv()
            slot = i % 2
            for zz in range(sp):
                block[slot, PIECE * zz : PIECE * (zz + 1), :] = landed[i, zz]
            copy = pltpu.make_async_copy(block.at[slot], g.region(t, p.f), local_sem.at[slot])
            copy.start()
            copy.wait()
        elif i >= n:
            remote(down_shard, down_own, dsend.at[0], drecv.at[i - n], p.along(1)).wait_recv()

    ahead = 6
    pltpu.make_async_copy(down_shard, down_own, drecv.at[p.z]).start()
    for i in range(ahead):
        launch(i)

    def step(t):
        if t < total:
            if t >= 2:
                launch(t - 2 + ahead)
            ready(t)
            g.begin(t)
        if 0 <= t - LAG < total:
            g.middle(t - LAG)
        if 0 <= t - 2 * LAG < total:
            g.late(t - 2 * LAG)

    T = qkv.shape[0]
    half = heads * HD
    tile = 256

    def project(i):
        hb = h_slot.shape[2]
        for b in range(tile // hb):
            k = i * (tile // hb) + b
            qkv[hb * k : hb * (k + 1), :] = nn(h_slot[k // 4, k % 4], qkv_w[...]).astype(BF)

    def stage():
        for i in range(3 * heads):
            stack[i] = jnp.zeros(stack.shape[1:], BF)
            stack[i, :, :HD] = qkv[:, i * HD : (i + 1) * HD]

    def head(h):
        def tile_of(i, _):
            q = stack[h, pl.ds(pl.multiple_of(i * tile, tile), tile), :]
            s = nt(q, stack[heads + h])
            m = jnp.max(s, axis=-1, keepdims=True)
            e = jnp.exp((s - m) * scale)
            l = jnp.sum(e, axis=-1, keepdims=True)
            r = nn(e.astype(BF), stack[2 * heads + h])
            heads_out[h, pl.ds(pl.multiple_of(i * tile, tile), tile), :] = (r / l).astype(BF)
            return 0

        lax.fori_loop(0, T // tile, tile_of, 0)

    def o_cross():
        return remote(o_send, o_recv, osem.at[0], osem.at[1], p.flip("core"))

    def o_out():
        for h in range(heads):
            o_send[:, h * HD : (h + 1) * HD] = heads_out[h, T // 2 :, :HD]
        o_cross().start()

    def o_home():
        o_cross().wait_recv()
        hb = T // 8
        low = p.core == 0
        for b in range(4):
            r = slice(hb * b, hb * (b + 1))
            mine = jnp.concatenate([heads_out[h, r, :HD] for h in range(heads)], axis=1)
            other = o_recv[r, :]
            o_full[b, :, :half] = jnp.where(low, mine, other)
            o_full[b, :, half:] = jnp.where(low, other, mine)
        to_homes(p, o_full, attn, hsend, hrecv, START)

    text_load = pltpu.make_async_copy(text, text_w, local_sem.at[3])

    def text_start():
        g.finish(0)
        g.finish(1)
        text_load.start()

    krows = kv_part.shape[1]

    def kv_product():
        text_load.wait()
        for c in range(2):
            cols = slice(c * WIDE, (c + 1) * WIDE)
            res = nn(text_mine[...], text_w[:, cols])
            for z in range(sp):
                kv_part[z, :, cols] = res[krows * z : krows * (z + 1)].astype(BF)
        along.start()

    slots, patches = resid.shape[:2]
    hb = T // 8
    loads = [pltpu.make_async_copy(outs[o], weights.at[o % 2], wsem.at[o]) for o in range(3)]

    def weights_start():
        for o in range(2):
            g.finish(2 + o)
            loads[o].start()

    def after(b):
        if b == 0:
            to_homes(p, o_full, attn, hsend, hrecv, WAIT_RECV)
            loads[0].wait()
            loads[1].wait()
        s, r = b // 2, slice(hb * (b % 2), hb * (b % 2 + 1))
        out = nn(attn[b], weights[0])
        branch[s, r, :] = out
        v = resid[s, r, :] + mod[2 * slots + s : 2 * slots + s + 1, :] * out
        x_one[s, r, :] = v
        c = v - jnp.mean(v, axis=-1, keepdims=True)
        n = c * lax.rsqrt(jnp.mean(c * c, axis=-1, keepdims=True) + 1e-06)
        low = (n * gain[:1, :]).astype(BF)
        cross_in[s, r, :] = low
        query[s, r, :] = nn(low, weights[1]).astype(BF)

    def text_end():
        g.finish(4)
        loads[2].start()
        along.end()
        count = kv_all.shape[1] // sp
        for s in range(slots):
            for z in range(sp):
                kv_all[s, count * z : count * (z + 1), :] = kv[z, count * s : count * (s + 1), :]

    def cross_attention(s):
        for h in range(2 * heads):
            c = slice(h * HD, (h + 1) * HD)
            cv = slice(WIDE + h * HD, WIDE + (h + 1) * HD)
            scores = nt(query[s, :, c], kv_all[s, :, c])
            m = jnp.max(scores, axis=-1, keepdims=True)
            e = jnp.exp((scores - m) * scale)
            l = jnp.sum(e, axis=-1, keepdims=True)
            cross[s, :, c] = (nn(e.astype(BF), kv_all[s, :, cv]) / l).astype(BF)

    def cross_project(s):
        if s == 0:
            loads[2].wait()
        for k in range(patches // hb):
            r = slice(hb * k, hb * (k + 1))
            x_two[s, r, :] = x_one[s, r, :] + nn(cross[s, r, :], weights[0])

    work = [functools.partial(project, i) for i in range(T // tile)]
    work += [text_start, stage]
    work += [functools.partial(head, h) for h in range(heads)]
    work.insert(-5, kv_product)
    work.insert(-2, along.sum)
    idle = lambda: None
    work += [o_out, o_home, weights_start, idle, idle, idle]
    work += [functools.partial(after, b) for b in range(4)]
    work += [text_end, functools.partial(cross_attention, 0), functools.partial(cross_attention, 1)]
    work += [functools.partial(cross_project, s) for s in range(slots)]
    interleave(FIRST, PER, work, [functools.partial(step, t) for t in range(total + 2 * LAG)])
    for i in range(5, total):
        g.finish(i)
    for i in range(n):
        for copy in pieces(i):
            copy.wait_send()
    for r in range(1, sp):
        down_z(r).wait_send()
    to_homes(p, o_full, attn, hsend, hrecv, WAIT_SEND)
    o_cross().wait_send()


def attend(plan, widths, sp, heads, scale, shards, down_shard, text_shard, h_slot, qkv_w, text_mine, resid, mod, gain):
    n = len(plan)
    total = n + sp + 2
    T = 8 * h_slot.shape[2]
    half = heads * HD
    trows = text_shard.shape[0]
    krows = text_mine.shape[0] // sp
    slots = resid.shape[0]
    any_space = pl.BlockSpec(memory_space=pl.ANY)
    vmem = pl.BlockSpec(memory_space=pltpu.VMEM)
    dma = pltpu.SemaphoreType.DMA
    shape = jax.ShapeDtypeStruct
    return pl.pallas_call(
        functools.partial(attend_kernel, plan, sp, heads, scale, len(widths)),
        out_shape=[shape((8 * BLOCK, w), BF) for w in widths]
        + [
            shape((8 * sp * down_shard.shape[0], WIDE), BF),
            shape((8 * trows, 2 * WIDE), BF),
            shape((T, 3 * half), BF),
            shape((4, T // 8, WIDE), BF),
            shape((slots, sp * krows // slots, 2 * WIDE), BF),
            shape(resid.shape, F32),
            shape(resid.shape, BF),
            shape(resid.shape, BF),
            shape(resid.shape, BF),
            shape(resid.shape, F32),
        ],
        in_specs=[vmem, any_space, any_space, vmem, vmem, vmem, vmem, vmem, vmem],
        out_specs=[any_space] * (len(widths) + 2) + [vmem] * 8,
        scratch_shapes=[
            pltpu.VMEM((n, sp, PIECE, WIDE), BF),
            pltpu.VMEM((2, BLOCK, WIDE), BF),
            pltpu.VMEM((3 * heads, T, 128), BF),
            pltpu.VMEM((heads, T, 128), BF),
            pltpu.VMEM((T // 2, half), BF),
            pltpu.VMEM((T // 2, half), BF),
            pltpu.VMEM((4, T // 8, WIDE), BF),
            pltpu.VMEM((8 * trows, 2 * WIDE), BF),
            pltpu.VMEM((sp, krows, 2 * WIDE), BF),
            pltpu.VMEM((sp - 1, krows, 2 * WIDE), BF),
            pltpu.VMEM((sp, krows, 2 * WIDE), BF),
            pltpu.VMEM((2, WIDE, WIDE), BF),
            pltpu.VMEM(resid.shape, F32),
            dma((total, 7)),
            dma((total, 7)),
            dma((n, sp - 1)),
            dma((n, sp - 1)),
            dma((sp - 1,)),
            dma((sp,)),
            dma((4,)),
            dma((2,)),
            dma((4,)),
            dma((4,)),
            dma((3,)),
            dma((sp - 1,)),
            dma((sp - 1,)),
            dma((sp - 1,)),
            dma((sp - 1,)),
        ],
        compiler_params=pltpu.CompilerParams(
            collective_id=5, has_side_effects=True, vmem_limit_bytes=60 * 2**20
        ),
        cost_estimate=pl.CostEstimate(flops=2**34, bytes_accessed=2**28, transcendentals=2**23),
        name="attend",
    )(shards, down_shard, text_shard, h_slot, qkv_w, text_mine, resid, mod, gain)


def split(refs, *counts):
    out = []
    for c in counts:
        out.append(refs[:c])
        refs = refs[c:]
    return out + [refs]


def attend_back_kernel(make, sp, heads, scale, *refs):
    sums = make()
    n_in = sums.n_in
    arrays, (go_blocks, qkv, kv_part, h_slot), results, (g, kv, gw), landings, scratch, rest = split(
        refs, n_in, 4, len(sums.results), 3, len(sums.landings), len(sums.scratch)
    )
    names = SimpleNamespace()
    for group_names, group_refs in ((sums.results, results), (sums.landings, landings), (sums.scratch, scratch)):
        names.__dict__.update(zip(group_names, group_refs))
    go_in, go_away, go_half, part, acc, gsend, grecv, esem, ksend, krecv = rest
    p = Place(sp)
    greet_list([p.flip(b) for b in ("core", "x", "y")] + group(p))
    sums.bind(p, arrays, names)
    to_owners(p, go_blocks, go_in, gsend, grecv, START)
    sums.begin()
    kv[p.z] = kv_part[...]

    def shares():
        own = kv.at[p.z]
        return [remote(own, own, ksend.at[r - 1], krecv.at[r - 1], p.along(r)) for r in range(1, sp)]

    T = qkv.shape[0]
    half = heads * HD
    rows = T // 8

    def cross():
        return remote(go_away, go_half.at[1], esem.at[0], esem.at[1], p.flip("core"))

    def cut():
        to_owners(p, go_blocks, go_in, gsend, grecv, WAIT_RECV)
        low = p.core == 0
        for b in range(4):
            first, other = go_in[b, :, :half], go_in[b, :, half:]
            go_half[0, b] = jnp.where(low, first, other)
            go_away[b] = jnp.where(low, other, first)
        cross().start()

    tile = 256

    def head(h):
        if h == 0:
            cross().wait_recv()
        for k in range(3):
            c = (k * heads + h) * HD
            part[k, :, :HD] = qkv[:, c : c + HD]
        for b in range(8):
            part[3, rows * b : rows * (b + 1), :HD] = go_half[b // 4, b % 4, :, h * HD : (h + 1) * HD]
        acc[...] = jnp.zeros(acc.shape, F32)

        def cols(i, _):
            sl = pl.ds(pl.multiple_of(i * tile, tile), tile)
            q, go = part[0, sl, :], part[3, sl, :]
            k, v = part[1], part[2]
            s = nt(k, q)
            m = jnp.max(s, axis=0, keepdims=True)
            e = jnp.exp((s - m) * scale)
            pr = e * (1.0 / jnp.sum(e, axis=0, keepdims=True))
            t = nt(v, go) * pr
            ds = (t - pr * jnp.sum(t, axis=0, keepdims=True)).astype(BF)
            acc[0] += nn(ds, q)
            acc[1] += nn(pr.astype(BF), go)
            part[0, sl, :] = (tn(ds, k) * scale).astype(BF)
            return 0

        lax.fori_loop(0, T // tile, cols, 0)
        c = h * HD
        g[:, c : c + HD] = part[0, :, :HD]
        c += half
        g[:, c : c + HD] = (acc[0, :, :HD] * scale).astype(BF)
        c += half
        g[:, c : c + HD] = acc[1, :, :HD].astype(BF)

    def weights(c):
        cols = slice(c, min(c + 512, g.shape[1]))
        gw[:, cols] = tn(h_slot[...], g[:, cols]).astype(BF)

    part[...] = jnp.zeros(part.shape, BF)
    work = [cut] + [functools.partial(head, h) for h in range(heads)]
    work += [functools.partial(weights, c) for c in range(0, g.shape[1], 512)]
    work.insert(2, lambda: [copy.start() for copy in shares()])
    interleave(2, 1, work, sums.steps())
    sums.end()
    for copy in shares():
        copy.wait()
    to_owners(p, go_blocks, go_in, gsend, grecv, WAIT_SEND)
    cross().wait_send()


def attend_back(plan, sp, heads, scale, grads, go_blocks, qkv, kv_part, h_slot):
    def make():
        sums = Sums(sp, plan, False, 0, 0)
        sums.n_in = len(grads)
        return sums

    sums = make()
    T = qkv.shape[0]
    half = heads * HD
    any_space = pl.BlockSpec(memory_space=pl.ANY)
    vmem = pl.BlockSpec(memory_space=pltpu.VMEM)
    dma = pltpu.SemaphoreType.DMA
    out = pl.pallas_call(
        functools.partial(attend_back_kernel, make, sp, heads, scale),
        out_shape=list(sums.results.values()) + [jax.ShapeDtypeStruct(a, BF) for a in (qkv.shape, (sp,) + kv_part.shape, (WIDE, qkv.shape[1]))] + list(sums.landings.values()),
        in_specs=[any_space] * len(grads) + [vmem] * 4,
        out_specs=[vmem] * (len(sums.results) + 3) + [any_space] * len(sums.landings),
        scratch_shapes=list(sums.scratch.values())
        + [
            pltpu.VMEM((4, T // 8, WIDE), BF),
            pltpu.VMEM((4, T // 8, half), BF),
            pltpu.VMEM((2, 4, T // 8, half), BF),
            pltpu.VMEM((4, T, 128), BF),
            pltpu.VMEM((2, T, 128), F32),
            dma((4,)),
            dma((4,)),
            dma((2,)),
            dma((sp - 1,)),
            dma((sp - 1,)),
        ],
        compiler_params=pltpu.CompilerParams(
            collective_id=6, has_side_effects=True, vmem_limit_bytes=62 * 2**20
        ),
        cost_estimate=pl.CostEstimate(flops=2**35, bytes_accessed=2**28, transcendentals=2**23),
        name="attend_back",
    )(*sums.arrays(grads), go_blocks, qkv, kv_part, h_slot)
    return out[:4]


def finish_kernel(make, sp, *refs):
    sums = make()
    arrays, (g, qkv_w, resid, grad_one, mod, small), results, (out, small_all), landings, scratch, rest = split(
        refs, sums.n_in, 6, len(sums.results), 2, len(sums.landings), len(sums.scratch)
    )
    names = SimpleNamespace()
    for group_names, group_refs in ((sums.results, results), (sums.landings, landings), (sums.scratch, scratch)):
        names.__dict__.update(zip(group_names, group_refs))
    home, gh, gh_in, blocks, mine, mine_in, partial, hsend, hrecv, esem, s1, r1, s2, r2 = rest
    p = Place(sp)
    near = others(p)
    greet_list(near + group(p))
    sums.bind(p, arrays, names)

    def cross():
        return remote(gh.at[1], gh_in, esem.at[0], esem.at[1], p.flip("core"))

    sums.begin()
    half_rows = gh.shape[2]

    def back(k):
        for b in range(4):
            first = (4 * k + b) * half_rows
            gh[k, b] = nt(g[first : first + half_rows, :], qkv_w[...])
        if k == 1:
            cross().start()

    slots = resid.shape[0]

    def add():
        cross().wait_recv()
        step = 16
        for b in range(4):

            def tile(i, _):
                r = pl.ds(pl.multiple_of(i * step, step), step)
                blocks[b, r, :] = (gh[0, b, r, :] + gh_in[b, r, :]).astype(BF)
                return 0

            lax.fori_loop(0, half_rows // step, tile, 0)
        to_homes(p, blocks, home, hsend, hrecv, START)

    def tail():
        to_homes(p, blocks, home, hsend, hrecv, WAIT_RECV)
        step = 32
        partial[...] = jnp.zeros(partial.shape, F32)
        for b in range(4):
            s, k = b // 2, b % 2

            def tile(i, _):
                start = pl.multiple_of(i * step, step)
                r = pl.ds(k * half_rows + start, step)
                v = resid[s, r, :]
                c = v - jnp.mean(v, axis=-1, keepdims=True)
                inv = lax.rsqrt(jnp.mean(c * c, axis=-1, keepdims=True) + 1e-06)
                n = c * inv
                g = home[b, pl.ds(start, step), :].astype(F32)
                gn = g * n
                partial[s, 0] += sum(g[8 * j : 8 * j + 8] for j in range(step // 8))
                partial[s, 1] += sum(gn[8 * j : 8 * j + 8] for j in range(step // 8))
                d = g * (1.0 + mod[slots + s : slots + s + 1, :])
                back = d - jnp.mean(d, axis=-1, keepdims=True) - n * jnp.mean(d * n, axis=-1, keepdims=True)
                out[s, r, :] = grad_one[s, r, :] + back * inv
                return 0

            lax.fori_loop(0, half_rows // step, tile, 0)
        mine[...] = small[...]
        for s in range(slots):
            for j in range(2):
                mine[slots * j + s : slots * j + s + 1, :] = jnp.sum(partial[s, j], axis=0, keepdims=True)
        for copy in along():
            copy.start()

    def along():
        return [remote(mine, mine_in.at[r - 1], s1.at[r - 1], r1.at[r - 1], p.along(r)) for r in range(1, sp)]

    def share(m):
        own = small_all.at[p.f]
        return remote(own, own, s2.at[m], r2.at[m], near[m])

    def total():
        for copy in along():
            copy.wait_recv()
        small_all[p.f] = mine[...] + sum(mine_in[r] for r in range(sp - 1))
        for m in range(7):
            share(m).start()

    idle = lambda: None
    work = [functools.partial(back, 1), functools.partial(back, 0), add, idle, idle, idle, tail, idle, total]
    interleave(1, 1, work, sums.steps())
    sums.end()
    for m in range(7):
        share(m).wait()
    for copy in along():
        copy.wait_send()
    to_homes(p, blocks, home, hsend, hrecv, WAIT_SEND)
    cross().wait_send()


def finish(sp, down, text, halves, g, qkv_w, resid, grad_one, mod, small):
    half = halves.shape[1]

    def make():
        sums = Sums(sp, [], True, text.shape[0] // 8, half)
        sums.n_in = 3
        return sums

    sums = make()
    rows = g.shape[0] // 8
    any_space = pl.BlockSpec(memory_space=pl.ANY)
    vmem = pl.BlockSpec(memory_space=pltpu.VMEM)
    dma = pltpu.SemaphoreType.DMA
    shape = jax.ShapeDtypeStruct
    out = pl.pallas_call(
        functools.partial(finish_kernel, make, sp),
        out_shape=list(sums.results.values())
        + [shape(resid.shape, F32), shape((8,) + small.shape, F32)]
        + list(sums.landings.values()),
        in_specs=[any_space] * 3 + [vmem] * 6,
        out_specs=[vmem] * (len(sums.results) + 2) + [any_space] * len(sums.landings),
        scratch_shapes=list(sums.scratch.values())
        + [
            pltpu.VMEM((4, rows, WIDE), BF),
            pltpu.VMEM((2, 4, rows, WIDE), F32),
            pltpu.VMEM((4, rows, WIDE), F32),
            pltpu.VMEM((4, rows, WIDE), BF),
            pltpu.VMEM(small.shape, F32),
            pltpu.VMEM((sp - 1,) + small.shape, F32),
            pltpu.VMEM((2, 2, 8, WIDE), F32),
            dma((4,)),
            dma((4,)),
            dma((2,)),
            dma((sp - 1,)),
            dma((sp - 1,)),
            dma((7,)),
            dma((7,)),
        ],
        compiler_params=pltpu.CompilerParams(
            collective_id=7, has_side_effects=True, vmem_limit_bytes=62 * 2**20
        ),
        name="finish",
    )(*sums.arrays([], down, text, halves), g, qkv_w, resid, grad_one, mod, small)
    return out[:5]


def temporal_kernel(heads, scale, trip, go, out, g):
    slots, rows, width = go.shape
    lanes = lax.broadcasted_iota(jnp.int32, (width, 128), 0) // HD
    member = (lanes == lax.broadcasted_iota(jnp.int32, (width, 128), 1)).astype(F32).astype(BF)
    across = lax.broadcasted_iota(jnp.int32, (128, width), 1) // HD
    member_t = (across == lax.broadcasted_iota(jnp.int32, (128, width), 0)).astype(F32).astype(BF)
    pairs = [(a, b) for a in range(slots) for b in range(slots)]

    def part(a, k):
        return trip[a, :, k * width : (k + 1) * width].astype(F32)

    def per_head(x):
        high = x.astype(BF)
        return nn(high, member) + nn((x - high.astype(F32)).astype(BF), member)

    def wide(x):
        return nn(x.astype(BF), member_t)

    s = {(a, b): per_head(part(a, 0) * part(b, 1)) * scale for a, b in pairs}
    p = {}
    for a in range(slots):
        m = functools.reduce(jnp.maximum, [s[a, b] for b in range(slots)])
        e = [jnp.exp(s[a, b] - m) for b in range(slots)]
        total = sum(e)
        for b in range(slots):
            p[a, b] = e[b] / total
    pw = {k: wide(v) for k, v in p.items()}
    d = [go[a].astype(F32) for a in range(slots)]
    for a in range(slots):
        out[a] = sum(pw[a, b] * part(b, 2) for b in range(slots)).astype(BF)
    for b in range(slots):
        g[b, :, 2 * width :] = sum(pw[a, b] * d[a] for a in range(slots)).astype(BF)
    dp = {(a, b): per_head(d[a] * part(b, 2)) for a, b in pairs}
    ds = {}
    for a in range(slots):
        mean = sum(dp[a, b] * p[a, b] for b in range(slots))
        for b in range(slots):
            ds[a, b] = wide(p[a, b] * (dp[a, b] - mean))
    for a in range(slots):
        g[a, :, :width] = (scale * sum(ds[a, b] * part(b, 1) for b in range(slots))).astype(BF)
        g[a, :, width : 2 * width] = (scale * sum(ds[b, a] * part(b, 0) for b in range(slots))).astype(BF)


def temporal(trip, go, heads, scale):
    slots, patches, width = go.shape
    rows = 64
    block = lambda w: pl.BlockSpec((slots, rows, w), lambda i: (0, i, 0))
    return pl.pallas_call(
        functools.partial(temporal_kernel, heads, scale),
        grid=(patches // rows,),
        out_shape=[jax.ShapeDtypeStruct((slots, patches, w), BF) for w in (width, 3 * width)],
        in_specs=[block(3 * width), block(width)],
        out_specs=[block(width), block(3 * width)],
        compiler_params=pltpu.CompilerParams(vmem_limit_bytes=48 * 2**20),
        cost_estimate=pl.CostEstimate(flops=2**32, bytes_accessed=2**24, transcendentals=2**16),
        name="temporal",
    )(trip, go)


HEADS = 16
EPS = 1e-06
HIGHEST = lax.Precision.HIGHEST
BOTH = ("fsdp", "sp")
PLAN = (
    [(0, 0), (1, 0), (2, 0)] + [(3, k * WIDE) for k in range(4)] + [(4, k * WIDE) for k in range(3)] + [(5, 0)]
)


def normalize(values):
    centred = values - jnp.mean(values, axis=-1, keepdims=True)
    return centred * lax.rsqrt(jnp.mean(centred * centred, axis=-1, keepdims=True) + EPS)


def normalize_back(values, grad_out):
    return jax.vjp(normalize, values)[1](grad_out)[0]


def gelu_tanh(values):
    return jax.nn.gelu(values, approximate=True)


def scatter(grad):
    part = lax.psum_scatter(grad.astype(BF), "fsdp", scatter_dimension=0, tiled=True)
    return lax.psum_scatter(part, "sp", scatter_dimension=0, tiled=True).astype(F32)


def sum_along(parts, sp):
    z = lax.axis_index("sp")
    total = lax.dynamic_index_in_dim(parts, z, 0, keepdims=False).astype(F32)
    for r in range(1, sp):
        part = lax.dynamic_index_in_dim(parts, (z + r) % sp, 0, keepdims=False)
        total += lax.ppermute(part, "sp", [(k, (k + r) % sp) for k in range(sp)]).astype(F32)
    return total.astype(BF)


class Moves:
    def __init__(self, fsdp, sp, slots):
        self.fsdp, self.sp, self.slots = fsdp, sp, slots
        self.core = lax.axis_index("fsdp") % 2
        self.z = lax.axis_index("sp")
        self.rounds = []
        for r in range(sp):
            pairs = []
            for f in range(fsdp):
                for z in range(sp):
                    t = (z - r) % sp
                    pairs.append((f * sp + z, (f - f % 2 + t % 2) * sp + slots * (f % 2) + t // 2))
            self.rounds.append(pairs)
        self.swap = [(f, f ^ 1) for f in range(fsdp)]

    def out(self, tokens):
        rows = tokens.shape[0] // self.sp
        blocks = tokens.reshape(self.sp, rows, tokens.shape[1])
        got = []
        for r, pairs in enumerate(self.rounds):
            t = (self.z - r) % self.sp
            block = lax.dynamic_index_in_dim(blocks, t, 0, keepdims=False)
            got.append(lax.ppermute(block, BOTH, pairs))
        return jnp.roll(jnp.stack(got), self.mine(), axis=0).reshape(tokens.shape)

    def home(self, tokens):
        rows = tokens.shape[0] // self.sp
        tokens = jnp.roll(tokens.reshape(self.sp, rows, -1), -self.mine(), axis=0).reshape(tokens.shape)
        out = jnp.zeros((self.sp, rows, tokens.shape[1]), tokens.dtype)
        for r, pairs in enumerate(self.rounds):
            back = lax.ppermute(tokens[r * rows : (r + 1) * rows], BOTH, [(b, a) for a, b in pairs])
            t = (self.z - r) % self.sp
            out = lax.dynamic_update_index_in_dim(out, back, t, 0)
        return out.reshape(tokens.shape)

    def mine(self):
        return 2 * (self.z % 2) + self.core

    def exchange(self, array):
        return lax.ppermute(array, "fsdp", self.swap)


def local(
    residual_in,
    condition,
    text_states,
    slot_item,
    cotangent,
    w_ada,
    w_qkv,
    w_out,
    w_cross_q,
    w_cross_kv,
    w_cross_out,
    w_up,
    w_down,
    w_temp_qkv,
    w_temp_out,
    g_cross,
    g_temp,
    t_gate,
):
    slots, patches, width = residual_in.shape[1:]
    text_local, text_width = text_states.shape[2:]
    sp = lax.axis_size("sp")
    fsdp = lax.axis_size("fsdp")
    f_index, z_index = lax.axis_index("fsdp"), lax.axis_index("sp")
    rows = w_qkv.shape[0]
    tok = slots * patches
    scale = HD ** (-0.5)
    moves = Moves(fsdp, sp, slots)
    core = f_index % 2

    def gather(shard):
        return lax.all_gather(shard.astype(BF), BOTH, axis=0, tiled=True)

    chosen = slot_item[0]
    video = (chosen[-1] == 0).astype(F32)

    cond = condition[0]
    cond_used = jnp.where((chosen == 0)[:, None], cond[0][None], cond[1][None])
    silu_low = jax.nn.silu(cond_used).astype(BF)
    text = text_states[0]
    text_used = jnp.where((chosen == 0)[:, None, None], text[0][None], text[1][None])
    kv_rows = w_cross_kv.shape[0]
    text_cut = text_used.reshape(slots * text_local, fsdp, sp, kv_rows)
    heads_half = HEADS // 2
    half = heads_half * HD
    resid = residual_in[0]
    normed_one = normalize(resid)
    small_slice = fsdp == 8 and sp == 4
    stacked_vectors = jnp.stack([g_cross, g_temp, t_gate]).astype(BF)
    if small_slice:
        qkv_shards = w_qkv.astype(BF).reshape(rows, 3, 2, half).transpose(2, 0, 1, 3).reshape(2, rows, 3 * half)
        silu_blocks = silu_low.astype(F32).reshape(slots, fsdp * sp, rows).transpose(1, 0, 2)
        qkv_half, h_slot, mod_rows, vectors, text_mine, silu_rows = front(
            sp,
            qkv_shards,
            w_ada.astype(BF),
            jnp.pad(silu_blocks, ((0, 0), (0, TILE - slots), (0, 0))),
            jnp.pad(stacked_vectors, ((0, 2 * TILE - 3), (0, 0))),
            text_cut.transpose(2, 0, 1, 3).reshape(sp, slots * text_local, fsdp * kv_rows),
            resid,
        )
        silu_rows = silu_rows[:, :slots].reshape(fsdp * slots, rows).astype(BF)
        modulation = mod_rows[: 6 * slots].reshape(6, slots, 1, width)
        vectors = vectors[:, :, :3].transpose(2, 0, 1, 3).reshape(3, width)
        low = [w.astype(BF) for w in (w_out, w_cross_q, w_cross_out, w_up, w_temp_qkv, w_temp_out)]
        shards = jnp.stack([low[o][:, c : c + width] for o, c in PLAN])
        (
            out_full,
            cross_q_full,
            cross_out_full,
            up_full,
            temp_qkv_full,
            temp_out_full,
            down_full,
            _,
            qkv,
            attn_tok,
            kv_all,
            branch_one,
            cross_in,
            query_c,
            cross_out,
            x_two,
        ) = attend(
            PLAN,
            [w.shape[1] for w in low],
            sp,
            heads_half,
            scale,
            shards,
            w_down.astype(BF),
            w_cross_kv.astype(BF),
            h_slot,
            qkv_half,
            text_mine,
            resid,
            mod_rows,
            jnp.broadcast_to(vectors[:1], (TILE, width)),
        )
        h_slot = h_slot.reshape(2 * tok, width)
        attn_tok = attn_tok.reshape(tok, width)
        shift_one, scale_one, gate_one, shift_two, scale_two, gate_two = (modulation[i] for i in range(6))
    else:
        silu_all = lax.all_gather(silu_low, "fsdp", axis=0, tiled=True)
        silu_rows = lax.dynamic_slice_in_dim(silu_all, (f_index * sp + z_index) * rows, rows, 1)
        modulation = lax.psum(
            lax.psum_scatter(nn(silu_rows, w_ada.astype(BF)), "fsdp", scatter_dimension=0, tiled=True), "sp"
        ).reshape(slots, 6, 1, width)
        shift_one, scale_one, gate_one, shift_two, scale_two, gate_two = (modulation[:, i] for i in range(6))
        vectors = lax.all_gather(stacked_vectors, BOTH, axis=1, tiled=True).astype(F32)
        qkv_half = lax.dynamic_index_in_dim(
            gather(w_qkv).reshape(width, 3, 2, half), core, 2, keepdims=False
        ).reshape(width, 3 * half)
        out_full = gather(w_out)
        cross_q_full = gather(w_cross_q)
        cross_out_full = gather(w_cross_out)
        up_full = gather(w_up)
        down_full = gather(w_down)
        temp_qkv_full = gather(w_temp_qkv)
        temp_out_full = gather(w_temp_out)
        kv_weight = lax.all_gather(w_cross_kv.astype(BF), "fsdp", axis=0, tiled=True)
        text_mine = lax.all_to_all(text_cut, "sp", split_axis=2, concat_axis=0, tiled=True)
        text_mine = text_mine.reshape(sp * slots * text_local, fsdp * kv_rows)
        kv_part = lax.psum_scatter(nn(text_mine, kv_weight), "sp", scatter_dimension=0, tiled=True).astype(BF)
        kv_all = (
            lax.all_gather(kv_part.reshape(1, slots, text_local, 2 * width), "sp", axis=0, tiled=True)
            .transpose(1, 0, 2, 3)
            .reshape(slots, sp * text_local, 2 * width)
        )
        h_one = (normed_one * (1.0 + scale_one) + shift_one).astype(BF).reshape(tok, width)
        h_mine = moves.out(h_one)
        h_slot = jnp.concatenate([h_mine, moves.exchange(h_mine)], axis=0)
        qkv = nn(h_slot, qkv_half).astype(BF)
        o_slot = spatial_fwd(qkv, heads_half, scale)
        o_mine = o_slot[:tok]
        o_other = moves.exchange(o_slot[tok:])
        o_full = jnp.where(
            core == 0,
            jnp.concatenate([o_mine, o_other], axis=1),
            jnp.concatenate([o_other, o_mine], axis=1),
        )
        attn_tok = moves.home(o_full)
    gain_cross, gain_temp, temp_gate = vectors[0], vectors[1], vectors[2]
    if small_slice:
        x_one = resid + gate_one * branch_one
        normed_two = normalize(x_one)
        cross_in, cross_out = cross_in.reshape(tok, width), cross_out.reshape(tok, width)
    else:
        branch_one = nn(attn_tok, out_full).reshape(slots, patches, width)
        x_one = resid + gate_one * branch_one
        normed_two = normalize(x_one)
        cross_in = (normed_two * gain_cross).astype(BF).reshape(tok, width)
        query_c = nn(cross_in, cross_q_full).astype(BF).reshape(slots, patches, width)
        cross_out = cross_fwd(query_c, kv_all, HEADS, scale).reshape(tok, width)
        x_two = x_one + nn(cross_out, cross_out_full).reshape(slots, patches, width)

    normed_three = normalize(x_two)
    h_three = (normed_three * (1.0 + scale_two) + shift_two).astype(BF).reshape(tok, width)
    up_proj = nn(h_three, up_full)
    activated = gelu_tanh(up_proj).astype(BF)
    branch_three = nn(activated, down_full).reshape(slots, patches, width)
    x_three = x_two + gate_two * branch_three

    normed_four = normalize(x_three)
    temp_in = (normed_four * gain_temp).astype(BF).reshape(tok, width)
    trip = nn(temp_in, temp_qkv_full).astype(BF).reshape(slots, patches, 3 * width)
    grad_out = cotangent[0].astype(F32)
    grad_b4 = (grad_out * (video * temp_gate)).astype(BF).reshape(tok, width)
    grad_to = nt(grad_b4, temp_out_full).astype(BF).reshape(slots, patches, width)
    temp_out, grad_trip = temporal(trip, grad_to, HEADS, scale)
    temp_out = temp_out.reshape(tok, width)
    grad_trip = grad_trip.reshape(tok, 3 * width)
    branch_four = nn(temp_out, temp_out_full).reshape(slots, patches, width)
    output = x_three + (video * temp_gate) * branch_four

    grad_tgate = video * jnp.sum(grad_out * branch_four, axis=(0, 1))
    grad_wto = tn(temp_out, grad_b4)
    grad_wtq = tn(temp_in, grad_trip)
    grad_temp_in = nt(grad_trip, temp_qkv_full).reshape(slots, patches, width)
    grad_gtemp = jnp.sum(grad_temp_in * normed_four, axis=(0, 1))
    grad_three = grad_out + normalize_back(x_three, grad_temp_in * gain_temp)

    grad_gate_two = jnp.sum(grad_three * branch_three, axis=1)
    grad_b3 = (grad_three * gate_two).astype(BF).reshape(tok, width)
    grad_wdown = tn(activated, grad_b3)
    grad_act = nt(grad_b3, down_full)
    grad_up = jax.vjp(gelu_tanh, up_proj)[1](grad_act)[0].astype(BF)
    grad_wup = tn(h_three, grad_up)
    grad_h_three = nt(grad_up, up_full).reshape(slots, patches, width)
    grad_shift_two = jnp.sum(grad_h_three, axis=1)
    grad_scale_two = jnp.sum(grad_h_three * normed_three, axis=1)
    grad_two = grad_three + normalize_back(x_two, grad_h_three * (1.0 + scale_two))

    grad_b2 = grad_two.astype(BF).reshape(tok, width)
    grad_wco = tn(cross_out, grad_b2)
    grad_co = nt(grad_b2, cross_out_full).astype(BF).reshape(slots, patches, width)
    grad_qc, grad_kv = cross_bwd(query_c, kv_all, grad_co, HEADS, scale)
    grad_qc = grad_qc.reshape(tok, width)
    grad_kv = (
        grad_kv.reshape(slots, sp, text_local, 2 * width)
        .transpose(1, 0, 2, 3)
        .reshape(sp * slots * text_local, 2 * width)
        .astype(BF)
    )
    grad_wcq = tn(cross_in, grad_qc)
    grad_cross_in = nt(grad_qc, cross_q_full).reshape(slots, patches, width)
    grad_gcross = jnp.sum(grad_cross_in * normed_two, axis=(0, 1))
    grad_one = grad_two + normalize_back(x_one, grad_cross_in * gain_cross)

    grad_gate_one = jnp.sum(grad_one * branch_one, axis=1)
    grad_b1 = (grad_one * gate_one).astype(BF).reshape(tok, width)
    grad_wout = tn(attn_tok, grad_b1)
    grad_attn = nt(grad_b1, out_full).astype(BF)
    if small_slice:
        late = [g.astype(BF) for g in (grad_wout, grad_wcq, grad_wco, grad_wup, grad_wtq, grad_wto)]
        pieces, grad_qkv, grad_kv, grad_wqkv_half = attend_back(
            PLAN,
            sp,
            heads_half,
            scale,
            late,
            grad_attn.reshape(sp, tok // sp, width),
            qkv,
            sum_along(grad_kv.reshape(sp, slots * text_local, 2 * width), sp),
            h_slot,
        )
        grad_kv = grad_kv.reshape(sp * slots * text_local, 2 * width)
        own = [jnp.concatenate([pieces[k] for k, (o, _) in enumerate(PLAN) if o == i], axis=1) for i in range(len(late))]
        own_out, own_cq, own_co, own_up, own_tq, own_to = own
    else:
        go_mine = moves.out(grad_attn)
        low_half, high_half = go_mine[:, :half], go_mine[:, half:]
        go_other = moves.exchange(jnp.where(core == 0, high_half, low_half))
        go_slot = jnp.concatenate([jnp.where(core == 0, low_half, high_half), go_other], axis=0)
        grad_qkv = spatial_bwd(qkv, go_slot, heads_half, scale)
        grad_kv = lax.all_gather(
            lax.psum_scatter(grad_kv, "sp", scatter_dimension=0, tiled=True), "sp", axis=0, tiled=True
        )
        grad_wqkv_half = tn(h_slot, grad_qkv).astype(BF)
    grad_wckv = tn(text_mine, grad_kv)
    known = [grad_gate_one, grad_shift_two, grad_scale_two, grad_gate_two]
    known_vectors = [grad_gcross, grad_gtemp, grad_tgate]
    if small_slice:
        zero = jnp.zeros((slots, width), F32)
        own_down, own_text, own_half, input_grad, small_sp = finish(
            sp,
            grad_wdown.astype(BF),
            grad_wckv.astype(BF),
            grad_wqkv_half,
            grad_qkv,
            qkv_half,
            resid,
            grad_one,
            mod_rows,
            jnp.concatenate([zero, zero] + known + [jnp.stack(known_vectors + [zero[0]])], axis=0),
        )
        own_text = own_text.transpose(1, 0, 2).reshape(kv_rows, 2 * width)
        own_half = jnp.where(core == 0, own_half, own_half[::-1])
        own_qkv = own_half.reshape(2, rows, 3, half).transpose(1, 2, 0, 3).reshape(rows, 3 * width)
    else:
        gh_slot = nt(grad_qkv, qkv_half)
        grad_h_one = moves.home((gh_slot[:tok] + moves.exchange(gh_slot[tok:])).astype(BF))
        grad_h_one = grad_h_one.astype(F32).reshape(slots, patches, width)
        input_grad = grad_one + normalize_back(resid, grad_h_one * (1.0 + scale_one))
        new = [jnp.sum(grad_h_one, axis=1), jnp.sum(grad_h_one * normed_one, axis=1)]
        small = jnp.concatenate(new + known + [jnp.stack(known_vectors)], axis=0)
        small_sp = jnp.sum(
            lax.all_gather(small, BOTH, axis=0).reshape(fsdp, sp, slots * 6 + 3, width), axis=1
        )
    grad_mod = small_sp[:, : slots * 6].reshape(fsdp, 6, slots, width).transpose(0, 2, 1, 3)
    grad_mod = grad_mod.reshape(fsdp * slots, 6 * width)
    grad_wada = jnp.dot(silu_rows.astype(F32).T, grad_mod, precision=HIGHEST, preferred_element_type=F32)
    grad_vec = lax.dynamic_slice_in_dim(
        jnp.sum(small_sp[:, slots * 6 : slots * 6 + 3], axis=0), (f_index * sp + z_index) * rows, rows, 1
    )
    if not small_slice:
        wide = grad_wqkv_half.reshape(width, 3, 1, half)
        zeros = jnp.zeros_like(wide)
        grad_wqkv = jnp.where(
            core == 0, jnp.concatenate([wide, zeros], axis=2), jnp.concatenate([zeros, wide], axis=2)
        ).reshape(width, 3 * width)
        own_qkv, own_out, own_cq, own_co = scatter(grad_wqkv), scatter(grad_wout), scatter(grad_wcq), scatter(grad_wco)
        own_up, own_down, own_tq, own_to = scatter(grad_wup), scatter(grad_wdown), scatter(grad_wtq), scatter(grad_wto)
        own_text = lax.psum_scatter(grad_wckv.astype(BF), "fsdp", scatter_dimension=0, tiled=True).astype(F32)
    return (
        output[None],
        input_grad[None],
        grad_wada,
        own_qkv,
        own_out,
        own_cq,
        own_text,
        own_co,
        own_up,
        own_down,
        own_tq,
        own_to,
        grad_vec[0],
        grad_vec[1],
        grad_vec[2],
    )


def solution(mesh):
    P = jax.sharding.PartitionSpec
    tokens = P("fsdp", None, "sp", None)
    weight = P(BOTH, None)
    vector = P(BOTH)
    return jax.shard_map(
        local,
        mesh=mesh,
        in_specs=(tokens, P("fsdp", None, None), tokens, P("fsdp", None), tokens)
        + (weight,) * 10
        + (vector,) * 3,
        out_specs=(tokens, tokens) + (weight,) * 10 + (vector,) * 3,
        check_vma=False,
    )
```

```python
import functools
from types import SimpleNamespace
import jax, jax.numpy as jnp
from jax import lax
from jax.experimental import pallas as pl
from jax.experimental.pallas import tpu as pltpu
HD=72
F32=jnp.float32; BF=jnp.bfloat16
def nt(a,b): return lax.dot_general(a,b,(((1,),(1,)),((),())),preferred_element_type=F32)
def tn(a,b): return lax.dot_general(a,b,(((0,),(0,)),((),())),preferred_element_type=F32)
def nn(a,b): return jnp.dot(a,b,preferred_element_type=F32)

def spatial_fwd_kernel(heads, scale, qkv, o, st, os):
    T = qkv.shape[0]
    W = heads*HD
    for i in range(3*heads):
        st[i] = jnp.zeros(st.shape[1:], BF)
        st[i, :, :HD] = qkv[:, i*HD:(i+1)*HD]
    tile = 256
    def head(h, _):
        k = st[heads+h]; v = st[2*heads+h]
        def rows(i, _):
            q = st[h, pl.ds(pl.multiple_of(i*tile,tile), tile), :]
            s = nt(q,k)
            m = jnp.max(s,axis=-1,keepdims=True)
            e = jnp.exp((s-m)*scale)
            l = jnp.sum(e,axis=-1,keepdims=True)
            r = nn(e.astype(BF), v)
            os[h, pl.ds(pl.multiple_of(i*tile,tile), tile), :] = (r/l).astype(BF)
            return 0
        lax.fori_loop(0, T//tile, rows, 0)
        return 0
    lax.fori_loop(0, heads, head, 0)
    for h in range(heads):
        o[:, h*HD:(h+1)*HD] = os[h, :, :HD]

def spatial_fwd(qkv, heads, scale):
    T=qkv.shape[0]
    return pl.pallas_call(functools.partial(spatial_fwd_kernel,heads,scale),
        out_shape=jax.ShapeDtypeStruct((T,heads*HD),BF),
        in_specs=[pl.BlockSpec(memory_space=pltpu.VMEM)],
        out_specs=pl.BlockSpec(memory_space=pltpu.VMEM),
        scratch_shapes=[pltpu.VMEM((3*heads,T,128),BF),pltpu.VMEM((heads,T,128),BF)],
        compiler_params=pltpu.CompilerParams(vmem_limit_bytes=48*2**20),
        cost_estimate=pl.CostEstimate(flops=4*heads*T*T*128,bytes_accessed=T*heads*HD*8,transcendentals=heads*T*T),
        name="spatial_fwd")(qkv)

def spatial_bwd_kernel(heads, scale, qkv, go, g, st, gs, acc):
    T = qkv.shape[0]
    for i in range(3*heads):
        st[i] = jnp.zeros(st.shape[1:], BF)
        st[i, :, :HD] = qkv[:, i*HD:(i+1)*HD]
    for h in range(heads):
        gs[h] = jnp.zeros(gs.shape[1:], BF)
        gs[h, :, :HD] = go[:, h*HD:(h+1)*HD]
    tile = 256
    def head(h, _):
        k = st[heads+h]; v = st[2*heads+h]
        acc[...] = jnp.zeros(acc.shape, F32)
        def cols(i, _):
            sl = pl.ds(pl.multiple_of(i*tile,tile), tile)
            q = st[h, sl, :]; gq_in = gs[h, sl, :]
            s = nt(k,q)
            m = jnp.max(s,axis=0,keepdims=True)
            e = jnp.exp((s-m)*scale)
            p = e * (1.0/jnp.sum(e,axis=0,keepdims=True))
            dp = nt(v,gq_in)
            t = dp*p
            d = jnp.sum(t,axis=0,keepdims=True)
            ds = (t-p*d).astype(BF)
            acc[0] += nn(ds,q)
            acc[1] += nn(p.astype(BF),gq_in)
            st[h, sl, :] = (tn(ds,k)*scale).astype(BF)
            return 0
        lax.fori_loop(0, T//tile, cols, 0)
        st[heads+h] = (acc[0]*scale).astype(BF)
        st[2*heads+h] = acc[1].astype(BF)
        return 0
    lax.fori_loop(0, heads, head, 0)
    for i in range(3*heads):
        g[:, i*HD:(i+1)*HD] = st[i, :, :HD]

def spatial_bwd(qkv, go, heads, scale):
    T=qkv.shape[0]
    return pl.pallas_call(functools.partial(spatial_bwd_kernel,heads,scale),
        out_shape=jax.ShapeDtypeStruct((T,3*heads*HD),BF),
        in_specs=[pl.BlockSpec(memory_space=pltpu.VMEM)]*2,
        out_specs=pl.BlockSpec(memory_space=pltpu.VMEM),
        scratch_shapes=[pltpu.VMEM((3*heads,T,128),BF),pltpu.VMEM((heads,T,128),BF),pltpu.VMEM((2,T,128),F32)],
        compiler_params=pltpu.CompilerParams(vmem_limit_bytes=56*2**20),
        cost_estimate=pl.CostEstimate(flops=10*heads*T*T*128,bytes_accessed=T*heads*HD*16,transcendentals=heads*T*T),
        name="spatial_bwd")(qkv, go)

def cross_fwd_kernel(heads, scale, q, kv, o):
    S,T,W = q.shape
    for h in range(heads):
        c = slice(h*HD,(h+1)*HD); cv = slice(W+h*HD, W+(h+1)*HD)
        s = nt(q[0,:,c], kv[0,:,c])
        m = jnp.max(s,axis=-1,keepdims=True)
        e = jnp.exp((s-m)*scale)
        l = jnp.sum(e,axis=-1,keepdims=True)
        o[0,:,c] = (nn(e.astype(BF), kv[0,:,cv])/l).astype(BF)

def cross_fwd(q, kv, heads, scale):
    S,T,W = q.shape; K=kv.shape[1]
    return pl.pallas_call(functools.partial(cross_fwd_kernel,heads,scale),
        grid=(S,),
        out_shape=jax.ShapeDtypeStruct((S,T,W),BF),
        in_specs=[pl.BlockSpec((1,T,W),lambda s:(s,0,0)),pl.BlockSpec((1,K,2*W),lambda s:(s,0,0))],
        out_specs=pl.BlockSpec((1,T,W),lambda s:(s,0,0)),
        compiler_params=pltpu.CompilerParams(vmem_limit_bytes=32*2**20),
        cost_estimate=pl.CostEstimate(flops=4*S*heads*T*K*128,bytes_accessed=S*T*W*4,transcendentals=S*heads*T*K),
        name="cross_fwd")(q,kv)

def cross_bwd_kernel(heads, scale, q, kv, go, gq, gkv):
    S,T,W = q.shape
    for h in range(heads):
        c = slice(h*HD,(h+1)*HD); cv = slice(W+h*HD, W+(h+1)*HD)
        qh=q[0,:,c]; kh=kv[0,:,c]; vh=kv[0,:,cv]; gh=go[0,:,c]
        s = nt(kh,qh)
        m = jnp.max(s,axis=0,keepdims=True)
        e = jnp.exp((s-m)*scale)
        p = e*(1.0/jnp.sum(e,axis=0,keepdims=True))
        dp = nt(vh,gh)
        t = dp*p
        ds = (t-p*jnp.sum(t,axis=0,keepdims=True)).astype(BF)
        gq[0,:,c] = (tn(ds,kh)*scale).astype(BF)
        gkv[0,:,c] = nn(ds,qh)*scale
        gkv[0,:,cv] = nn(p.astype(BF),gh)

def cross_bwd(q, kv, go, heads, scale):
    S,T,W = q.shape; K=kv.shape[1]
    return pl.pallas_call(functools.partial(cross_bwd_kernel,heads,scale),
        grid=(S,),
        out_shape=(jax.ShapeDtypeStruct((S,T,W),BF),jax.ShapeDtypeStruct((S,K,2*W),F32)),
        in_specs=[pl.BlockSpec((1,T,W),lambda s:(s,0,0)),pl.BlockSpec((1,K,2*W),lambda s:(s,0,0)),pl.BlockSpec((1,T,W),lambda s:(s,0,0))],
        out_specs=(pl.BlockSpec((1,T,W),lambda s:(s,0,0)),pl.BlockSpec((1,K,2*W),lambda s:(s,0,0))),
        compiler_params=pltpu.CompilerParams(vmem_limit_bytes=32*2**20),
        cost_estimate=pl.CostEstimate(flops=10*S*heads*T*K*128,bytes_accessed=S*T*W*8,transcendentals=S*heads*T*K),
        name="cross_bwd")(q,kv,go)


MESH = pl.DeviceIdType.MESH
BLOCK = 144
PIECE = 36
WIDE = 1152


class Place:
    def __init__(self, sp):
        self.sp = sp
        self.f = lax.axis_index("fsdp")
        self.z = lax.axis_index("sp")
        self.core = self.f % 2
        self.x = (self.f // 2) % 2
        self.y = self.f // 4
        self.q = self.f // 2

    def flip(self, bit):
        step = {"core": 1, "x": 2, "y": 4}[bit]
        here = {"core": self.core, "x": self.x, "y": self.y}[bit]
        return (self.f + step * (1 - 2 * here), self.z)

    def along(self, r):
        return (self.f, (self.z + r) % self.sp)

    def peers(self):
        return [self.flip(b) for b in ("core", "x", "y")] + [self.along(r) for r in range(1, self.sp)]


def greet(place):
    barrier = pltpu.get_barrier_semaphore()
    peers = place.peers()
    for peer in peers:
        pl.semaphore_signal(barrier, inc=1, device_id=peer, device_id_type=MESH)
    pl.semaphore_wait(barrier, len(peers))


def remote(src, dst, send, recv, device):
    return pltpu.make_async_remote_copy(
        src_ref=src, dst_ref=dst, send_sem=send, recv_sem=recv, device_id=device, device_id_type=MESH
    )


class Gather:
    def __init__(self, place, chunks, send, recv):
        self.place, self.chunks, self.send, self.recv = place, chunks, send, recv

    def region(self, i, f):
        array, row, rows, columns, _ = self.chunks[i]
        return array.at[pl.ds(pl.multiple_of(row(f), 16), rows), columns]

    def copy(self, i, event, f, bit):
        src = self.region(i, f)
        return remote(src, src, self.send.at[i, event], self.recv.at[i, event], self.place.flip(bit))

    def bits(self, i):
        return ("x", "y") if self.chunks[i][4] == 0 else ("y", "x")

    def copies(self, i):
        p = self.place
        first, second = self.bits(i)
        f = p.f
        f_first = p.flip(first)[0]
        f_second = p.flip(second)[0]
        f_diagonal = f_first + f_second - f
        return [
            self.copy(i, 0, f, first),
            self.copy(i, 1, f, second),
            self.copy(i, 2, f_first, second),
            self.copy(i, 3, f, "core"),
            self.copy(i, 4, f_first, "core"),
            self.copy(i, 5, f_second, "core"),
            self.copy(i, 6, f_diagonal, "core"),
        ]

    def begin(self, i):
        c = self.copies(i)
        for e in (0, 1, 3):
            c[e].start()

    def middle(self, i):
        c = self.copies(i)
        c[0].wait_recv()
        c[2].start()
        c[4].start()

    def late(self, i):
        c = self.copies(i)
        c[1].wait_recv()
        c[5].start()
        c[2].wait_recv()
        c[6].start()

    def finish(self, i):
        c = self.copies(i)
        for e in (3, 4, 5, 6):
            c[e].wait_recv()
        for one in c:
            one.wait_send()


def gather_kernel(plan, sp, shards, down_shard, text_shard, *rest):
    n_out = len({o for o, _ in plan})
    outs = rest[:n_out]
    down, text = rest[n_out], rest[n_out + 1]
    landed, block, send, recv, zsend, zrecv, dsend, drecv, local_sem = rest[n_out + 2 :]
    p = Place(sp)
    greet(p)
    n = len(plan)
    ahead = 3

    def launch(i):
        if i < n:
            for r in range(1, sp):
                remote(
                    shards.at[i], landed.at[i, p.z], zsend.at[i, r - 1], zrecv.at[i, r - 1], p.along(r)
                ).start()
            landed[i, p.z] = shards[i]
        elif i == n:
            for r in range(1, sp):
                remote(down_shard, down_own, dsend.at[r - 1], drecv.at[p.z], p.along(r)).start()

    rows = down_shard.shape[0]
    down_own = down.at[pl.ds(pl.multiple_of(p.f * (sp * rows) + p.z * rows, 16), rows), :]
    for i in range(ahead):
        launch(i)
    pltpu.make_async_copy(down_shard, down_own, drecv.at[p.z]).start()
    trows = text_shard.shape[0]
    text_own = text.at[pl.ds(pl.multiple_of(p.f * trows, 16), trows), :]
    text_copy = pltpu.make_async_copy(text_shard, text_own, local_sem.at[2])
    text_copy.start()

    chunks = [
        (outs[o], lambda f: f * BLOCK, BLOCK, pl.ds(c, WIDE), k % 2) for k, (o, c) in enumerate(plan)
    ]
    chunks += [
        (down, lambda f, j=j: f * (sp * rows) + j * rows, rows, pl.ds(0, WIDE), (n + j) % 2) for j in range(sp)
    ]
    chunks += [(text, lambda f: f * trows, trows, pl.ds(k * WIDE, WIDE), (n + k) % 2) for k in range(2)]
    g = Gather(p, chunks, send, recv)

    def ready(i):
        if i < n:
            for r in range(1, sp):
                remote(
                    shards.at[i], landed.at[i, p.z], zsend.at[i, r - 1], zrecv.at[i, r - 1], p.along(r)
                ).wait_recv()
            slot = i % 2
            for zz in range(sp):
                block[slot, PIECE * zz : PIECE * (zz + 1), :] = landed[i, zz]
            copy = pltpu.make_async_copy(block.at[slot], g.region(i, p.f), local_sem.at[slot])
            copy.start()
            copy.wait()
        elif i < n + sp:
            remote(down_shard, down_own, dsend.at[0], drecv.at[i - n], p.along(1)).wait_recv()
        elif i == n + sp:
            text_copy.wait()

    total = len(chunks)
    for t in range(total + 2):
        if t < total:
            launch(t + ahead)
            ready(t)
            g.begin(t)
        if 0 <= t - 1 < total:
            g.middle(t - 1)
        if 0 <= t - 2 < total:
            g.late(t - 2)
    for i in range(total):
        g.finish(i)
    for i in range(n):
        for r in range(1, sp):
            remote(
                shards.at[i], landed.at[i, p.z], zsend.at[i, r - 1], zrecv.at[i, r - 1], p.along(r)
            ).wait_send()
    for r in range(1, sp):
        remote(down_shard, down_own, dsend.at[r - 1], drecv.at[p.z], p.along(r)).wait_send()


def gather_all(plan, widths, sp, shards, down_shard, text_shard):
    n = len(plan)
    total = n + sp + 2
    any_space = pl.BlockSpec(memory_space=pl.ANY)
    vmem = pl.BlockSpec(memory_space=pltpu.VMEM)
    dma = pltpu.SemaphoreType.DMA
    return pl.pallas_call(
        functools.partial(gather_kernel, plan, sp),
        out_shape=[jax.ShapeDtypeStruct((8 * BLOCK, w), BF) for w in widths]
        + [
            jax.ShapeDtypeStruct((8 * sp * down_shard.shape[0], WIDE), BF),
            jax.ShapeDtypeStruct((8 * text_shard.shape[0], 2 * WIDE), BF),
        ],
        in_specs=[vmem, any_space, any_space],
        out_specs=[any_space] * (len(widths) + 2),
        scratch_shapes=[
            pltpu.VMEM((n, sp, PIECE, WIDE), BF),
            pltpu.VMEM((2, BLOCK, WIDE), BF),
            dma((total, 7)),
            dma((total, 7)),
            dma((n, sp - 1)),
            dma((n, sp - 1)),
            dma((sp - 1,)),
            dma((sp,)),
            dma((3,)),
        ],
        compiler_params=pltpu.CompilerParams(
            collective_id=1, has_side_effects=True, vmem_limit_bytes=48 * 2**20
        ),
        name="gather_all",
    )(shards, down_shard, text_shard)


RING = 6
PIECES, DOWN, TEXT_ROWS, HALVES = range(4)
DELAY = 2


class Reduce:
    def __init__(self, place, chunks, sems):
        self.p, self.chunks = place, chunks
        self.core_send, self.core_recv, self.two_send = sems.core_send, sems.core_recv, sems.two_send
        self.two_recv, self.one_send, self.one_recv, self.load = sems.two_recv, sems.one_send, sems.one_recv, sems.load

    def slot(self, i):
        return self.chunks[i].slot

    def before(self, i):
        same = [k for k in range(i) if self.chunks[k].sums is self.chunks[i].sums and self.slot(k) == self.slot(i)]
        return same[-1] if same else None

    def after(self, i):
        return [k for k in range(i + 1, len(self.chunks)) if self.before(k) == i]

    def cross(self, i):
        c = self.chunks[i]
        return remote(
            c.sent(1 - self.p.core), c.arrived, self.core_send.at[i], self.core_recv.at[i], self.p.flip("core")
        )

    def start(self, i):
        if self.chunks[i].sent is not None:
            self.cross(i).start()

    def loads(self, i):
        c = self.chunks[i]
        sums = c.sums.at[self.slot(i)]
        out = []
        if c.kept is not None:
            out.append(pltpu.make_async_copy(c.kept(self.p.core), sums, self.load.at[i % 3, 0]))
            if c.sent is not None:
                out.append(pltpu.make_async_copy(c.arrived, c.other.at[i % 2], self.load.at[i % 3, 1]))
        else:
            out.append(pltpu.make_async_copy(c.arrived, sums, self.load.at[i % 3, 0]))
        return out

    def prefetch(self, i):
        k = self.before(i)
        if k is not None:
            self.two(k).wait_send()
            self.one(k).wait_send()
        if self.chunks[i].sent is not None:
            self.cross(i).wait_recv()
        for copy in self.loads(i):
            copy.start()

    def views(self, i):
        c, p = self.chunks[i], self.p
        sums = c.sums
        s = self.slot(i)
        if c.order == 0:
            return ("y", "x", sums.at[s, 1 - p.y], lambda k: (s, p.y, k), 1 - p.x, p.x)
        return ("x", "y", sums.at[s, :, 1 - p.x], lambda k: (s, k, p.x), 1 - p.y, p.y)

    def two(self, i):
        first, _, leaving, _, _, _ = self.views(i)
        return remote(leaving, self.chunks[i].two, self.two_send.at[i], self.two_recv.at[i], self.p.flip(first))

    def one(self, i):
        _, second, _, at, away, _ = self.views(i)
        return remote(
            self.chunks[i].sums.at[at(away)],
            self.chunks[i].one,
            self.one_send.at[i],
            self.one_recv.at[i],
            self.p.flip(second),
        )

    def add(self, i):
        c = self.chunks[i]
        for copy in self.loads(i):
            copy.wait()
        s = self.slot(i)
        if c.kept is not None and c.sent is not None:
            rows = c.sums.shape[-2]
            sums, other = c.sums, c.other

            def tile(t, _):
                r = pl.ds(pl.multiple_of(t * 16, 16), 16)
                for a in range(2):
                    for b in range(2):
                        sums[s, a, b, r, :] = (
                            sums[s, a, b, r, :].astype(F32) + other[i % 2, a, b, r, :].astype(F32)
                        ).astype(BF)
                return 0

            lax.fori_loop(0, rows // 16, tile, 0)
        self.two(i).start()

    def second(self, i):
        c = self.chunks[i]
        _, _, _, at, away, stay = self.views(i)
        self.two(i).wait_recv()
        sums, two = c.sums, c.two
        rows = sums.shape[-2]

        def fold(k):
            def tile(t, _):
                r = pl.ds(pl.multiple_of(t * 16, 16), 16)
                here = at(k) + (r, slice(None))
                sums[here] = (sums[here].astype(F32) + two[k, r, :].astype(F32)).astype(BF)
                return 0

            lax.fori_loop(0, rows // 16, tile, 0)

        fold(away)
        self.one(i).start()
        fold(stay)

    def third(self, i, store):
        c = self.chunks[i]
        _, _, _, at, _, stay = self.views(i)
        self.one(i).wait_recv()
        store(lambda r: c.sums[at(stay) + (r, slice(None))].astype(F32) + c.one[r, :].astype(F32))

    def drain(self, i, total):
        if self.chunks[i].sent is not None:
            self.cross(i).wait_send()
        if not self.after(i):
            self.two(i).wait_send()
            self.one(i).wait_send()


def along_z(p, sp, source, landing, send, recv):
    return [
        remote(source((p.z + r) % sp), landing(r - 1), send(r - 1), recv(r - 1), p.along(r)) for r in range(1, sp)
    ]


class Sums:
    def __init__(self, sp, plan, down, text, half):
        self.sp, self.plan, self.down, self.text, self.half = sp, plan, down, text, half
        self.blocks = len(plan) + (sp if down else 0)
        self.total = self.blocks + (2 if text else 0) + (2 if half else 0)
        shape = jax.ShapeDtypeStruct
        self.results, self.landings, self.scratch = {}, {}, {}
        block = (BLOCK, WIDE)
        if self.blocks:
            self.landings.update(arrived=shape((self.blocks, 2, 2) + block, BF))
            self.scratch.update(sums=pltpu.VMEM((min(RING, self.blocks), 2, 2) + block, BF))
            self.scratch.update(other=pltpu.VMEM((2, 2, 2) + block, BF))
            self.scratch.update(two=pltpu.VMEM((self.blocks, 2) + block, BF))
            self.scratch.update(one=pltpu.VMEM((self.blocks,) + block, BF))
        if plan:
            n = len(plan)
            self.results.update(piece=shape((n, PIECE, WIDE), F32))
            self.scratch.update(pieces=pltpu.VMEM((n, sp, PIECE, WIDE), BF))
            self.scratch.update(pieces_in=pltpu.VMEM((n, sp - 1, PIECE, WIDE), BF))
        if down:
            self.results.update(down=shape(block, F32))
            self.scratch.update(blocks_d=pltpu.VMEM((sp,) + block, BF))
            self.scratch.update(blocks_d_in=pltpu.VMEM((sp - 1,) + block, BF))
        if text:
            self.results.update(text=shape((2, text, WIDE), F32))
            self.landings.update(arrived_text=shape((2, 2, 2, text, WIDE), BF))
            self.scratch.update(sums_t=pltpu.VMEM((2, 2, 2, text, WIDE), BF))
            self.scratch.update(other_t=pltpu.VMEM((2, 2, 2, text, WIDE), BF))
            self.scratch.update(two_t=pltpu.VMEM((2, 2, text, WIDE), BF))
            self.scratch.update(one_t=pltpu.VMEM((2, text, WIDE), BF))
        if half:
            self.results.update(half=shape((2, PIECE, half), F32))
            self.landings.update(arrived_half=shape((2, 2, BLOCK, half), BF))
            self.scratch.update(sums_h=pltpu.VMEM((2, 2, 2, BLOCK, half), BF))
            self.scratch.update(two_h=pltpu.VMEM((2, 2, BLOCK, half), BF))
            self.scratch.update(one_h=pltpu.VMEM((2, BLOCK, half), BF))
            self.scratch.update(pieces_h=pltpu.VMEM((2, sp, PIECE, half), BF))
            self.scratch.update(pieces_h_in=pltpu.VMEM((2, sp - 1, PIECE, half), BF))
        dma = pltpu.SemaphoreType.DMA
        each = dma((self.total,))
        self.scratch.update(
            core_send=each, core_recv=each, two_send=each, two_recv=each, one_send=each, one_recv=each
        )
        self.scratch.update(load=dma((3, 2)))
        self.scratch.update(zsend=dma((self.total, sp - 1)))
        self.scratch.update(zrecv=dma((self.total, sp - 1)))

    def arrays(self, grads, down=None, text=None, halves=None):
        out = [g.reshape(2, 2, 2, BLOCK, g.shape[1]) for g in grads]
        if self.down:
            out.append(down.reshape(2, 2, 2, self.sp, BLOCK, WIDE))
        if self.text:
            out.append(text.reshape(2, 2, 2, self.text, 2 * WIDE))
        if self.half:
            out.append(halves.reshape(2, 2, 2, BLOCK, self.half))
        return out

    def bind(self, place, arrays, refs):
        arrays = list(arrays)
        self.p, self.refs = place, refs
        halves = arrays.pop() if self.half else None
        text = arrays.pop() if self.text else None
        down = arrays.pop() if self.down else None
        chunks = []
        if self.text:
            for k in range(2):
                view = lambda core, k=k: text.at[:, :, core, :, pl.ds(k * WIDE, WIDE)]
                chunks.append(SimpleNamespace(kept=view, sent=view, kind=TEXT_ROWS, index=k, slot=k))
                chunks[-1].__dict__.update(sums=refs.sums_t, other=refs.other_t, arrived=refs.arrived_text.at[k])
                chunks[-1].__dict__.update(two=refs.two_t.at[k], one=refs.one_t.at[k])
        blocks = []
        if self.down:
            for j in range(self.sp):
                view = lambda core, j=j: down.at[:, :, core, j]
                blocks.append(SimpleNamespace(kept=view, sent=view, kind=DOWN, index=j))
        for k, (o, c) in enumerate(self.plan):
            view = lambda core, o=o, c=c: arrays[o].at[:, :, core, :, pl.ds(c, WIDE)]
            blocks.append(SimpleNamespace(kept=view, sent=view, kind=PIECES, index=k))
        for k, c in enumerate(blocks):
            c.__dict__.update(sums=refs.sums, other=refs.other, arrived=refs.arrived.at[k], slot=k % min(RING, self.blocks))
            c.__dict__.update(two=refs.two.at[k], one=refs.one.at[k])
        chunks, plain = blocks, chunks
        if self.half:
            view = lambda core: halves.at[:, :, core]
            for k in range(2):
                chunks.append(SimpleNamespace(kept=None if k else view, sent=view if k else None, kind=HALVES, index=k, slot=k))
                chunks[-1].__dict__.update(sums=refs.sums_h, arrived=refs.arrived_half)
                chunks[-1].__dict__.update(two=refs.two_h.at[k], one=refs.one_h.at[k])
        chunks = chunks + plain
        for k, c in enumerate(chunks):
            c.order = k % 2
        self.chunks = chunks
        self.red = Reduce(place, chunks, refs)

    def sends(self, i):
        c, refs, p, sp = self.chunks[i], self.refs, self.p, self.sp
        k = c.index
        sems = (lambda r: refs.zsend.at[i, r], lambda r: refs.zrecv.at[i, r])
        if c.kind == PIECES:
            return along_z(p, sp, lambda z: refs.pieces.at[k, z], lambda r: refs.pieces_in.at[k, r], *sems)
        if c.kind == HALVES:
            return along_z(p, sp, lambda z: refs.pieces_h.at[k, z], lambda r: refs.pieces_h_in.at[k, r], *sems)
        if c.kind == DOWN and k == sp - 1:
            return along_z(p, sp, lambda z: refs.blocks_d.at[z], lambda r: refs.blocks_d_in.at[r], *sems)
        return []

    def store(self, i):
        c, sp = self.chunks[i], self.sp
        k = c.index

        def cut(target):
            def inner(value):
                for z in range(sp):
                    low = PIECE * z - PIECE * z % 16
                    high = PIECE * (z + 1)
                    high += -high % 16
                    rows = value(pl.ds(low, high - low))
                    target[k, z] = rows[PIECE * z - low : PIECE * z - low + PIECE].astype(BF)

            return inner

        def tiles(target, rows, kind):
            def inner(value):
                def tile(t, _):
                    r = pl.ds(pl.multiple_of(t * 16, 16), 16)
                    target[k, r, :] = value(r).astype(kind)
                    return 0

                lax.fori_loop(0, rows // 16, tile, 0)

            return inner

        if c.kind == PIECES:
            return cut(self.refs.pieces)
        if c.kind == HALVES:
            return cut(self.refs.pieces_h)
        if c.kind == DOWN:
            return tiles(self.refs.blocks_d, BLOCK, BF)
        return tiles(self.refs.text, self.text, F32)

    def last(self, i):
        c, refs, p, sp = self.chunks[i], self.refs, self.p, self.sp
        k = c.index
        for copy in self.sends(i):
            copy.wait_recv()
        if c.kind in (PIECES, HALVES):
            result, mine, others_in = (
                (refs.piece, refs.pieces, refs.pieces_in)
                if c.kind == PIECES
                else (refs.half, refs.pieces_h, refs.pieces_h_in)
            )
            result[k] = mine[k, p.z].astype(F32) + sum(others_in[k, r].astype(F32) for r in range(sp - 1))
        elif c.kind == DOWN and k == sp - 1:

            def tile(t, _):
                r = pl.ds(pl.multiple_of(t * 16, 16), 16)
                refs.down[r, :] = refs.blocks_d[p.z, r, :].astype(F32) + sum(
                    refs.blocks_d_in[a, r, :].astype(F32) for a in range(sp - 1)
                )
                return 0

            lax.fori_loop(0, BLOCK // 16, tile, 0)

    ahead = 4

    def begin(self):
        for i in range(min(self.ahead, self.total)):
            self.red.start(i)
        self.red.prefetch(0)

    def step(self, t):
        red, total = self.red, self.total
        if t + self.ahead < total:
            red.start(t + self.ahead)
        if t + 1 < total:
            red.prefetch(t + 1)
        if t < total:
            red.add(t)
        if 0 <= t - DELAY < total:
            red.second(t - DELAY)
        i = t - 2 * DELAY
        if 0 <= i < total:
            red.third(i, self.store(i))
            for copy in self.sends(i):
                copy.start()
        if 0 <= i - 2 < total:
            self.last(i - 2)

    def steps(self):
        return [functools.partial(self.step, t) for t in range(self.total + 2 * DELAY + 2)]

    def end(self):
        for i in range(self.total):
            self.red.drain(i, self.total)
            for copy in self.sends(i):
                copy.wait_send()


MOD_ROWS = 16
START, WAIT_RECV, WAIT_SEND = range(3)
TILE = 8


class Pairs:
    def __init__(self, p):
        self.p = p

    def owner(self, t):
        p = self.p
        return (p.f - p.core + t % 2, 2 * p.core + t // 2)

    def is_owner(self, t):
        p = self.p
        return jnp.logical_and(p.core == t % 2, p.z == 2 * p.core + t // 2)

    def source(self, z):
        p = self.p
        return (p.f - p.core + p.z // 2, z)

    def is_source(self, z):
        p = self.p
        return jnp.logical_and(p.core == p.z // 2, p.z == z)

    def mine(self):
        return 2 * (self.p.z % 2) + self.p.core


def to_owners(p, blocks, landing, send, recv, do, only=range(4)):
    pairs = Pairs(p)
    for i in only:
        if do == WAIT_RECV:
            remote(blocks.at[0], landing.at[i], send.at[0], recv.at[i], pairs.owner(0)).wait_recv()
            continue
        far = remote(blocks.at[i], landing.at[p.z], send.at[i], recv.at[p.z], pairs.owner(i))
        near = pltpu.make_async_copy(blocks.at[i], landing.at[p.z], recv.at[p.z])

        @pl.when(jnp.logical_not(pairs.is_owner(i)))
        def _():
            far.start() if do == START else far.wait_send()

        if do == START:

            @pl.when(pairs.is_owner(i))
            def _():
                near.start()


def to_homes(p, blocks, landing, send, recv, do):
    pairs = Pairs(p)
    mine = pairs.mine()
    for i in range(4):
        if do == WAIT_RECV:
            remote(blocks.at[0], landing.at[i], send.at[0], recv.at[i], pairs.source(0)).wait_recv()
            continue
        far = remote(blocks.at[i], landing.at[mine], send.at[i], recv.at[mine], pairs.source(i))
        near = pltpu.make_async_copy(blocks.at[i], landing.at[mine], recv.at[mine])

        @pl.when(jnp.logical_not(pairs.is_source(i)))
        def _():
            far.start() if do == START else far.wait_send()

        if do == START:

            @pl.when(pairs.is_source(i))
            def _():
                near.start()


def others(p):
    out = []
    for m in range(1, 8):
        f = p.f
        for bit, step, here in ((1, 1, p.core), (2, 2, p.x), (4, 4, p.y)):
            if m & bit:
                f = f + step * (1 - 2 * here)
        out.append((f, p.z))
    return out


def group(p):
    sib = p.flip("core")[0]
    return [p.along(r) for r in range(1, p.sp)] + [(sib, (p.z + r) % p.sp) for r in range(1, p.sp)]


def greet_list(peers):
    barrier = pltpu.get_barrier_semaphore()
    for peer in peers:
        pl.semaphore_signal(barrier, inc=1, device_id=peer, device_id_type=MESH)
    pl.semaphore_wait(barrier, len(peers))


def front_kernel(
    sp,
    shards,
    ada,
    silu,
    vectors,
    text,
    resid,
    full,
    h_slot,
    modulation,
    vector_rows,
    text_mine,
    silu_in,
    vectors_all,
    landed,
    block,
    parts,
    parts_in,
    sums_in,
    vec_own,
    vec_in,
    text_in,
    h_blocks,
    send,
    recv,
    zsend,
    zrecv,
    csend,
    crecv,
    local_sem,
    s1,
    r1,
    s2,
    r2,
    s3,
    r3,
    sv1,
    rv1,
    sv2,
    rv2,
    st,
    rt,
    sh,
    rh,
    sx,
    rx,
):
    p = Place(sp)
    near = others(p)
    greet_list(near + group(p))
    here = lambda f: full.at[pl.ds(pl.multiple_of(f * BLOCK, 16), BLOCK), :]
    orders = [1 - p.core, p.core]

    def cond(m):
        f = near[m][0]
        return remote(silu.at[f * sp + p.z], silu_in.at[p.f], s1.at[m], r1.at[m], near[m])

    for m in range(7):
        cond(m).start()
    silu_in[p.f] = silu[p.f * sp + p.z]

    vec_own[...] = vectors[:TILE, :].astype(F32)
    vec_in[p.z] = vec_own[...]

    def vec_z(r):
        return remote(vec_own, vec_in.at[p.z], sv1.at[r - 1], rv1.at[r - 1], p.along(r))

    for r in range(1, sp):
        vec_z(r).start()

    def spread(k, r):
        return remote(
            shards.at[orders[k]], landed.at[orders[k], p.z], zsend.at[k, r - 1], zrecv.at[k, r - 1], p.along(r)
        )

    for k in range(2):
        for r in range(1, sp):
            spread(k, r).start()
        landed[orders[k], p.z] = shards[orders[k]]

    def text_z(r):
        z = (p.z + r) % sp
        return remote(text.at[z], text_in.at[p.z], st.at[r - 1], rt.at[r - 1], p.along(r))

    for r in range(1, sp):
        text_z(r).start()
    text_in[p.z] = text[p.z]

    for m in range(7):
        cond(m).wait_recv()
    rows = jnp.concatenate([silu_in[f][:2] for f in range(8)], axis=0).astype(BF)
    slots = 2
    for j in range(6):
        res = nn(rows, ada[:, j * WIDE : (j + 1) * WIDE])
        for f in range(8):
            parts[f, slots * j : slots * (j + 1), :] = res[slots * f : slots * (f + 1)]
    for f in range(8):
        parts[f, 6 * slots :, :] = jnp.zeros((MOD_ROWS - 6 * slots, WIDE), F32)

    def part(m):
        return remote(parts.at[near[m][0]], parts_in.at[m], s2.at[m], r2.at[m], near[m])

    for m in range(7):
        part(m).start()

    sibling = p.flip("core")[0]

    def cross():
        return remote(block.at[0], here(p.f), csend.at[0], crecv.at[0], p.flip("core"))

    def copies(k):
        f = sibling if k == 0 else p.f
        first, second = ("x", "y") if k == 0 else ("y", "x")
        step = p.flip(first)[0] - p.f
        return [
            remote(here(g), here(g), send.at[k, e], recv.at[k, e], p.flip(bit))
            for e, g, bit in ((0, f, first), (1, f, second), (2, f + step, second))
        ]

    for k in range(2):
        for r in range(1, sp):
            spread(k, r).wait_recv()
        for zz in range(sp):
            block[k, PIECE * zz : PIECE * (zz + 1), :] = landed[orders[k], zz]
        if k == 0:
            cross().start()
    own = pltpu.make_async_copy(block.at[1], here(p.f), local_sem.at[0])
    own.start()

    for m in range(7):
        part(m).wait_recv()
    parts[p.f] = parts[p.f] + sum(parts_in[m] for m in range(7))

    def total(r):
        return remote(parts.at[p.f], sums_in.at[r - 1], s3.at[r - 1], r3.at[r - 1], p.along(r))

    for r in range(1, sp):
        total(r).start()
    own.wait()
    for e in (0, 1):
        copies(1)[e].start()
    cross().wait_recv()
    for e in (0, 1):
        copies(0)[e].start()
    for r in range(1, sp):
        vec_z(r).wait_recv()

    def vec_f(m):
        return remote(vec_in, vectors_all.at[p.f], sv2.at[m], rv2.at[m], near[m])

    for m in range(7):
        vec_f(m).start()
    vectors_all[p.f] = vec_in[...]
    for r in range(1, sp):
        total(r).wait_recv()
    modulation[...] = parts[p.f] + sum(sums_in[r] for r in range(sp - 1))

    patches = resid.shape[1]
    step = 32
    for s in range(slots):
        for k in range(2):

            def tile(i, _):
                r = pl.multiple_of(i * step, step)
                v = resid[s, pl.ds(k * (patches // 2) + r, step), :]
                c = v - jnp.mean(v, axis=-1, keepdims=True)
                n = c * lax.rsqrt(jnp.mean(c * c, axis=-1, keepdims=True) + 1e-06)
                h = n * (1.0 + modulation[slots + s : slots + s + 1, :]) + modulation[s : s + 1, :]
                h_blocks[2 * s + k, pl.ds(r, step), :] = h.astype(BF)
                return 0

            lax.fori_loop(0, patches // 2 // step, tile, 0)
            to_owners(p, h_blocks, h_slot.at[0], sh, rh, START, [2 * s + k])
    for k in (1, 0):
        copies(k)[0].wait_recv()
        copies(k)[2].start()
    for r in range(1, sp):
        text_z(r).wait_recv()
    text_rows = text_in.shape[1]
    for zz in range(sp):
        text_mine[text_rows * zz : text_rows * (zz + 1), :] = text_in[zz]

    def swap(z):
        return remote(h_slot.at[0, z], h_slot.at[1, z], sx.at[z], rx.at[z], p.flip("core"))

    for z in range(sp):
        to_owners(p, h_blocks, h_slot.at[0], sh, rh, WAIT_RECV, [z])
        swap(z).start()
    for k in range(2):
        copies(k)[1].wait_recv()
        copies(k)[2].wait_recv()
        for e in range(3):
            copies(k)[e].wait_send()
        for r in range(1, sp):
            spread(k, r).wait_send()
    cross().wait_send()
    for m in range(7):
        vec_f(m).wait_recv()
        vec_f(m).wait_send()
        part(m).wait_send()
        cond(m).wait_send()
    vector_rows[...] = jnp.concatenate([vectors_all[f, z] for f in range(8) for z in range(sp)], axis=1)
    for r in range(1, sp):
        vec_z(r).wait_send()
        total(r).wait_send()
        text_z(r).wait_send()
    to_owners(p, h_blocks, h_slot.at[0], sh, rh, WAIT_SEND)
    for z in range(sp):
        swap(z).wait()


def front(sp, shards, ada, silu, vectors, text, resid):
    half = shards.shape[2]
    patches = resid.shape[1]
    text_rows, depth = text.shape[1:]
    dma = pltpu.SemaphoreType.DMA
    vmem = pl.BlockSpec(memory_space=pltpu.VMEM)
    any_space = pl.BlockSpec(memory_space=pl.ANY)
    shape = jax.ShapeDtypeStruct
    lanes = silu.shape[2]
    return pl.pallas_call(
        functools.partial(front_kernel, sp),
        out_shape=[
            shape((8 * BLOCK, half), BF),
            shape((2, 4, patches // 2, WIDE), BF),
            shape((MOD_ROWS, WIDE), F32),
            shape((TILE, 8 * sp * lanes), F32),
            shape((sp * text_rows, depth), BF),
            shape((8, TILE, lanes), F32),
        ],
        in_specs=[vmem] * 6,
        out_specs=[any_space] + [vmem] * 5,
        scratch_shapes=[
            pltpu.VMEM((8, sp, TILE, lanes), F32),
            pltpu.VMEM((2, sp, PIECE, half), BF),
            pltpu.VMEM((2, BLOCK, half), BF),
            pltpu.VMEM((8, MOD_ROWS, WIDE), F32),
            pltpu.VMEM((7, MOD_ROWS, WIDE), F32),
            pltpu.VMEM((sp - 1, MOD_ROWS, WIDE), F32),
            pltpu.VMEM((TILE, lanes), F32),
            pltpu.VMEM((sp, TILE, lanes), F32),
            pltpu.VMEM((sp, text_rows, depth), BF),
            pltpu.VMEM((4, patches // 2, WIDE), BF),
            dma((2, 3)),
            dma((2, 3)),
            dma((2, sp - 1)),
            dma((2, sp - 1)),
            dma((1,)),
            dma((1,)),
            dma((1,)),
        ]
        + [dma((7,))] * 4
        + [dma((sp - 1,))] * 4
        + [dma((7,))] * 2
        + [dma((sp - 1,))] * 2
        + [dma((4,))] * 4,
        compiler_params=pltpu.CompilerParams(
            collective_id=4, has_side_effects=True, vmem_limit_bytes=48 * 2**20
        ),
        name="front",
    )(shards, ada, silu, vectors, text, resid)


LAG = 3
FIRST = 8
PER = 2


def interleave(first, per, work, steps):
    steps = list(steps)
    for _ in range(first):
        steps.pop(0)()
    for k, piece in enumerate(work):
        piece()
        if steps and k % per == per - 1:
            steps.pop(0)()
    for step in steps:
        step()


class SumAlong:
    def __init__(self, p, part, landing, out, send, recv, send_again, recv_again):
        self.p, self.part, self.landing, self.out = p, part, landing, out
        self.sems = (send, recv, send_again, recv_again)

    def parts(self):
        send, recv = self.sems[:2]
        return along_z(
            self.p,
            self.p.sp,
            lambda z: self.part.at[z],
            lambda r: self.landing.at[r],
            lambda r: send.at[r],
            lambda r: recv.at[r],
        )

    def shares(self):
        own = self.out.at[self.p.z]
        send, recv = self.sems[2:]
        return [
            remote(own, own, send.at[r - 1], recv.at[r - 1], self.p.along(r)) for r in range(1, self.p.sp)
        ]

    def start(self):
        for copy in self.parts():
            copy.start()

    def sum(self):
        for copy in self.parts():
            copy.wait_recv()
        z = self.p.z
        for c in range(self.out.shape[2] // WIDE):
            cols = slice(c * WIDE, (c + 1) * WIDE)
            self.out[z, :, cols] = (
                self.part[z, :, cols].astype(F32)
                + sum(self.landing[r, :, cols].astype(F32) for r in range(self.p.sp - 1))
            ).astype(BF)
        for copy in self.shares():
            copy.start()

    def end(self):
        for copy in self.parts():
            copy.wait_send()
        for copy in self.shares():
            copy.wait()


def attend_kernel(plan, sp, heads, scale, n_out, *refs):
    shards, down_shard, text_shard, h_slot, qkv_w, text_mine, resid, mod, gain = refs[:9]
    refs = refs[9:]
    outs = refs[:n_out]
    down, text, qkv, attn, kv_all, branch, cross_in, query, cross, x_two = refs[n_out : n_out + 10]
    refs = refs[n_out + 10 :]
    landed, block, stack, heads_out, o_send, o_recv, o_full, text_w, kv_part, kv_in, kv, weights, x_one = refs[:13]
    send, recv, zsend, zrecv, dsend, drecv, local_sem, osem, hsend, hrecv, wsem = refs[13:24]
    p = Place(sp)
    along = SumAlong(p, kv_part, kv_in, kv, *refs[24:])
    greet_list([p.flip(b) for b in ("core", "x", "y")] + group(p))
    n = len(plan)
    rows = down_shard.shape[0]
    trows = text_shard.shape[0]
    down_own = down.at[pl.ds(pl.multiple_of(p.f * (sp * rows) + p.z * rows, 16), rows), :]
    text_own = text.at[pl.ds(pl.multiple_of(p.f * trows, 16), trows), :]
    text_copy = pltpu.make_async_copy(text_shard, text_own, local_sem.at[2])
    text_copy.start()

    chunks = [(text, lambda f: f * trows, trows, pl.ds(k * WIDE, WIDE), k % 2) for k in range(2)]
    chunks += [(outs[o], lambda f: f * BLOCK, BLOCK, pl.ds(c, WIDE), k % 2) for k, (o, c) in enumerate(plan)]
    chunks += [
        (down, lambda f, j=j: f * (sp * rows) + j * rows, rows, pl.ds(0, WIDE), (n + j) % 2) for j in range(sp)
    ]
    total = len(chunks)
    g = Gather(p, chunks, send, recv)

    def pieces(i):
        return [
            remote(shards.at[i], landed.at[i, p.z], zsend.at[i, r - 1], zrecv.at[i, r - 1], p.along(r))
            for r in range(1, sp)
        ]

    def down_z(r):
        return remote(down_shard, down_own, dsend.at[r - 1], drecv.at[p.z], p.along(r))

    def launch(i):
        if i < n:
            for copy in pieces(i):
                copy.start()
            landed[i, p.z] = shards[i]
        elif i == n:
            for r in range(1, sp):
                down_z(r).start()

    def ready(t):
        if t == 0:
            text_copy.wait()
        i = t - 2
        if 0 <= i < n:
            for copy in pieces(i):
                copy.wait_recv()
            slot = i % 2
            for zz in range(sp):
                block[slot, PIECE * zz : PIECE * (zz + 1), :] = landed[i, zz]
            copy = pltpu.make_async_copy(block.at[slot], g.region(t, p.f), local_sem.at[slot])
            copy.start()
            copy.wait()
        elif i >= n:
            remote(down_shard, down_own, dsend.at[0], drecv.at[i - n], p.along(1)).wait_recv()

    ahead = 6
    pltpu.make_async_copy(down_shard, down_own, drecv.at[p.z]).start()
    for i in range(ahead):
        launch(i)

    def step(t):
        if t < total:
            if t >= 2:
                launch(t - 2 + ahead)
            ready(t)
            g.begin(t)
        if 0 <= t - LAG < total:
            g.middle(t - LAG)
        if 0 <= t - 2 * LAG < total:
            g.late(t - 2 * LAG)

    T = qkv.shape[0]
    half = heads * HD
    tile = 256

    def project(i):
        hb = h_slot.shape[2]
        for b in range(tile // hb):
            k = i * (tile // hb) + b
            qkv[hb * k : hb * (k + 1), :] = nn(h_slot[k // 4, k % 4], qkv_w[...]).astype(BF)

    def stage():
        for i in range(3 * heads):
            stack[i] = jnp.zeros(stack.shape[1:], BF)
            stack[i, :, :HD] = qkv[:, i * HD : (i + 1) * HD]

    def head(h):
        def tile_of(i, _):
            q = stack[h, pl.ds(pl.multiple_of(i * tile, tile), tile), :]
            s = nt(q, stack[heads + h])
            m = jnp.max(s, axis=-1, keepdims=True)
            e = jnp.exp((s - m) * scale)
            l = jnp.sum(e, axis=-1, keepdims=True)
            r = nn(e.astype(BF), stack[2 * heads + h])
            heads_out[h, pl.ds(pl.multiple_of(i * tile, tile), tile), :] = (r / l).astype(BF)
            return 0

        lax.fori_loop(0, T // tile, tile_of, 0)

    def o_cross():
        return remote(o_send, o_recv, osem.at[0], osem.at[1], p.flip("core"))

    def o_out():
        for h in range(heads):
            o_send[:, h * HD : (h + 1) * HD] = heads_out[h, T // 2 :, :HD]
        o_cross().start()

    def o_home():
        o_cross().wait_recv()
        hb = T // 8
        low = p.core == 0
        for b in range(4):
            r = slice(hb * b, hb * (b + 1))
            mine = jnp.concatenate([heads_out[h, r, :HD] for h in range(heads)], axis=1)
            other = o_recv[r, :]
            o_full[b, :, :half] = jnp.where(low, mine, other)
            o_full[b, :, half:] = jnp.where(low, other, mine)
        to_homes(p, o_full, attn, hsend, hrecv, START)

    text_load = pltpu.make_async_copy(text, text_w, local_sem.at[3])

    def text_start():
        g.finish(0)
        g.finish(1)
        text_load.start()

    krows = kv_part.shape[1]

    def kv_product():
        text_load.wait()
        for c in range(2):
            cols = slice(c * WIDE, (c + 1) * WIDE)
            res = nn(text_mine[...], text_w[:, cols])
            for z in range(sp):
                kv_part[z, :, cols] = res[krows * z : krows * (z + 1)].astype(BF)
        along.start()

    slots, patches = resid.shape[:2]
    hb = T // 8
    loads = [pltpu.make_async_copy(outs[o], weights.at[o % 2], wsem.at[o]) for o in range(3)]

    def weights_start():
        for o in range(2):
            g.finish(2 + o)
            loads[o].start()

    def after(b):
        if b == 0:
            to_homes(p, o_full, attn, hsend, hrecv, WAIT_RECV)
            loads[0].wait()
            loads[1].wait()
        s, r = b // 2, slice(hb * (b % 2), hb * (b % 2 + 1))
        out = nn(attn[b], weights[0])
        branch[s, r, :] = out
        v = resid[s, r, :] + mod[2 * slots + s : 2 * slots + s + 1, :] * out
        x_one[s, r, :] = v
        c = v - jnp.mean(v, axis=-1, keepdims=True)
        n = c * lax.rsqrt(jnp.mean(c * c, axis=-1, keepdims=True) + 1e-06)
        low = (n * gain[:1, :]).astype(BF)
        cross_in[s, r, :] = low
        query[s, r, :] = nn(low, weights[1]).astype(BF)

    def text_end():
        g.finish(4)
        loads[2].start()
        along.end()
        count = kv_all.shape[1] // sp
        for s in range(slots):
            for z in range(sp):
                kv_all[s, count * z : count * (z + 1), :] = kv[z, count * s : count * (s + 1), :]

    def cross_attention(s):
        for h in range(2 * heads):
            c = slice(h * HD, (h + 1) * HD)
            cv = slice(WIDE + h * HD, WIDE + (h + 1) * HD)
            scores = nt(query[s, :, c], kv_all[s, :, c])
            m = jnp.max(scores, axis=-1, keepdims=True)
            e = jnp.exp((scores - m) * scale)
            l = jnp.sum(e, axis=-1, keepdims=True)
            cross[s, :, c] = (nn(e.astype(BF), kv_all[s, :, cv]) / l).astype(BF)

    def cross_project(s):
        if s == 0:
            loads[2].wait()
        for k in range(patches // hb):
            r = slice(hb * k, hb * (k + 1))
            x_two[s, r, :] = x_one[s, r, :] + nn(cross[s, r, :], weights[0])

    work = [functools.partial(project, i) for i in range(T // tile)]
    work += [text_start, stage]
    work += [functools.partial(head, h) for h in range(heads)]
    work.insert(-5, kv_product)
    work.insert(-2, along.sum)
    idle = lambda: None
    work += [o_out, o_home, weights_start, idle, idle, idle]
    work += [functools.partial(after, b) for b in range(4)]
    work += [text_end, functools.partial(cross_attention, 0), functools.partial(cross_attention, 1)]
    work += [functools.partial(cross_project, s) for s in range(slots)]
    interleave(FIRST, PER, work, [functools.partial(step, t) for t in range(total + 2 * LAG)])
    for i in range(5, total):
        g.finish(i)
    for i in range(n):
        for copy in pieces(i):
            copy.wait_send()
    for r in range(1, sp):
        down_z(r).wait_send()
    to_homes(p, o_full, attn, hsend, hrecv, WAIT_SEND)
    o_cross().wait_send()


def attend(plan, widths, sp, heads, scale, shards, down_shard, text_shard, h_slot, qkv_w, text_mine, resid, mod, gain):
    n = len(plan)
    total = n + sp + 2
    T = 8 * h_slot.shape[2]
    half = heads * HD
    trows = text_shard.shape[0]
    krows = text_mine.shape[0] // sp
    slots = resid.shape[0]
    any_space = pl.BlockSpec(memory_space=pl.ANY)
    vmem = pl.BlockSpec(memory_space=pltpu.VMEM)
    dma = pltpu.SemaphoreType.DMA
    shape = jax.ShapeDtypeStruct
    return pl.pallas_call(
        functools.partial(attend_kernel, plan, sp, heads, scale, len(widths)),
        out_shape=[shape((8 * BLOCK, w), BF) for w in widths]
        + [
            shape((8 * sp * down_shard.shape[0], WIDE), BF),
            shape((8 * trows, 2 * WIDE), BF),
            shape((T, 3 * half), BF),
            shape((4, T // 8, WIDE), BF),
            shape((slots, sp * krows // slots, 2 * WIDE), BF),
            shape(resid.shape, F32),
            shape(resid.shape, BF),
            shape(resid.shape, BF),
            shape(resid.shape, BF),
            shape(resid.shape, F32),
        ],
        in_specs=[vmem, any_space, any_space, vmem, vmem, vmem, vmem, vmem, vmem],
        out_specs=[any_space] * (len(widths) + 2) + [vmem] * 8,
        scratch_shapes=[
            pltpu.VMEM((n, sp, PIECE, WIDE), BF),
            pltpu.VMEM((2, BLOCK, WIDE), BF),
            pltpu.VMEM((3 * heads, T, 128), BF),
            pltpu.VMEM((heads, T, 128), BF),
            pltpu.VMEM((T // 2, half), BF),
            pltpu.VMEM((T // 2, half), BF),
            pltpu.VMEM((4, T // 8, WIDE), BF),
            pltpu.VMEM((8 * trows, 2 * WIDE), BF),
            pltpu.VMEM((sp, krows, 2 * WIDE), BF),
            pltpu.VMEM((sp - 1, krows, 2 * WIDE), BF),
            pltpu.VMEM((sp, krows, 2 * WIDE), BF),
            pltpu.VMEM((2, WIDE, WIDE), BF),
            pltpu.VMEM(resid.shape, F32),
            dma((total, 7)),
            dma((total, 7)),
            dma((n, sp - 1)),
            dma((n, sp - 1)),
            dma((sp - 1,)),
            dma((sp,)),
            dma((4,)),
            dma((2,)),
            dma((4,)),
            dma((4,)),
            dma((3,)),
            dma((sp - 1,)),
            dma((sp - 1,)),
            dma((sp - 1,)),
            dma((sp - 1,)),
        ],
        compiler_params=pltpu.CompilerParams(
            collective_id=5, has_side_effects=True, vmem_limit_bytes=60 * 2**20
        ),
        cost_estimate=pl.CostEstimate(flops=2**34, bytes_accessed=2**28, transcendentals=2**23),
        name="attend",
    )(shards, down_shard, text_shard, h_slot, qkv_w, text_mine, resid, mod, gain)


def split(refs, *counts):
    out = []
    for c in counts:
        out.append(refs[:c])
        refs = refs[c:]
    return out + [refs]


def attend_back_kernel(make, sp, heads, scale, *refs):
    sums = make()
    n_in = sums.n_in
    arrays, (go_blocks, qkv, kv_part, h_slot), results, (g, kv, gw), landings, scratch, rest = split(
        refs, n_in, 4, len(sums.results), 3, len(sums.landings), len(sums.scratch)
    )
    names = SimpleNamespace()
    for group_names, group_refs in ((sums.results, results), (sums.landings, landings), (sums.scratch, scratch)):
        names.__dict__.update(zip(group_names, group_refs))
    go_in, go_away, go_half, part, acc, gsend, grecv, esem, ksend, krecv = rest
    p = Place(sp)
    greet_list([p.flip(b) for b in ("core", "x", "y")] + group(p))
    sums.bind(p, arrays, names)
    to_owners(p, go_blocks, go_in, gsend, grecv, START)
    sums.begin()
    kv[p.z] = kv_part[...]

    def shares():
        own = kv.at[p.z]
        return [remote(own, own, ksend.at[r - 1], krecv.at[r - 1], p.along(r)) for r in range(1, sp)]

    T = qkv.shape[0]
    half = heads * HD
    rows = T // 8

    def cross():
        return remote(go_away, go_half.at[1], esem.at[0], esem.at[1], p.flip("core"))

    def cut():
        to_owners(p, go_blocks, go_in, gsend, grecv, WAIT_RECV)
        low = p.core == 0
        for b in range(4):
            first, other = go_in[b, :, :half], go_in[b, :, half:]
            go_half[0, b] = jnp.where(low, first, other)
            go_away[b] = jnp.where(low, other, first)
        cross().start()

    tile = 256

    def head(h):
        if h == 0:
            cross().wait_recv()
        for k in range(3):
            c = (k * heads + h) * HD
            part[k, :, :HD] = qkv[:, c : c + HD]
        for b in range(8):
            part[3, rows * b : rows * (b + 1), :HD] = go_half[b // 4, b % 4, :, h * HD : (h + 1) * HD]
        acc[...] = jnp.zeros(acc.shape, F32)

        def cols(i, _):
            sl = pl.ds(pl.multiple_of(i * tile, tile), tile)
            q, go = part[0, sl, :], part[3, sl, :]
            k, v = part[1], part[2]
            s = nt(k, q)
            m = jnp.max(s, axis=0, keepdims=True)
            e = jnp.exp((s - m) * scale)
            pr = e * (1.0 / jnp.sum(e, axis=0, keepdims=True))
            t = nt(v, go) * pr
            ds = (t - pr * jnp.sum(t, axis=0, keepdims=True)).astype(BF)
            acc[0] += nn(ds, q)
            acc[1] += nn(pr.astype(BF), go)
            part[0, sl, :] = (tn(ds, k) * scale).astype(BF)
            return 0

        lax.fori_loop(0, T // tile, cols, 0)
        c = h * HD
        g[:, c : c + HD] = part[0, :, :HD]
        c += half
        g[:, c : c + HD] = (acc[0, :, :HD] * scale).astype(BF)
        c += half
        g[:, c : c + HD] = acc[1, :, :HD].astype(BF)

    def weights(c):
        cols = slice(c, min(c + 512, g.shape[1]))
        gw[:, cols] = tn(h_slot[...], g[:, cols]).astype(BF)

    part[...] = jnp.zeros(part.shape, BF)
    work = [cut] + [functools.partial(head, h) for h in range(heads)]
    work += [functools.partial(weights, c) for c in range(0, g.shape[1], 512)]
    work.insert(2, lambda: [copy.start() for copy in shares()])
    interleave(2, 1, work, sums.steps())
    sums.end()
    for copy in shares():
        copy.wait()
    to_owners(p, go_blocks, go_in, gsend, grecv, WAIT_SEND)
    cross().wait_send()


def attend_back(plan, sp, heads, scale, grads, go_blocks, qkv, kv_part, h_slot):
    def make():
        sums = Sums(sp, plan, False, 0, 0)
        sums.n_in = len(grads)
        return sums

    sums = make()
    T = qkv.shape[0]
    half = heads * HD
    any_space = pl.BlockSpec(memory_space=pl.ANY)
    vmem = pl.BlockSpec(memory_space=pltpu.VMEM)
    dma = pltpu.SemaphoreType.DMA
    out = pl.pallas_call(
        functools.partial(attend_back_kernel, make, sp, heads, scale),
        out_shape=list(sums.results.values()) + [jax.ShapeDtypeStruct(a, BF) for a in (qkv.shape, (sp,) + kv_part.shape, (WIDE, qkv.shape[1]))] + list(sums.landings.values()),
        in_specs=[any_space] * len(grads) + [vmem] * 4,
        out_specs=[vmem] * (len(sums.results) + 3) + [any_space] * len(sums.landings),
        scratch_shapes=list(sums.scratch.values())
        + [
            pltpu.VMEM((4, T // 8, WIDE), BF),
            pltpu.VMEM((4, T // 8, half), BF),
            pltpu.VMEM((2, 4, T // 8, half), BF),
            pltpu.VMEM((4, T, 128), BF),
            pltpu.VMEM((2, T, 128), F32),
            dma((4,)),
            dma((4,)),
            dma((2,)),
            dma((sp - 1,)),
            dma((sp - 1,)),
        ],
        compiler_params=pltpu.CompilerParams(
            collective_id=6, has_side_effects=True, vmem_limit_bytes=62 * 2**20
        ),
        cost_estimate=pl.CostEstimate(flops=2**35, bytes_accessed=2**28, transcendentals=2**23),
        name="attend_back",
    )(*sums.arrays(grads), go_blocks, qkv, kv_part, h_slot)
    return out[:4]


def finish_kernel(make, sp, *refs):
    sums = make()
    arrays, (g, qkv_w, resid, grad_one, mod, small), results, (out, small_all), landings, scratch, rest = split(
        refs, sums.n_in, 6, len(sums.results), 2, len(sums.landings), len(sums.scratch)
    )
    names = SimpleNamespace()
    for group_names, group_refs in ((sums.results, results), (sums.landings, landings), (sums.scratch, scratch)):
        names.__dict__.update(zip(group_names, group_refs))
    home, gh, gh_in, blocks, mine, mine_in, partial, hsend, hrecv, esem, s1, r1, s2, r2 = rest
    p = Place(sp)
    near = others(p)
    greet_list(near + group(p))
    sums.bind(p, arrays, names)

    def cross():
        return remote(gh.at[1], gh_in, esem.at[0], esem.at[1], p.flip("core"))

    sums.begin()
    half_rows = gh.shape[2]

    def back(k):
        for b in range(4):
            first = (4 * k + b) * half_rows
            gh[k, b] = nt(g[first : first + half_rows, :], qkv_w[...])
        if k == 1:
            cross().start()

    slots = resid.shape[0]

    def add():
        cross().wait_recv()
        step = 16
        for b in range(4):

            def tile(i, _):
                r = pl.ds(pl.multiple_of(i * step, step), step)
                blocks[b, r, :] = (gh[0, b, r, :] + gh_in[b, r, :]).astype(BF)
                return 0

            lax.fori_loop(0, half_rows // step, tile, 0)
        to_homes(p, blocks, home, hsend, hrecv, START)

    def tail():
        to_homes(p, blocks, home, hsend, hrecv, WAIT_RECV)
        step = 32
        partial[...] = jnp.zeros(partial.shape, F32)
        for b in range(4):
            s, k = b // 2, b % 2

            def tile(i, _):
                start = pl.multiple_of(i * step, step)
                r = pl.ds(k * half_rows + start, step)
                v = resid[s, r, :]
                c = v - jnp.mean(v, axis=-1, keepdims=True)
                inv = lax.rsqrt(jnp.mean(c * c, axis=-1, keepdims=True) + 1e-06)
                n = c * inv
                g = home[b, pl.ds(start, step), :].astype(F32)
                gn = g * n
                partial[s, 0] += sum(g[8 * j : 8 * j + 8] for j in range(step // 8))
                partial[s, 1] += sum(gn[8 * j : 8 * j + 8] for j in range(step // 8))
                d = g * (1.0 + mod[slots + s : slots + s + 1, :])
                back = d - jnp.mean(d, axis=-1, keepdims=True) - n * jnp.mean(d * n, axis=-1, keepdims=True)
                out[s, r, :] = grad_one[s, r, :] + back * inv
                return 0

            lax.fori_loop(0, half_rows // step, tile, 0)
        mine[...] = small[...]
        for s in range(slots):
            for j in range(2):
                mine[slots * j + s : slots * j + s + 1, :] = jnp.sum(partial[s, j], axis=0, keepdims=True)
        for copy in along():
            copy.start()

    def along():
        return [remote(mine, mine_in.at[r - 1], s1.at[r - 1], r1.at[r - 1], p.along(r)) for r in range(1, sp)]

    def share(m):
        own = small_all.at[p.f]
        return remote(own, own, s2.at[m], r2.at[m], near[m])

    def total():
        for copy in along():
            copy.wait_recv()
        small_all[p.f] = mine[...] + sum(mine_in[r] for r in range(sp - 1))
        for m in range(7):
            share(m).start()

    idle = lambda: None
    work = [functools.partial(back, 1), functools.partial(back, 0), add, idle, idle, idle, tail, idle, total]
    interleave(1, 1, work, sums.steps())
    sums.end()
    for m in range(7):
        share(m).wait()
    for copy in along():
        copy.wait_send()
    to_homes(p, blocks, home, hsend, hrecv, WAIT_SEND)
    cross().wait_send()


def finish(sp, down, text, halves, g, qkv_w, resid, grad_one, mod, small):
    half = halves.shape[1]

    def make():
        sums = Sums(sp, [], True, text.shape[0] // 8, half)
        sums.n_in = 3
        return sums

    sums = make()
    rows = g.shape[0] // 8
    any_space = pl.BlockSpec(memory_space=pl.ANY)
    vmem = pl.BlockSpec(memory_space=pltpu.VMEM)
    dma = pltpu.SemaphoreType.DMA
    shape = jax.ShapeDtypeStruct
    out = pl.pallas_call(
        functools.partial(finish_kernel, make, sp),
        out_shape=list(sums.results.values())
        + [shape(resid.shape, F32), shape((8,) + small.shape, F32)]
        + list(sums.landings.values()),
        in_specs=[any_space] * 3 + [vmem] * 6,
        out_specs=[vmem] * (len(sums.results) + 2) + [any_space] * len(sums.landings),
        scratch_shapes=list(sums.scratch.values())
        + [
            pltpu.VMEM((4, rows, WIDE), BF),
            pltpu.VMEM((2, 4, rows, WIDE), F32),
            pltpu.VMEM((4, rows, WIDE), F32),
            pltpu.VMEM((4, rows, WIDE), BF),
            pltpu.VMEM(small.shape, F32),
            pltpu.VMEM((sp - 1,) + small.shape, F32),
            pltpu.VMEM((2, 2, 8, WIDE), F32),
            dma((4,)),
            dma((4,)),
            dma((2,)),
            dma((sp - 1,)),
            dma((sp - 1,)),
            dma((7,)),
            dma((7,)),
        ],
        compiler_params=pltpu.CompilerParams(
            collective_id=7, has_side_effects=True, vmem_limit_bytes=62 * 2**20
        ),
        name="finish",
    )(*sums.arrays([], down, text, halves), g, qkv_w, resid, grad_one, mod, small)
    return out[:5]


def temporal_kernel(heads, scale, trip, go, out, g):
    slots, rows, width = go.shape
    lanes = lax.broadcasted_iota(jnp.int32, (width, 128), 0) // HD
    member = (lanes == lax.broadcasted_iota(jnp.int32, (width, 128), 1)).astype(F32).astype(BF)
    across = lax.broadcasted_iota(jnp.int32, (128, width), 1) // HD
    member_t = (across == lax.broadcasted_iota(jnp.int32, (128, width), 0)).astype(F32).astype(BF)
    pairs = [(a, b) for a in range(slots) for b in range(slots)]

    def part(a, k):
        return trip[a, :, k * width : (k + 1) * width].astype(F32)

    def per_head(x):
        high = x.astype(BF)
        return nn(high, member) + nn((x - high.astype(F32)).astype(BF), member)

    def wide(x):
        return nn(x.astype(BF), member_t)

    s = {(a, b): per_head(part(a, 0) * part(b, 1)) * scale for a, b in pairs}
    p = {}
    for a in range(slots):
        m = functools.reduce(jnp.maximum, [s[a, b] for b in range(slots)])
        e = [jnp.exp(s[a, b] - m) for b in range(slots)]
        total = sum(e)
        for b in range(slots):
            p[a, b] = e[b] / total
    pw = {k: wide(v) for k, v in p.items()}
    d = [go[a].astype(F32) for a in range(slots)]
    for a in range(slots):
        out[a] = sum(pw[a, b] * part(b, 2) for b in range(slots)).astype(BF)
    for b in range(slots):
        g[b, :, 2 * width :] = sum(pw[a, b] * d[a] for a in range(slots)).astype(BF)
    dp = {(a, b): per_head(d[a] * part(b, 2)) for a, b in pairs}
    ds = {}
    for a in range(slots):
        mean = sum(dp[a, b] * p[a, b] for b in range(slots))
        for b in range(slots):
            ds[a, b] = wide(p[a, b] * (dp[a, b] - mean))
    for a in range(slots):
        g[a, :, :width] = (scale * sum(ds[a, b] * part(b, 1) for b in range(slots))).astype(BF)
        g[a, :, width : 2 * width] = (scale * sum(ds[b, a] * part(b, 0) for b in range(slots))).astype(BF)


def temporal(trip, go, heads, scale):
    slots, patches, width = go.shape
    rows = 64
    block = lambda w: pl.BlockSpec((slots, rows, w), lambda i: (0, i, 0))
    return pl.pallas_call(
        functools.partial(temporal_kernel, heads, scale),
        grid=(patches // rows,),
        out_shape=[jax.ShapeDtypeStruct((slots, patches, w), BF) for w in (width, 3 * width)],
        in_specs=[block(3 * width), block(width)],
        out_specs=[block(width), block(3 * width)],
        compiler_params=pltpu.CompilerParams(vmem_limit_bytes=48 * 2**20),
        cost_estimate=pl.CostEstimate(flops=2**32, bytes_accessed=2**24, transcendentals=2**16),
        name="temporal",
    )(trip, go)


HEADS = 16
EPS = 1e-06
HIGHEST = lax.Precision.HIGHEST
BOTH = ("fsdp", "sp")
PLAN = (
    [(0, 0), (1, 0), (2, 0)] + [(3, k * WIDE) for k in range(4)] + [(4, k * WIDE) for k in range(3)] + [(5, 0)]
)


def normalize(values):
    centred = values - jnp.mean(values, axis=-1, keepdims=True)
    return centred * lax.rsqrt(jnp.mean(centred * centred, axis=-1, keepdims=True) + EPS)


def normalize_back(values, grad_out):
    return jax.vjp(normalize, values)[1](grad_out)[0]


def gelu_tanh(values):
    return jax.nn.gelu(values, approximate=True)


def scatter(grad):
    part = lax.psum_scatter(grad.astype(BF), "fsdp", scatter_dimension=0, tiled=True)
    return lax.psum_scatter(part, "sp", scatter_dimension=0, tiled=True).astype(F32)


def sum_along(parts, sp):
    z = lax.axis_index("sp")
    total = lax.dynamic_index_in_dim(parts, z, 0, keepdims=False).astype(F32)
    for r in range(1, sp):
        part = lax.dynamic_index_in_dim(parts, (z + r) % sp, 0, keepdims=False)
        total += lax.ppermute(part, "sp", [(k, (k + r) % sp) for k in range(sp)]).astype(F32)
    return total.astype(BF)


class Moves:
    def __init__(self, fsdp, sp, slots):
        self.fsdp, self.sp, self.slots = fsdp, sp, slots
        self.core = lax.axis_index("fsdp") % 2
        self.z = lax.axis_index("sp")
        self.rounds = []
        for r in range(sp):
            pairs = []
            for f in range(fsdp):
                for z in range(sp):
                    t = (z - r) % sp
                    pairs.append((f * sp + z, (f - f % 2 + t % 2) * sp + slots * (f % 2) + t // 2))
            self.rounds.append(pairs)
        self.swap = [(f, f ^ 1) for f in range(fsdp)]

    def out(self, tokens):
        rows = tokens.shape[0] // self.sp
        blocks = tokens.reshape(self.sp, rows, tokens.shape[1])
        got = []
        for r, pairs in enumerate(self.rounds):
            t = (self.z - r) % self.sp
            block = lax.dynamic_index_in_dim(blocks, t, 0, keepdims=False)
            got.append(lax.ppermute(block, BOTH, pairs))
        return jnp.roll(jnp.stack(got), self.mine(), axis=0).reshape(tokens.shape)

    def home(self, tokens):
        rows = tokens.shape[0] // self.sp
        tokens = jnp.roll(tokens.reshape(self.sp, rows, -1), -self.mine(), axis=0).reshape(tokens.shape)
        out = jnp.zeros((self.sp, rows, tokens.shape[1]), tokens.dtype)
        for r, pairs in enumerate(self.rounds):
            back = lax.ppermute(tokens[r * rows : (r + 1) * rows], BOTH, [(b, a) for a, b in pairs])
            t = (self.z - r) % self.sp
            out = lax.dynamic_update_index_in_dim(out, back, t, 0)
        return out.reshape(tokens.shape)

    def mine(self):
        return 2 * (self.z % 2) + self.core

    def exchange(self, array):
        return lax.ppermute(array, "fsdp", self.swap)


def local(
    residual_in,
    condition,
    text_states,
    slot_item,
    cotangent,
    w_ada,
    w_qkv,
    w_out,
    w_cross_q,
    w_cross_kv,
    w_cross_out,
    w_up,
    w_down,
    w_temp_qkv,
    w_temp_out,
    g_cross,
    g_temp,
    t_gate,
):
    slots, patches, width = residual_in.shape[1:]
    text_local, text_width = text_states.shape[2:]
    sp = lax.axis_size("sp")
    fsdp = lax.axis_size("fsdp")
    f_index, z_index = lax.axis_index("fsdp"), lax.axis_index("sp")
    rows = w_qkv.shape[0]
    tok = slots * patches
    scale = HD ** (-0.5)
    moves = Moves(fsdp, sp, slots)
    core = f_index % 2

    def gather(shard):
        return lax.all_gather(shard.astype(BF), BOTH, axis=0, tiled=True)

    chosen = slot_item[0]
    video = (chosen[-1] == 0).astype(F32)

    cond = condition[0]
    cond_used = jnp.where((chosen == 0)[:, None], cond[0][None], cond[1][None])
    silu_low = jax.nn.silu(cond_used).astype(BF)
    text = text_states[0]
    text_used = jnp.where((chosen == 0)[:, None, None], text[0][None], text[1][None])
    kv_rows = w_cross_kv.shape[0]
    text_cut = text_used.reshape(slots * text_local, fsdp, sp, kv_rows)
    heads_half = HEADS // 2
    half = heads_half * HD
    resid = residual_in[0]
    normed_one = normalize(resid)
    small_slice = fsdp == 8 and sp == 4
    stacked_vectors = jnp.stack([g_cross, g_temp, t_gate]).astype(BF)
    if small_slice:
        qkv_shards = w_qkv.astype(BF).reshape(rows, 3, 2, half).transpose(2, 0, 1, 3).reshape(2, rows, 3 * half)
        silu_blocks = silu_low.astype(F32).reshape(slots, fsdp * sp, rows).transpose(1, 0, 2)
        qkv_half, h_slot, mod_rows, vectors, text_mine, silu_rows = front(
            sp,
            qkv_shards,
            w_ada.astype(BF),
            jnp.pad(silu_blocks, ((0, 0), (0, TILE - slots), (0, 0))),
            jnp.pad(stacked_vectors, ((0, 2 * TILE - 3), (0, 0))),
            text_cut.transpose(2, 0, 1, 3).reshape(sp, slots * text_local, fsdp * kv_rows),
            resid,
        )
        silu_rows = silu_rows[:, :slots].reshape(fsdp * slots, rows).astype(BF)
        modulation = mod_rows[: 6 * slots].reshape(6, slots, 1, width)
        low = [w.astype(BF) for w in (w_out, w_cross_q, w_cross_out, w_up, w_temp_qkv, w_temp_out)]
        shards = jnp.stack([low[o][:, c : c + width] for o, c in PLAN])
        (
            out_full,
            cross_q_full,
            cross_out_full,
            up_full,
            temp_qkv_full,
            temp_out_full,
            down_full,
            _,
            qkv,
            attn_tok,
            kv_all,
            branch_one,
            cross_in,
            query_c,
            cross_out,
            x_two,
        ) = attend(
            PLAN,
            [w.shape[1] for w in low],
            sp,
            heads_half,
            scale,
            shards,
            w_down.astype(BF),
            w_cross_kv.astype(BF),
            h_slot,
            qkv_half,
            text_mine,
            resid,
            mod_rows,
            vectors,
        )
        h_slot = h_slot.reshape(2 * tok, width)
        attn_tok = attn_tok.reshape(tok, width)
        shift_one, scale_one, gate_one, shift_two, scale_two, gate_two = (modulation[i] for i in range(6))
    else:
        silu_all = lax.all_gather(silu_low, "fsdp", axis=0, tiled=True)
        silu_rows = lax.dynamic_slice_in_dim(silu_all, (f_index * sp + z_index) * rows, rows, 1)
        modulation = lax.psum(
            lax.psum_scatter(nn(silu_rows, w_ada.astype(BF)), "fsdp", scatter_dimension=0, tiled=True), "sp"
        ).reshape(slots, 6, 1, width)
        shift_one, scale_one, gate_one, shift_two, scale_two, gate_two = (modulation[:, i] for i in range(6))
        vectors = lax.all_gather(stacked_vectors, BOTH, axis=1, tiled=True).astype(F32)
        qkv_half = lax.dynamic_index_in_dim(
            gather(w_qkv).reshape(width, 3, 2, half), core, 2, keepdims=False
        ).reshape(width, 3 * half)
        out_full = gather(w_out)
        cross_q_full = gather(w_cross_q)
        cross_out_full = gather(w_cross_out)
        up_full = gather(w_up)
        down_full = gather(w_down)
        temp_qkv_full = gather(w_temp_qkv)
        temp_out_full = gather(w_temp_out)
        kv_weight = lax.all_gather(w_cross_kv.astype(BF), "fsdp", axis=0, tiled=True)
        text_mine = lax.all_to_all(text_cut, "sp", split_axis=2, concat_axis=0, tiled=True)
        text_mine = text_mine.reshape(sp * slots * text_local, fsdp * kv_rows)
        kv_part = lax.psum_scatter(nn(text_mine, kv_weight), "sp", scatter_dimension=0, tiled=True).astype(BF)
        kv_all = (
            lax.all_gather(kv_part.reshape(1, slots, text_local, 2 * width), "sp", axis=0, tiled=True)
            .transpose(1, 0, 2, 3)
            .reshape(slots, sp * text_local, 2 * width)
        )
        h_one = (normed_one * (1.0 + scale_one) + shift_one).astype(BF).reshape(tok, width)
        h_mine = moves.out(h_one)
        h_slot = jnp.concatenate([h_mine, moves.exchange(h_mine)], axis=0)
        qkv = nn(h_slot, qkv_half).astype(BF)
        o_slot = spatial_fwd(qkv, heads_half, scale)
        o_mine = o_slot[:tok]
        o_other = moves.exchange(o_slot[tok:])
        o_full = jnp.where(
            core == 0,
            jnp.concatenate([o_mine, o_other], axis=1),
            jnp.concatenate([o_other, o_mine], axis=1),
        )
        attn_tok = moves.home(o_full)
    gain_cross, gain_temp, temp_gate = vectors[0], vectors[1], vectors[2]
    if small_slice:
        x_one = resid + gate_one * branch_one
        normed_two = normalize(x_one)
        cross_in, cross_out = cross_in.reshape(tok, width), cross_out.reshape(tok, width)
    else:
        branch_one = nn(attn_tok, out_full).reshape(slots, patches, width)
        x_one = resid + gate_one * branch_one
        normed_two = normalize(x_one)
        cross_in = (normed_two * gain_cross).astype(BF).reshape(tok, width)
        query_c = nn(cross_in, cross_q_full).astype(BF).reshape(slots, patches, width)
        cross_out = cross_fwd(query_c, kv_all, HEADS, scale).reshape(tok, width)
        x_two = x_one + nn(cross_out, cross_out_full).reshape(slots, patches, width)

    normed_three = normalize(x_two)
    h_three = (normed_three * (1.0 + scale_two) + shift_two).astype(BF).reshape(tok, width)
    up_proj = nn(h_three, up_full)
    activated = gelu_tanh(up_proj).astype(BF)
    branch_three = nn(activated, down_full).reshape(slots, patches, width)
    x_three = x_two + gate_two * branch_three

    normed_four = normalize(x_three)
    temp_in = (normed_four * gain_temp).astype(BF).reshape(tok, width)
    trip = nn(temp_in, temp_qkv_full).astype(BF).reshape(slots, patches, 3 * width)
    grad_out = cotangent[0].astype(F32)
    grad_b4 = (grad_out * (video * temp_gate)).astype(BF).reshape(tok, width)
    grad_to = nt(grad_b4, temp_out_full).astype(BF).reshape(slots, patches, width)
    temp_out, grad_trip = temporal(trip, grad_to, HEADS, scale)
    temp_out = temp_out.reshape(tok, width)
    grad_trip = grad_trip.reshape(tok, 3 * width)
    branch_four = nn(temp_out, temp_out_full).reshape(slots, patches, width)
    output = x_three + (video * temp_gate) * branch_four

    grad_tgate = video * jnp.sum(grad_out * branch_four, axis=(0, 1))
    grad_wto = tn(temp_out, grad_b4)
    grad_wtq = tn(temp_in, grad_trip)
    grad_temp_in = nt(grad_trip, temp_qkv_full).reshape(slots, patches, width)
    grad_gtemp = jnp.sum(grad_temp_in * normed_four, axis=(0, 1))
    grad_three = grad_out + normalize_back(x_three, grad_temp_in * gain_temp)

    grad_gate_two = jnp.sum(grad_three * branch_three, axis=1)
    grad_b3 = (grad_three * gate_two).astype(BF).reshape(tok, width)
    grad_wdown = tn(activated, grad_b3)
    grad_act = nt(grad_b3, down_full)
    grad_up = jax.vjp(gelu_tanh, up_proj)[1](grad_act)[0].astype(BF)
    grad_wup = tn(h_three, grad_up)
    grad_h_three = nt(grad_up, up_full).reshape(slots, patches, width)
    grad_shift_two = jnp.sum(grad_h_three, axis=1)
    grad_scale_two = jnp.sum(grad_h_three * normed_three, axis=1)
    grad_two = grad_three + normalize_back(x_two, grad_h_three * (1.0 + scale_two))

    grad_b2 = grad_two.astype(BF).reshape(tok, width)
    grad_wco = tn(cross_out, grad_b2)
    grad_co = nt(grad_b2, cross_out_full).astype(BF).reshape(slots, patches, width)
    grad_qc, grad_kv = cross_bwd(query_c, kv_all, grad_co, HEADS, scale)
    grad_qc = grad_qc.reshape(tok, width)
    grad_kv = (
        grad_kv.reshape(slots, sp, text_local, 2 * width)
        .transpose(1, 0, 2, 3)
        .reshape(sp * slots * text_local, 2 * width)
        .astype(BF)
    )
    grad_wcq = tn(cross_in, grad_qc)
    grad_cross_in = nt(grad_qc, cross_q_full).reshape(slots, patches, width)
    grad_gcross = jnp.sum(grad_cross_in * normed_two, axis=(0, 1))
    grad_one = grad_two + normalize_back(x_one, grad_cross_in * gain_cross)

    grad_gate_one = jnp.sum(grad_one * branch_one, axis=1)
    grad_b1 = (grad_one * gate_one).astype(BF).reshape(tok, width)
    grad_wout = tn(attn_tok, grad_b1)
    grad_attn = nt(grad_b1, out_full).astype(BF)
    if small_slice:
        late = [g.astype(BF) for g in (grad_wout, grad_wcq, grad_wco, grad_wup, grad_wtq, grad_wto)]
        pieces, grad_qkv, grad_kv, grad_wqkv_half = attend_back(
            PLAN,
            sp,
            heads_half,
            scale,
            late,
            grad_attn.reshape(sp, tok // sp, width),
            qkv,
            sum_along(grad_kv.reshape(sp, slots * text_local, 2 * width), sp),
            h_slot,
        )
        grad_kv = grad_kv.reshape(sp * slots * text_local, 2 * width)
        own = [jnp.concatenate([pieces[k] for k, (o, _) in enumerate(PLAN) if o == i], axis=1) for i in range(len(late))]
        own_out, own_cq, own_co, own_up, own_tq, own_to = own
    else:
        go_mine = moves.out(grad_attn)
        low_half, high_half = go_mine[:, :half], go_mine[:, half:]
        go_other = moves.exchange(jnp.where(core == 0, high_half, low_half))
        go_slot = jnp.concatenate([jnp.where(core == 0, low_half, high_half), go_other], axis=0)
        grad_qkv = spatial_bwd(qkv, go_slot, heads_half, scale)
        grad_kv = lax.all_gather(
            lax.psum_scatter(grad_kv, "sp", scatter_dimension=0, tiled=True), "sp", axis=0, tiled=True
        )
        grad_wqkv_half = tn(h_slot, grad_qkv).astype(BF)
    grad_wckv = tn(text_mine, grad_kv)
    known = [grad_gate_one, grad_shift_two, grad_scale_two, grad_gate_two]
    known_vectors = [grad_gcross, grad_gtemp, grad_tgate]
    if small_slice:
        zero = jnp.zeros((slots, width), F32)
        own_down, own_text, own_half, input_grad, small_sp = finish(
            sp,
            grad_wdown.astype(BF),
            grad_wckv.astype(BF),
            grad_wqkv_half,
            grad_qkv,
            qkv_half,
            resid,
            grad_one,
            mod_rows,
            jnp.concatenate([zero, zero] + known + [jnp.stack(known_vectors + [zero[0]])], axis=0),
        )
        own_text = own_text.transpose(1, 0, 2).reshape(kv_rows, 2 * width)
        own_half = jnp.where(core == 0, own_half, own_half[::-1])
        own_qkv = own_half.reshape(2, rows, 3, half).transpose(1, 2, 0, 3).reshape(rows, 3 * width)
    else:
        gh_slot = nt(grad_qkv, qkv_half)
        grad_h_one = moves.home((gh_slot[:tok] + moves.exchange(gh_slot[tok:])).astype(BF))
        grad_h_one = grad_h_one.astype(F32).reshape(slots, patches, width)
        input_grad = grad_one + normalize_back(resid, grad_h_one * (1.0 + scale_one))
        new = [jnp.sum(grad_h_one, axis=1), jnp.sum(grad_h_one * normed_one, axis=1)]
        small = jnp.concatenate(new + known + [jnp.stack(known_vectors)], axis=0)
        small_sp = jnp.sum(
            lax.all_gather(small, BOTH, axis=0).reshape(fsdp, sp, slots * 6 + 3, width), axis=1
        )
    grad_mod = small_sp[:, : slots * 6].reshape(fsdp, 6, slots, width).transpose(0, 2, 1, 3)
    grad_mod = grad_mod.reshape(fsdp * slots, 6 * width)
    grad_wada = jnp.dot(silu_rows.astype(F32).T, grad_mod, precision=HIGHEST, preferred_element_type=F32)
    grad_vec = lax.dynamic_slice_in_dim(
        jnp.sum(small_sp[:, slots * 6 : slots * 6 + 3], axis=0), (f_index * sp + z_index) * rows, rows, 1
    )
    if not small_slice:
        wide = grad_wqkv_half.reshape(width, 3, 1, half)
        zeros = jnp.zeros_like(wide)
        grad_wqkv = jnp.where(
            core == 0, jnp.concatenate([wide, zeros], axis=2), jnp.concatenate([zeros, wide], axis=2)
        ).reshape(width, 3 * width)
        own_qkv, own_out, own_cq, own_co = scatter(grad_wqkv), scatter(grad_wout), scatter(grad_wcq), scatter(grad_wco)
        own_up, own_down, own_tq, own_to = scatter(grad_wup), scatter(grad_wdown), scatter(grad_wtq), scatter(grad_wto)
        own_text = lax.psum_scatter(grad_wckv.astype(BF), "fsdp", scatter_dimension=0, tiled=True).astype(F32)
    return (
        output[None],
        input_grad[None],
        grad_wada,
        own_qkv,
        own_out,
        own_cq,
        own_text,
        own_co,
        own_up,
        own_down,
        own_tq,
        own_to,
        grad_vec[0],
        grad_vec[1],
        grad_vec[2],
    )


def solution(mesh):
    P = jax.sharding.PartitionSpec
    tokens = P("fsdp", None, "sp", None)
    weight = P(BOTH, None)
    vector = P(BOTH)
    return jax.shard_map(
        local,
        mesh=mesh,
        in_specs=(tokens, P("fsdp", None, None), tokens, P("fsdp", None), tokens)
        + (weight,) * 10
        + (vector,) * 3,
        out_specs=(tokens, tokens) + (weight,) * 10 + (vector,) * 3,
        check_vma=False,
    )
```
